32 devices in a mesh: dp: 8 (over z, y), mp: 4 (over x, core).
Axes of the slice: x: 2, y: 2, z: 4, core: 2. Of those that a mesh axis runs over, the one named last changes fastest.
Arguments:
- block_input: bfloat16 [8192, 1024], P(('dp', 'mp')), may hold values from -6 to 6
- latent_table: bfloat16 [256, 1024], replicated, may hold values from -6 to 6
- latent_segments: int32 [8, 1024], P('dp'), may hold values from 0 to 15, as said below
- input_segments: int32 [8, 1024], P('dp'), may hold values from 0 to 15, as said below
- ln_gain: float32 [4, 1024], replicated, may hold values from 0.1 to 1.9
- ln_bias: float32 [4, 1024], replicated, may hold values from -2.5 to 2.5
- cross_query: bfloat16 [1024, 1024], P(None, 'mp'), may hold values from -0.1875 to 0.1875
- cross_key: bfloat16 [1024, 1024], P(None, 'mp'), may hold values from -0.1875 to 0.1875
- cross_value: bfloat16 [1024, 1024], P(None, 'mp'), may hold values from -0.1875 to 0.1875
- cross_out: bfloat16 [1024, 1024], P(None, 'mp'), may hold values from -1 to 1
- self_query: bfloat16 [1024, 1024], P(None, 'mp'), may hold values from -0.1875 to 0.1875
- self_key: bfloat16 [1024, 1024], P(None, 'mp'), may hold values from -0.1875 to 0.1875
- self_value: bfloat16 [1024, 1024], P(None, 'mp'), may hold values from -0.1875 to 0.1875
- self_out: bfloat16 [1024, 1024], P(None, 'mp'), may hold values from -1 to 1
- up_proj: bfloat16 [1024, 4096], P(None, 'mp'), may hold values from -0.1875 to 0.1875
- down_proj: bfloat16 [1024, 4096], P(None, 'mp'), may hold values from -0.125 to 0.125
- out_grad: bfloat16 [8192, 1024], P(('dp', 'mp')), may hold values from -6 to 6
Outputs:
- block_output: float32 [8192, 1024], P(('dp', 'mp'))
- input_grad: float32 [8192, 1024], P(('dp', 'mp'))
- table_grad: float32 [256, 1024], replicated
- ln_gain_grad: float32 [4, 1024], replicated
- ln_bias_grad: float32 [3, 1024], replicated
- mlp_bias_grad: float32 [1024], replicated
- cross_query_grad: float32 [1024, 1024], P('dp', 'mp')
- cross_key_grad: float32 [1024, 1024], P('dp', 'mp')
- cross_value_grad: float32 [1024, 1024], P('dp', 'mp')
- cross_out_grad: float32 [1024, 1024], P('dp', 'mp')
- self_query_grad: float32 [1024, 1024], P('dp', 'mp')
- self_key_grad: float32 [1024, 1024], P('dp', 'mp')
- self_value_grad: float32 [1024, 1024], P('dp', 'mp')
- self_out_grad: float32 [1024, 1024], P('dp', 'mp')
- up_proj_grad: float32 [1024, 4096], P('dp', 'mp')
- down_proj_grad: float32 [1024, 4096], P('dp', 'mp')
The draws below stay inside these ranges and needn't reach their ends.
Inputs may be any that keep to these rules, and one draw needn't show every extreme that they name: `latent_segments`: in each packed row the ids never fall, every id from 0 to 15 occurs, no image has more than 256 latent rows, and one image has exactly 256. `input_segments`: in each packed row the ids never fall, every id from 0 to 15 occurs, no image has more than 256 input rows, and one image has exactly 256.
All inputs are finite; a program needn't handle non-finite values.
Results may differ from the reference program's by a relative error of at most 0.028.
Values may be sent and summed in bfloat16 or wider, within the bound.
No kernel may reach another device: no remote copies, remote signals or barrier semaphores. Data moves between devices by JAX's collectives and lax.ppermute only.
A program may use at most 128 MiB of HBM per device.

```python
import jax
import jax.numpy as jnp
from jax import lax

D = 1024
HEADS = 8
HEAD = 128
FF = 4096
LAT_TAB = 256
ROWS_DP = 1024
IMG_DP = 16
ROWS = 8192
N_DP = 8
N_MP = 4


def image_lengths(key, row_total, image_count, longest):
    rest_rows = row_total - longest
    others = image_count - 1
    base_rows = rest_rows // (2 * others)
    spare_rows = rest_rows - others * base_rows
    split_keys = jax.random.split(key, 2)
    shares = jax.random.randint(split_keys[0], (others,), 2, 4, dtype=jnp.int32)
    extra_rows = spare_rows * shares // jnp.sum(shares)
    shortfall = spare_rows - jnp.sum(extra_rows)
    extra_rows = extra_rows + (jnp.arange(others, dtype=jnp.int32) < shortfall).astype(jnp.int32)
    lengths = jnp.concatenate([base_rows + extra_rows, jnp.full((1,), longest, jnp.int32)])
    placing = jax.random.randint(split_keys[1], (), 0, image_count, dtype=jnp.int32)
    indices = jnp.arange(image_count, dtype=jnp.int32)
    new_order = jnp.where(indices < placing, indices, jnp.where(indices == placing, image_count - 1, indices - 1))
    return lengths[new_order]


def segment_ids(key, longest):
    lengths = image_lengths(key, ROWS_DP, IMG_DP, longest)
    row_ends = jnp.cumsum(lengths)
    positions = jnp.arange(ROWS_DP, dtype=jnp.int32)
    return jnp.sum((row_ends[None, :] <= positions[:, None]).astype(jnp.int32), axis=1, dtype=jnp.int32)


def packed_rows(key, longest):
    row_keys = jax.random.split(key, N_DP)
    return jax.vmap(lambda row_key: segment_ids(row_key, longest))(row_keys)


def draw_latent_segments(key, part):
    return packed_rows(jax.random.fold_in(key, 17), LAT_TAB)


def draw_input_segments(key, part):
    return packed_rows(jax.random.fold_in(key, 29), LAT_TAB)


def with_spikes(result, rng, source, target, shards_of, factor):
    def block_of(position):
        return (jnp.arange(result.shape[position]) // (result.shape[position] // shards_of)).reshape((-1,) + (1,) * (result.ndim - 1 - position))

    one_side = jax.random.permutation(rng, shards_of)[block_of(target)]
    other_side = (block_of(target) + shards_of // 2) % shards_of
    return jnp.where((block_of(source) == one_side) | (block_of(source) == other_side), factor * result, result)


def levels(rng, dims, shards, least, largest):
    def one(position, parts):
        steps = jax.random.uniform(jax.random.fold_in(jax.random.fold_in(rng, 6), position), (parts,), jnp.float32, least / len(shards), largest / len(shards))
        return jnp.repeat(jnp.exp(steps), dims[position] // parts).reshape((-1,) + (1,) * (len(dims) - position - 1))

    loudness = one(*shards[0])
    for cut in shards[1:]:
        loudness = loudness * one(*cut)
    return loudness


def gaussian(own_key, extent, scale, reach, shards=(), held_as=jnp.bfloat16):
    loudness = levels(own_key, extent, shards, -0.22, 0.18) if shards else 1.0
    drawn = jax.random.normal(own_key, extent, jnp.float32) * scale * loudness
    return jnp.minimum(jnp.maximum(drawn, -reach), reach).astype(held_as)


def gaussian_with(own_key, extent, deviation, limit, cuts, heavy, kind=jnp.bfloat16):
    entries = deviation * jax.random.normal(own_key, extent, jnp.float32)
    if cuts:
        entries = entries * levels(own_key, extent, cuts, -0.22, 0.18)
    return jnp.clip(with_spikes(entries, jax.random.fold_in(own_key, 3), *heavy), -limit, limit).astype(kind)


def setup_inputs(seed: int = 0) -> dict:
    key_of = jax.random.split(jax.random.key(seed), 18)
    block_input = gaussian(key_of[0], (ROWS, D), 1.0, 6.0, ((0, 32),))
    latent_table = gaussian(key_of[1], (LAT_TAB, D), 1.0, 6.0)
    latent_segments = draw_latent_segments(jax.random.fold_in(key_of[17], 71), 0)
    input_segments = draw_input_segments(jax.random.fold_in(key_of[17], 71), 0)
    ln_gain = jnp.clip(1.0 + 0.18 * jax.random.normal(key_of[4], (4, D), jnp.float32), 0.1, 1.9)
    ln_bias = gaussian(key_of[5], (4, D), 0.5, 2.5, (), jnp.float32)
    cross_query = gaussian(key_of[6], (D, D), D ** -0.5, 0.1875, ((1, 4),))
    cross_key = gaussian(key_of[7], (D, D), D ** -0.5, 0.1875, ((1, 4),))
    cross_value = gaussian(key_of[8], (D, D), D ** -0.5, 0.1875, ((1, 4),))
    cross_out = gaussian(key_of[9], (D, D), (D // 32) ** -0.5, 1.0, ((1, 4),))
    self_query = gaussian(key_of[10], (D, D), D ** -0.5, 0.1875, ((1, 4),))
    self_key = gaussian(key_of[11], (D, D), D ** -0.5, 0.1875, ((1, 4),))
    self_value = gaussian(key_of[12], (D, D), D ** -0.5, 0.1875, ((1, 4),))
    self_out = gaussian(key_of[13], (D, D), (D // 32) ** -0.5, 1.0, ((1, 4),))
    up_proj = gaussian(key_of[14], (D, FF), D ** -0.5, 0.1875, ((1, 4),))
    down_proj = gaussian(key_of[15], (D, FF), (FF // 2) ** -0.5, 0.125, ((1, 4),))
    out_grad = gaussian_with(key_of[16], (ROWS, D), 1.0, 6.0, ((0, 32),), (0, 1, 32, 2.75))
    return {"block_input": block_input, "latent_table": latent_table, "latent_segments": latent_segments, "input_segments": input_segments, "ln_gain": ln_gain, "ln_bias": ln_bias, "cross_query": cross_query, "cross_key": cross_key, "cross_value": cross_value, "cross_out": cross_out, "self_query": self_query, "self_key": self_key, "self_value": self_value, "self_out": self_out, "up_proj": up_proj, "down_proj": down_proj, "out_grad": out_grad}


norm_eps = 1e-05
masked_score = -1e+30
highest = lax.Precision.HIGHEST
gelu_coeff = 0.7978845608028654

@jax.custom_vjp
def low(v):
    return lax.optimization_barrier(v.astype(jnp.bfloat16)).astype(jnp.float32)

@jax.custom_vjp
def low_back(v):
    return v

def low_keep(v):
    return (low(v), None)

def low_pass(kept, grad):
    return (grad,)

def back_keep(v):
    return (v, None)

def back_low(kept, grad):
    return (low(grad),)
low.defvjp(low_keep, low_pass)
low_back.defvjp(back_keep, back_low)

def rounded(values):
    return low_back(low(values))

def matmul(left, right):
    return jnp.dot(left, right, precision=highest)

def layer_norm(values, gain, offset):
    average = lax.optimization_barrier(jnp.mean(values, axis=-1, keepdims=True))
    centred = values - average
    spread = lax.optimization_barrier(jnp.mean(centred * centred, axis=-1, keepdims=True))
    return centred * lax.rsqrt(spread + norm_eps) * gain + offset

def gelu_tanh(values):
    return 0.5 * values * (1.0 + jnp.tanh(gelu_coeff * (values + 0.044715 * values * values * values)))

def split_project(normed, weight_list):
    return [matmul(normed, weight) for weight in weight_list]

def merge_project(rows, weight):
    width = rows.shape[1] // N_MP
    total = jnp.zeros((rows.shape[0], weight.shape[0]), jnp.float32)
    for group in range(N_MP):
        piece = matmul(rows[:, group * width:(group + 1) * width], weight[:, group * width:(group + 1) * width].T)
        total = total + low_back(piece)
    return total

def attend(queries, key_rows, values, query_ids, key_ids):
    length = queries.shape[0]
    query_heads = queries.reshape(length, HEADS, HEAD)
    key_heads = key_rows.reshape(key_rows.shape[0], HEADS, HEAD)
    value_heads = values.reshape(values.shape[0], HEADS, HEAD)
    scores = jnp.einsum('qhd,khd->hqk', query_heads, key_heads, precision=highest) * HEAD ** (-0.5)
    allowed = query_ids[:, None] == key_ids[None, :]
    scores = low_back(jnp.where(allowed[None], scores, masked_score))
    row_peak = lax.optimization_barrier(jnp.max(scores, axis=-1, keepdims=True))
    log_total = row_peak + jnp.log(lax.optimization_barrier(jnp.sum(jnp.exp(scores - row_peak), axis=-1, keepdims=True)))
    weights = low(jnp.exp(scores - log_total))
    mixed_heads = jnp.einsum('hqk,khd->qhd', weights, value_heads, precision=highest)
    return mixed_heads.reshape(length, HEADS * HEAD)

def block_layer(params, block_rows, latent_ids, input_ids):
    table_rows, gain_rows, offsets, cross_query, cross_key, cross_value, cross_out, self_query, self_key, self_value, self_out, up_proj, down_proj = params
    length = latent_ids.shape[0]
    earlier = lax.optimization_barrier(jnp.sum((latent_ids[None, :] < latent_ids[:, None]).astype(jnp.int32), axis=1, dtype=jnp.int32))
    slot_index = jnp.arange(length, dtype=jnp.int32) - earlier
    start_rows = table_rows[slot_index]
    normed_latent = low(layer_norm(start_rows, gain_rows[0], offsets[0]))
    normed_input = low(layer_norm(block_rows, gain_rows[1], offsets[1]))
    queries = rounded(split_project(normed_latent, [cross_query])[0])
    key_part, value_part = split_project(normed_input, [cross_key, cross_value])
    key_rows = rounded(key_part)
    values = rounded(value_part)
    mixed_rows = rounded(attend(queries, key_rows, values, latent_ids, input_ids))
    after_cross = start_rows + merge_project(mixed_rows, cross_out)
    normed_self = low(layer_norm(after_cross, gain_rows[2], offsets[2]))
    query_part, key_part, value_part = split_project(normed_self, [self_query, self_key, self_value])
    self_queries = rounded(query_part)
    self_keys = rounded(key_part)
    self_values = rounded(value_part)
    self_mixed = rounded(attend(self_queries, self_keys, self_values, latent_ids, latent_ids))
    after_self = after_cross + merge_project(self_mixed, self_out)
    normed_mlp = low(layer_norm(after_self, gain_rows[3], offsets[3]))
    hidden = low_back(split_project(normed_mlp, [up_proj])[0])
    active = low(gelu_tanh(hidden))
    return after_self + merge_project(active, down_proj)

def reference(block_input, latent_table, latent_segments, input_segments, ln_gain, ln_bias, cross_query, cross_key, cross_value, cross_out, self_query, self_key, self_value, self_out, up_proj, down_proj, out_grad):
    params = tuple((tensor.astype(jnp.float32) for tensor in (latent_table, ln_gain, ln_bias, cross_query, cross_key, cross_value, cross_out, self_query, self_key, self_value, self_out, up_proj, down_proj)))
    inputs = block_input.astype(jnp.float32).reshape(N_DP, ROWS_DP, D)
    checked_layer = jax.checkpoint(block_layer)

    def forward(weights, rows_all):

        def one_row(row_item):
            return checked_layer(weights, row_item[0], row_item[1], row_item[2])
        return lax.map(one_row, (rows_all, latent_segments, input_segments))
    outputs, pullback = jax.vjp(forward, params, inputs)
    weight_grads, input_grads = pullback(out_grad.astype(jnp.float32).reshape(N_DP, ROWS_DP, D))
    block_output = outputs.reshape(N_DP * ROWS_DP, D).astype(jnp.float32)
    input_grad = input_grads.reshape(N_DP * ROWS_DP, D).astype(jnp.float32)
    offset_grads = weight_grads[2]
    return (block_output, input_grad, weight_grads[0], weight_grads[1], offset_grads[:3], offset_grads[3], weight_grads[3], weight_grads[4], weight_grads[5], weight_grads[6], weight_grads[7], weight_grads[8], weight_grads[9], weight_grads[10], weight_grads[11], weight_grads[12])
```

```python
import jax
import jax.numpy as jnp
from jax import lax
from jax.sharding import PartitionSpec as P

HEAD = 128


norm_eps = 1e-05
masked_score = -1e30
highest = lax.Precision.HIGHEST
gelu_coeff = 0.7978845608028654


def layer_norm(values, gain, offset):
    average = jnp.mean(values, axis=-1, keepdims=True)
    centred = values - average
    spread = jnp.mean(centred * centred, axis=-1, keepdims=True)
    return centred * lax.rsqrt(spread + norm_eps) * gain + offset


def gelu_tanh(values):
    return (
        0.5 * values * (1.0 + jnp.tanh(gelu_coeff * (values + 0.044715 * values * values * values)))
    )


def project(left, right):
    return jnp.dot(left, right, preferred_element_type=jnp.float32)


def project_back(left, right):
    return lax.dot_general(
        left, right, (((1,), (1,)), ((), ())), preferred_element_type=jnp.float32
    )


def outer_sum(left, right):
    return lax.dot_general(
        left, right, (((0,), (0,)), ((), ())), preferred_element_type=jnp.float32
    )


def rows_of(source, row_start, row_count):
    return lax.dynamic_slice_in_dim(source, row_start, row_count, 0)


def swap(values, axis, bit):
    return lax.ppermute(values, axis, [(i, i ^ bit) for i in range(lax.axis_size(axis))])


def share_rows(own):
    far = swap(own, "mp", 2)
    near = swap(own, "mp", 1)
    across = swap(far, "mp", 1)
    return jnp.concatenate([own, near, far, across])


def sum_rows(parts):
    count = parts.shape[0] // 4
    own, near, far, across = (parts[i * count : (i + 1) * count] for i in range(4))
    low = jnp.bfloat16
    got_far = swap(across.astype(low), "mp", 1)
    send_far = (far + got_far.astype(jnp.float32)).astype(low)
    got_own = swap(near.astype(low), "mp", 1)
    got_all = swap(send_far, "mp", 2)
    return own + got_own.astype(jnp.float32) + got_all.astype(jnp.float32)


def split_heads(rows):
    return rows.reshape(rows.shape[0], rows.shape[1] // HEAD, HEAD)


def block_size():
    return 512


def masked_scores(query_block, key_heads, query_ids, key_ids):
    scores = jnp.einsum(
        "qhd,khd->hqk", query_block, key_heads, preferred_element_type=jnp.float32
    ) * HEAD ** (-0.5)
    allowed = query_ids[:, None] == key_ids[None, :]
    return jnp.where(allowed[None], scores, masked_score)


def attention(queries, key_rows, values, query_ids, key_ids):
    row_total = queries.shape[0]
    local_width = queries.shape[1]
    block_rows = block_size()
    key_heads = split_heads(key_rows)
    value_heads = split_heads(values)

    def one_block(block_index):
        row_start = block_index * block_rows
        query_block = split_heads(rows_of(queries, row_start, block_rows))
        scores = masked_scores(
            query_block, key_heads, rows_of(query_ids, row_start, block_rows), key_ids
        )
        row_peak = jnp.max(scores, axis=-1, keepdims=True)
        log_total = row_peak + jnp.log(jnp.sum(jnp.exp(scores - row_peak), axis=-1, keepdims=True))
        weights = jnp.exp(scores - log_total).astype(jnp.bfloat16)
        mixed_heads = jnp.einsum(
            "hqk,khd->qhd", weights, value_heads, preferred_element_type=jnp.float32
        )
        return (mixed_heads.reshape(block_rows, local_width), log_total)

    mixed_blocks, log_blocks = lax.map(one_block, jnp.arange(row_total // block_rows))
    return (mixed_blocks.reshape(row_total, local_width).astype(jnp.bfloat16), log_blocks)


def attention_back(queries, key_rows, values, log_blocks, grad_mixed, query_ids, key_ids):
    row_total = queries.shape[0]
    local_width = queries.shape[1]
    block_rows = block_size()
    key_heads = split_heads(key_rows)
    value_heads = split_heads(values)
    score_scale = HEAD ** (-0.5)

    def one_block(running, block_item):
        block_index, log_total = block_item
        key_grad, value_grad = running
        row_start = block_index * block_rows
        query_block = split_heads(rows_of(queries, row_start, block_rows))
        grad_block = split_heads(rows_of(grad_mixed, row_start, block_rows))
        scores = masked_scores(
            query_block, key_heads, rows_of(query_ids, row_start, block_rows), key_ids
        )
        row_probs = jnp.exp(scores - log_total)
        grad_probs = jnp.einsum(
            "qhd,khd->hqk", grad_block, value_heads, preferred_element_type=jnp.float32
        )
        row_inner = jnp.sum(row_probs * grad_probs, axis=-1, keepdims=True)
        grad_scores = (row_probs * (grad_probs - row_inner)).astype(jnp.bfloat16)
        query_grad = (
            jnp.einsum("hqk,khd->qhd", grad_scores, key_heads, preferred_element_type=jnp.float32)
            * score_scale
        )
        key_grad = (
            key_grad
            + jnp.einsum(
                "hqk,qhd->khd", grad_scores, query_block, preferred_element_type=jnp.float32
            )
            * score_scale
        )
        value_grad = value_grad + jnp.einsum(
            "hqk,qhd->khd",
            row_probs.astype(jnp.bfloat16),
            grad_block,
            preferred_element_type=jnp.float32,
        )
        return ((key_grad, value_grad), query_grad.reshape(block_rows, local_width))

    zero_grads = jnp.zeros(key_heads.shape, jnp.float32)
    (key_grad, value_grad), query_blocks = lax.scan(
        one_block, (zero_grads, zero_grads), (jnp.arange(row_total // block_rows), log_blocks)
    )
    key_count = key_rows.shape[0]
    return (
        query_blocks.reshape(row_total, local_width).astype(jnp.bfloat16),
        key_grad.reshape(key_count, local_width).astype(jnp.bfloat16),
        value_grad.reshape(key_count, local_width).astype(jnp.bfloat16),
    )


def body(
    block_input,
    latent_table,
    latent_segments,
    input_segments,
    ln_gain,
    ln_bias,
    cross_query,
    cross_key,
    cross_value,
    cross_out,
    self_query,
    self_key,
    self_value,
    self_out,
    up_proj,
    down_proj,
    out_grad,
):
    low = jnp.bfloat16
    local_count = block_input.shape[0]
    member = lax.axis_index("mp")
    slots = latent_table.shape[0]
    order = [member ^ k for k in range(4)]

    def relative(ids):
        return jnp.concatenate([rows_of(ids, k * local_count, local_count) for k in order])

    row_total = latent_segments.shape[1]
    latent_abs = latent_segments[0]
    latent_ids = relative(latent_abs)
    input_ids = relative(input_segments[0])
    positions = relative(jnp.arange(row_total, dtype=jnp.int32))
    earlier = jnp.sum(
        (latent_abs[None, :] < latent_ids[:, None]).astype(jnp.int32), axis=1, dtype=jnp.int32
    )
    table_pick = (
        (positions - earlier)[:, None] == jnp.arange(slots, dtype=jnp.int32)[None, :]
    ).astype(low)
    own_pick = table_pick[:local_count]
    start_rows = project(own_pick, latent_table)
    table_rows = latent_table.astype(jnp.float32)
    normed_table = layer_norm(table_rows, ln_gain[0], ln_bias[0]).astype(low)
    input_rows = block_input.astype(jnp.float32)
    normed_input = layer_norm(input_rows, ln_gain[1], ln_bias[1]).astype(low)
    whole_input = share_rows(normed_input)
    whole_grad_out = share_rows(out_grad)
    table_queries = project(normed_table, cross_query).astype(low)
    cross_queries = project(table_pick, table_queries).astype(low)
    cross_keys = project(whole_input, cross_key).astype(low)
    cross_values = project(whole_input, cross_value).astype(low)
    cross_mixed, cross_logs = attention(
        cross_queries, cross_keys, cross_values, latent_ids, input_ids
    )
    after_cross = start_rows + sum_rows(project_back(cross_mixed, cross_out))
    normed_self = layer_norm(after_cross, ln_gain[2], ln_bias[2]).astype(low)
    whole_self = share_rows(normed_self)
    self_queries = project(whole_self, self_query).astype(low)
    self_keys = project(whole_self, self_key).astype(low)
    self_values = project(whole_self, self_value).astype(low)
    self_mixed, self_logs = attention(self_queries, self_keys, self_values, latent_ids, latent_ids)
    after_self = after_cross + sum_rows(project_back(self_mixed, self_out))
    normed_mlp = layer_norm(after_self, ln_gain[3], ln_bias[3]).astype(low)
    whole_mlp = share_rows(normed_mlp)
    hidden = project(whole_mlp, up_proj)
    active = gelu_tanh(hidden).astype(low)
    grad_active = project(whole_grad_out, down_proj)
    gelu_value, gelu_pull = jax.vjp(gelu_tanh, hidden)
    grad_hidden = gelu_pull(grad_active)[0].astype(low)
    grad_normed = sum_rows(project_back(grad_hidden, up_proj))
    block_output = after_self + sum_rows(project_back(active, down_proj))
    down_grad = outer_sum(whole_grad_out, active).astype(low)
    up_grad = outer_sum(whole_mlp, grad_hidden).astype(low)
    grad_last = out_grad.astype(jnp.float32)
    norm_value, norm_pull = jax.vjp(layer_norm, after_self, ln_gain[3], ln_bias[3])
    grad_rows, gain_mlp, bias_mlp = norm_pull(grad_normed)
    grad_self = grad_last + grad_rows
    whole_grad = share_rows(grad_self.astype(low))
    self_out_grad = outer_sum(whole_grad, self_mixed).astype(low)
    grad_mixed = project(whole_grad, self_out).astype(low)
    query_grads, key_grads, value_grads = attention_back(
        self_queries, self_keys, self_values, self_logs, grad_mixed, latent_ids, latent_ids
    )
    self_grads = outer_sum(
        whole_self, jnp.concatenate([query_grads, key_grads, value_grads], axis=1)
    ).astype(low)
    grad_normed = sum_rows(
        project_back(query_grads, self_query)
        + project_back(key_grads, self_key)
        + project_back(value_grads, self_value)
    )
    norm_value, norm_pull = jax.vjp(layer_norm, after_cross, ln_gain[2], ln_bias[2])
    grad_rows, gain_self, bias_self = norm_pull(grad_normed)
    grad_cross = grad_self + grad_rows
    whole_grad = share_rows(grad_cross.astype(low))
    cross_out_grad = outer_sum(whole_grad, cross_mixed).astype(low)
    grad_mixed = project(whole_grad, cross_out).astype(low)
    query_grads, key_grads, value_grads = attention_back(
        cross_queries, cross_keys, cross_values, cross_logs, grad_mixed, latent_ids, input_ids
    )
    slot_grads = outer_sum(table_pick, query_grads)
    cross_query_grad = outer_sum(normed_table, slot_grads.astype(low)).astype(low)
    key_value_grads = jnp.concatenate([key_grads, value_grads], axis=1)
    cross_grads = outer_sum(whole_input, key_value_grads).astype(low)
    grad_input = sum_rows(
        project_back(key_grads, cross_key) + project_back(value_grads, cross_value)
    )
    norm_value, norm_pull = jax.vjp(layer_norm, input_rows, ln_gain[1], ln_bias[1])
    grad_input_rows, gain_input, bias_input = norm_pull(grad_input)

    axes = ("dp", "mp")
    table_terms = jnp.concatenate(
        [
            project_back(slot_grads.astype(low), cross_query),
            outer_sum(own_pick, grad_cross.astype(low)),
        ],
        axis=1,
    ).astype(low)
    width = table_terms.shape[1] // 2
    table_terms = lax.psum(table_terms, axes).astype(jnp.float32)
    norm_value, norm_pull = jax.vjp(layer_norm, table_rows, ln_gain[0], ln_bias[0])
    grad_rows, gain_latent, bias_latent = norm_pull(table_terms[:, :width])
    table_grad = table_terms[:, width:] + grad_rows
    small = lax.psum(
        jnp.stack([gain_input, gain_self, gain_mlp, bias_input, bias_self, bias_mlp]), axes
    )
    ln_gain_grad = jnp.concatenate([gain_latent[None], small[:3]])
    ln_bias_grad = jnp.concatenate([bias_latent[None], small[3:5]])

    def summed(pieces):
        whole = jnp.concatenate(pieces, axis=1) if len(pieces) > 1 else pieces[0]
        return lax.psum_scatter(whole, "dp", scatter_dimension=0, tiled=True).astype(jnp.float32)

    mlp_sum = summed([up_grad, down_grad])
    self_sum = summed([self_grads, self_out_grad])
    cross_sum = summed([cross_query_grad, cross_grads, cross_out_grad])
    up_width = up_grad.shape[1]
    heads_width = cross_query.shape[1]

    def column(whole, index):
        return whole[:, index * heads_width : (index + 1) * heads_width]

    return (
        block_output,
        grad_input_rows,
        table_grad,
        ln_gain_grad,
        ln_bias_grad,
        small[5],
        column(cross_sum, 0),
        column(cross_sum, 1),
        column(cross_sum, 2),
        column(cross_sum, 3),
        column(self_sum, 0),
        column(self_sum, 1),
        column(self_sum, 2),
        column(self_sum, 3),
        mlp_sum[:, :up_width],
        mlp_sum[:, up_width:],
    )


def solution(mesh):
    placed = (
        P(("dp", "mp"), None),
        P(),
        P("dp", None),
        P("dp", None),
        P(),
        P(),
        P(None, "mp"),
        P(None, "mp"),
        P(None, "mp"),
        P(None, "mp"),
        P(None, "mp"),
        P(None, "mp"),
        P(None, "mp"),
        P(None, "mp"),
        P(None, "mp"),
        P(None, "mp"),
        P(("dp", "mp"), None),
    )
    return jax.shard_map(
        body,
        mesh=mesh,
        in_specs=placed,
        out_specs=(
            P(("dp", "mp"), None),
            P(("dp", "mp"), None),
            P(),
            P(),
            P(),
            P(),
            P("dp", "mp"),
            P("dp", "mp"),
            P("dp", "mp"),
            P("dp", "mp"),
            P("dp", "mp"),
            P("dp", "mp"),
            P("dp", "mp"),
            P("dp", "mp"),
            P("dp", "mp"),
            P("dp", "mp"),
        ),
        check_vma=False,
    )
```

```python
import jax
import jax.numpy as jnp
import numpy as np
from jax import lax
from jax.experimental import pallas as pl
from jax.experimental.pallas import tpu as pltpu
from jax.sharding import PartitionSpec as P

HEAD = 128
norm_eps = 1e-05
masked_score = -1e30
gelu_coeff = 0.7978845608028654
gelu_cubic = 0.044715
log2_e = 1.4426950408889634
score_scale = HEAD ** (-0.5)
exp2_scale = score_scale * log2_e
LOW = jnp.bfloat16
F32 = jnp.float32
VMEM_BYTES = 40 * 1024 * 1024


def layer_norm(values, gain, offset):
    average = jnp.mean(values, axis=-1, keepdims=True)
    centred = values - average
    spread = jnp.mean(centred * centred, axis=-1, keepdims=True)
    return centred * lax.rsqrt(spread + norm_eps) * gain + offset


def layer_norm_back(values, gain, grad):
    average = jnp.mean(values, axis=-1, keepdims=True)
    centred = values - average
    spread = jnp.mean(centred * centred, axis=-1, keepdims=True)
    inverse = lax.rsqrt(spread + norm_eps)
    normal = centred * inverse
    scaled = grad * gain
    inner = jnp.mean(scaled * normal, axis=-1, keepdims=True)
    back = inverse * (scaled - jnp.mean(scaled, axis=-1, keepdims=True) - normal * inner)
    return (
        back,
        jnp.sum(grad * normal, axis=0, keepdims=True),
        jnp.sum(grad, axis=0, keepdims=True),
    )


def dot(left, right):
    return jnp.dot(left, right, preferred_element_type=F32)


def dot_last(left, right):
    return lax.dot_general(left, right, (((1,), (1,)), ((), ())), preferred_element_type=F32)


def dot_first(left, right):
    return lax.dot_general(left, right, (((0,), (0,)), ((), ())), preferred_element_type=F32)


def shape(dims, kind=F32):
    return jax.ShapeDtypeStruct(dims, kind)


def local_kernel(body, name, ins, outs, scratch=(), smem=(), flops=0):
    spaces = [pltpu.SMEM if i in smem else pltpu.VMEM for i in range(len(ins))]
    moved = sum(int(np.prod(a.shape)) * a.dtype.itemsize for a in list(ins) + list(outs))
    return pl.pallas_call(
        body,
        name=name,
        out_shape=list(outs),
        in_specs=[pl.BlockSpec(memory_space=s) for s in spaces],
        out_specs=[pl.BlockSpec(memory_space=pltpu.VMEM)] * len(outs),
        scratch_shapes=list(scratch),
        compiler_params=pltpu.CompilerParams(vmem_limit_bytes=VMEM_BYTES),
        cost_estimate=pl.CostEstimate(flops=int(flops), bytes_accessed=moved, transcendentals=0),
    )(*ins)


def swap(values, axis, bit):
    return lax.ppermute(values, axis, [(i, i ^ bit) for i in range(lax.axis_size(axis))])


def share_rows(own):
    far = swap(own, "mp", 2)
    near = swap(own, "mp", 1)
    return near, far, swap(far, "mp", 1)


def send_far(far_part, across_part):
    got = swap(across_part, "mp", 1)
    return swap((far_part + got.astype(F32)).astype(LOW), "mp", 2)


def axis_bits():
    bits = []
    for axis in ("mp", "dp"):
        bits += [(axis, 1 << i) for i in range(lax.axis_size(axis).bit_length() - 1)]
    return bits


def reversed_bits(count):
    width = count.bit_length() - 1
    return np.array([int(format(i, "b").zfill(width)[::-1], 2) if width else 0 for i in range(count)], np.int32)


def scatter_sum(keep, sent, bits):
    for step, (axis, bit) in enumerate(bits):
        if step:
            half = keep.shape[0] // 2
            keep, sent = keep[:half], keep[half:].astype(LOW)
        keep = keep + swap(sent, axis, bit).astype(F32)
    return keep


def gather_back(values, bits):
    for axis, bit in reversed(bits):
        values = jnp.concatenate([values, swap(values, axis, bit)])
    return values


def sum_everywhere(values, bits):
    for axis, bit in bits:
        values = values + swap(values, axis, bit)
    return values


def tile_active(bounds, block, tile):
    return (bounds[2, tile] <= bounds[1, block]) & (bounds[3, tile] >= bounds[0, block])


def attend_block(block, queries, keys, value_ts, q_ids, k_ids, bounds, mixed, row, logs, scratch):
    scores, peak, total, acc = scratch
    count = queries.shape[0] // 2
    heads = queries.shape[1] // HEAD
    query_rows = queries[row : row + count, :]
    ids = q_ids[:, block * count : (block + 1) * count]
    peak[...] = jnp.full(peak.shape, masked_score, F32)
    total[...] = jnp.zeros(total.shape, F32)
    acc[...] = jnp.zeros(acc.shape, F32)
    for tile in range(4):
        inner = (tile % 2) * count

        @pl.when(tile_active(bounds, block, tile))
        def _(tile=tile, inner=inner):
            allowed = k_ids[tile * count : (tile + 1) * count, :] == ids
            for h in range(heads):
                cols = slice(h * HEAD, (h + 1) * HEAD)
                part = dot_last(keys[tile // 2][inner : inner + count, cols], query_rows[:, cols])
                part = jnp.where(allowed, part, masked_score)
                scores[h, tile] = part
                peak[h : h + 1, :] = jnp.maximum(
                    peak[h : h + 1, :], jnp.max(part, axis=0, keepdims=True)
                )

    for tile in range(4):
        inner = (tile % 2) * count

        @pl.when(tile_active(bounds, block, tile))
        def _(tile=tile, inner=inner):
            for h in range(heads):
                weights = jnp.exp2((scores[h, tile] - peak[h : h + 1, :]) * exp2_scale)
                total[h : h + 1, :] += jnp.sum(weights, axis=0, keepdims=True)
                acc[h] += dot(
                    value_ts[tile // 2][h * HEAD : (h + 1) * HEAD, inner : inner + count],
                    weights.astype(LOW),
                )

    for h in range(heads):
        sums = total[h : h + 1, :]
        mixed[row : row + count, h * HEAD : (h + 1) * HEAD] = (acc[h] / sums).T.astype(LOW)
        logs[h : h + 1, row : row + count] = peak[h : h + 1, :] * exp2_scale + jnp.log2(sums)


def attend_scratch(count, heads):
    return [
        pltpu.VMEM((heads, 4, count, count), F32),
        pltpu.VMEM((8, count), F32),
        pltpu.VMEM((8, count), F32),
        pltpu.VMEM((heads, HEAD, count), F32),
    ]


def project_pair(blocks, weights, transposed, flops_of=None):
    count, width = blocks[0].shape[0], weights[0].shape[1]
    outs = [shape((2 * count, width), LOW) for w in weights]
    outs += [shape((width, 2 * count), LOW) for i in transposed]

    def body(*refs):
        ins, res = refs[: 2 + len(weights)], refs[2 + len(weights) :]
        project_into(ins[:2], ins[2:], res, transposed)

    return local_kernel(
        body, "project_pair", list(blocks) + list(weights), outs,
        flops=4 * count * blocks[0].shape[1] * width * len(weights),
    )


def project_into(blocks, weights, res, transposed):
    count = blocks[0].shape[0]
    for i, weight in enumerate(weights):
        for b in range(2):
            part = dot(blocks[b][...], weight[...])
            res[i][b * count : (b + 1) * count, :] = part.astype(LOW)
            if i in transposed:
                res[len(weights) + transposed.index(i)][:, b * count : (b + 1) * count] = (
                    part.T.astype(LOW)
                )


def attend_far(far, across, weights, queries, near_set, out_weight, ids):
    count = far.shape[0]
    width = out_weight.shape[1]
    heads = width // HEAD
    with_query = len(weights) == 3
    q_ids, k_ids, bounds = ids
    ins = [far, across, *weights, near_set[0], near_set[2], out_weight, q_ids, k_ids, bounds]
    if not with_query:
        ins.append(queries)
    n_weights = len(weights)
    pair = shape((2 * count, width), LOW)
    turned = shape((width, 2 * count), LOW)
    outs = [pair] * n_weights + [turned, turned]
    outs += [pair, shape((8, 2 * count)), shape((count, far.shape[1])), shape((count, far.shape[1]), LOW)]

    def body(*refs):
        n_in = len(ins)
        refs_in, res, scratch = refs[:n_in], refs[n_in : n_in + len(outs)], refs[n_in + len(outs) :]
        blocks, ws = refs_in[:2], refs_in[2 : 2 + n_weights]
        near_keys, near_values, wo, qi, ki, bnd = refs_in[2 + n_weights : 8 + n_weights]
        project_into(blocks, ws, res[: n_weights + 2], [0, 1])
        query_ref = res[2] if with_query else refs_in[-1]
        mixed, logs, far_out, across_out = res[n_weights + 2 :]
        for b in (1, 0):
            attend_block(
                2 + b, query_ref, (near_keys, res[0]), (near_values, res[n_weights + 1]),
                qi, ki, bnd, mixed, b * count, logs, scratch,
            )
            part = dot_last(mixed[b * count : (b + 1) * count, :], wo[...])
            if b:
                across_out[...] = part.astype(LOW)
            else:
                far_out[...] = part

    flops = 4 * count * far.shape[1] * width * (n_weights + 1) + 2 * 4 * count * 2 * count * width
    return local_kernel(
        body, "attend_far", ins, outs, attend_scratch(count, heads), smem=(7 + n_weights,), flops=flops
    )


def attend_near(queries, near_set, far_set, out_weight, ids):
    width = out_weight.shape[1]
    heads = width // HEAD
    count = queries.shape[0] // 2
    dim = out_weight.shape[0]
    q_ids, k_ids, bounds = ids
    ins = [queries, near_set[0], far_set[0], near_set[1], far_set[1], out_weight, q_ids, k_ids, bounds]
    outs = [
        shape((2 * count, width), LOW), shape((8, 2 * count)),
        shape((count, dim)), shape((count, dim), LOW),
    ]

    def body(q, k0, k1, v0, v1, wo, qi, ki, bnd, mixed, logs, own_out, near_out, *scratch):
        for b in (1, 0):
            attend_block(b, q, (k0, k1), (v0, v1), qi, ki, bnd, mixed, b * count, logs, scratch)
            part = dot_last(mixed[b * count : (b + 1) * count, :], wo[...])
            if b:
                near_out[...] = part.astype(LOW)
            else:
                own_out[...] = part

    flops = 4 * count * dim * width + 2 * 4 * count * 2 * count * width
    return local_kernel(body, "attend_near", ins, outs, attend_scratch(count, heads), smem=(8,), flops=flops)


def back_block(block, row, grads, queries, logs, keys, key_ts, values, q_ids, k_ids, bounds,
               query_grads, key_acc, value_acc, scratch):
    probs, grad_probs, inner_sum, acc = scratch
    count = queries.shape[0] // 2
    heads = queries.shape[1] // HEAD
    query_rows = queries[row : row + count, :]
    ids = q_ids[:, block * count : (block + 1) * count]
    inner_sum[...] = jnp.zeros(inner_sum.shape, F32)
    acc[...] = jnp.zeros(acc.shape, F32)
    for tile in range(4):
        inner = (tile % 2) * count

        @pl.when(tile_active(bounds, block, tile))
        def _(tile=tile, inner=inner):
            allowed = k_ids[tile * count : (tile + 1) * count, :] == ids
            for h in range(heads):
                cols = slice(h * HEAD, (h + 1) * HEAD)
                part = dot_last(keys[tile // 2][inner : inner + count, cols], query_rows[:, cols])
                exact = jnp.where(
                    allowed,
                    jnp.exp2(part * exp2_scale - logs[h : h + 1, row : row + count]),
                    0.0,
                )
                pulled = dot_last(values[tile // 2][inner : inner + count, cols], grads[:, cols])
                probs[h, tile] = exact
                grad_probs[h, tile] = pulled
                inner_sum[h : h + 1, :] += jnp.sum(exact * pulled, axis=0, keepdims=True)
                value_acc[tile * count : (tile + 1) * count, cols] += dot(
                    exact.astype(LOW), grads[:, cols]
                )

    for tile in range(4):
        inner = (tile % 2) * count

        @pl.when(tile_active(bounds, block, tile))
        def _(tile=tile, inner=inner):
            for h in range(heads):
                cols = slice(h * HEAD, (h + 1) * HEAD)
                score_grads = (
                    probs[h, tile] * (grad_probs[h, tile] - inner_sum[h : h + 1, :])
                ).astype(LOW)
                key_acc[tile * count : (tile + 1) * count, cols] += dot(
                    score_grads, query_rows[:, cols]
                )
                acc[h] += dot(key_ts[tile // 2][cols, inner : inner + count], score_grads)

    for h in range(heads):
        query_grads[row : row + count, h * HEAD : (h + 1) * HEAD] = (
            (acc[h] * score_scale).T.astype(LOW)
        )


def back_scratch(count, heads):
    return [
        pltpu.VMEM((heads, 4, count, count), F32),
        pltpu.VMEM((heads, 4, count, count), F32),
        pltpu.VMEM((8, count), F32),
        pltpu.VMEM((heads, HEAD, count), F32),
    ]


def back_near(grads, out_weight, queries, logs, kept, ids):
    count = queries.shape[0] // 2
    width = queries.shape[1]
    q_ids, k_ids, bounds = ids
    ins = [*grads, out_weight, queries, logs, *kept, q_ids, k_ids, bounds]
    outs = [shape((2 * count, width), LOW), shape((4 * count, width)), shape((4 * count, width))]

    def body(g0, g1, wo, q, lg, k0, k1, t0, t1, v0, v1, qi, ki, bnd, dq, dk, dv, *scratch):
        dk[...] = jnp.zeros(dk.shape, F32)
        dv[...] = jnp.zeros(dv.shape, F32)
        for b, g in enumerate((g0, g1)):
            mixed_grads = dot(g[...], wo[...]).astype(LOW)
            back_block(b, b * count, mixed_grads, q, lg, (k0, k1), (t0, t1), (v0, v1), qi, ki, bnd,
                       dq, dk, dv, scratch)

    flops = 4 * count * out_weight.shape[0] * width + 2 * 10 * count * 2 * count * width
    return local_kernel(body, "back_near", ins, outs, back_scratch(count, width // HEAD), smem=(13,), flops=flops)


def back_far(grads, out_weight, queries, logs, kept, ids, sums, weights):
    count = queries.shape[0] // 2
    width = queries.shape[1]
    dim = out_weight.shape[0]
    q_ids, k_ids, bounds = ids
    ins = [*grads, out_weight, queries, logs, *kept, q_ids, k_ids, bounds, *sums, *weights]
    whole = shape((4 * count, width), LOW)
    outs = [shape((2 * count, width), LOW), whole, whole, shape((count, dim)), shape((count, dim), LOW)]

    def body(*refs):
        g0, g1, wo, q, lg, k0, k1, t0, t1, v0, v1, qi, ki, bnd, dk_in, dv_in = refs[:16]
        ws = refs[16 : 16 + len(weights)]
        dq, dk, dv, far_out, across_out, key_acc, value_acc, *scratch = refs[16 + len(weights) :]
        key_acc[...] = dk_in[...]
        value_acc[...] = dv_in[...]
        for b, g in enumerate((g0, g1)):
            mixed_grads = dot(g[...], wo[...]).astype(LOW)
            back_block(2 + b, b * count, mixed_grads, q, lg, (k0, k1), (t0, t1), (v0, v1), qi, ki, bnd,
                       dq, key_acc, value_acc, scratch)
        dk[...] = (key_acc[...] * score_scale).astype(LOW)
        dv[...] = value_acc[...].astype(LOW)
        for b in (1, 0):
            rows = slice((2 + b) * count, (3 + b) * count)
            part = dot_last(dk[rows, :], ws[0][...]) + dot_last(dv[rows, :], ws[1][...])
            if len(ws) == 3:
                part = part + dot_last(dq[b * count : (b + 1) * count, :], ws[2][...])
            if b:
                across_out[...] = part.astype(LOW)
            else:
                far_out[...] = part

    scratch = [pltpu.VMEM((4 * count, width), F32)] * 2 + back_scratch(count, width // HEAD)
    flops = 4 * count * dim * width * (1 + len(weights)) + 2 * 10 * count * 2 * count * width
    return local_kernel(body, "back_far", ins, outs, scratch, smem=(13,), flops=flops)


def pull_near(pairs):
    dim = pairs[0][1].shape[0]
    count = pairs[0][2]
    ins = [p[0] for p in pairs] + [p[1] for p in pairs]
    outs = [shape((count, dim)), shape((count, dim), LOW)]

    def body(*refs):
        n = len(pairs)
        own_out, near_out = refs[2 * n :]
        for b in range(2):
            part = None
            for i in range(n):
                term = dot_last(refs[i][b * count : (b + 1) * count, :], refs[n + i][...])
                part = term if part is None else part + term
            if b:
                near_out[...] = part.astype(LOW)
            else:
                own_out[...] = part

    flops = sum(4 * count * dim * p[1].shape[1] for p in pairs)
    return local_kernel(body, "pull_near", ins, outs, flops=flops)


def mlp_pair(rows, grads, up_proj, down_proj):
    count, dim = rows[0].shape
    units = up_proj.shape[1]
    step = 256
    outs = [
        shape((2 * count, units), LOW), shape((2 * count, units), LOW),
        shape((count, dim)), shape((count, dim), LOW),
    ]

    def body(x0, x1, g0, g1, up, down, active, grad_hidden, first_out, second_out):
        for b, (x, g) in enumerate(((x0, g0), (x1, g1))):
            for at in range(0, units, step):
                hidden = dot(x[...], up[:, at : at + step])
                pulled = dot(g[...], down[:, at : at + step])
                square = hidden * hidden
                bent = jnp.tanh(gelu_coeff * (hidden + gelu_cubic * hidden * square))
                half = 0.5 * (1.0 + bent)
                slope = half + 0.5 * hidden * (1.0 - bent * bent) * (
                    gelu_coeff * (1.0 + 3.0 * gelu_cubic * square)
                )
                active[b * count : (b + 1) * count, at : at + step] = (hidden * half).astype(LOW)
                grad_hidden[b * count : (b + 1) * count, at : at + step] = (pulled * slope).astype(LOW)
        for b in (1, 0):
            part = dot_last(grad_hidden[b * count : (b + 1) * count, :], up[...])
            if b:
                second_out[...] = part.astype(LOW)
            else:
                first_out[...] = part

    return local_kernel(
        body, "mlp_pair", [*rows, *grads, up_proj, down_proj], outs, flops=12 * count * dim * units
    )


def pull_pair(rows, weight):
    count, dim = rows.shape[0] // 2, weight.shape[0]
    outs = [shape((count, dim)), shape((count, dim), LOW)]

    def body(x, w, first_out, second_out):
        first_out[...] = dot_last(x[:count, :], w[...])
        second_out[...] = dot_last(x[count:, :], w[...]).astype(LOW)

    return local_kernel(body, "pull_pair", [rows, weight], outs, flops=4 * count * dim * weight.shape[1])


def norm_rows(terms, gain, offset):
    kept = terms[0]

    def body(k, p, n, f, g, o, after, normed):
        total = k[...] + p[...] + n[...].astype(F32) + f[...].astype(F32)
        after[...] = total
        normed[...] = layer_norm(total, g[...], o[...]).astype(LOW)

    return local_kernel(
        body, "norm_rows", [*terms, gain, offset], [shape(kept.shape), shape(kept.shape, LOW)]
    )


def norm_rows_back(values, gain, terms, grads):
    def body(v, g, p, n, f, dy, out, out_low, sums):
        total = p[...] + n[...].astype(F32) + f[...].astype(F32)
        back, gain_sum, offset_sum = layer_norm_back(v[...].astype(F32), g[...], total)
        if grads is not None:
            back = back + dy[...].astype(F32)
            out_low[...] = back.astype(LOW)
        out[...] = back
        sums[0:1, :] = gain_sum
        sums[1:2, :] = offset_sum

    ins = [values, gain, *terms]
    outs = [shape(values.shape)]
    if grads is not None:
        ins.append(grads)
        outs.append(shape(values.shape, LOW))
    outs.append(shape((2, values.shape[1])))
    if grads is None:
        def plain(v, g, p, n, f, out, sums):
            body(v, g, p, n, f, None, out, None, sums)
        return local_kernel(plain, "norm_back", ins, outs)
    return local_kernel(body, "norm_back", ins, outs)


def outer_sums(groups, dp_bits):
    n_dp = lax.axis_size("dp")
    dim = groups[0][0][0].shape[1]
    chunk = dim // n_dp
    turn = reversed_bits(n_dp)
    place = lax.axis_index("dp")
    aligned = chunk % 128 == 0
    ins, plan = [], []
    for blocks, rights in groups:
        left_at = len(ins)
        ins += list(blocks)
        right_list = []
        for parts in rights:
            right_list.append((len(ins), len(parts), parts[0].shape[1]))
            ins += list(parts)
        plan.append((left_at, len(blocks), blocks[0].shape[0], right_list))
    width = sum(r[2] for p in plan for r in p[3])
    where = (jnp.asarray(turn) ^ place if aligned else jnp.arange(n_dp, dtype=jnp.int32)).reshape(1, n_dp)
    steps = n_dp if aligned else dim // 128
    if not aligned:
        where = jnp.arange(steps, dtype=jnp.int32).reshape(1, steps)
    ins.append(where.astype(jnp.int32))
    rows = dim // 2
    outs = [shape((rows, width)), shape((rows, width), LOW)]

    def body(*refs):
        spots = refs[len(ins) - 1]
        keep, sent = refs[len(ins) :]

        def one(index, target, base):
            at = pl.multiple_of(spots[0, base + index] * 128, 128)
            column = 0
            for left_at, n_blocks, count, rights in plan:
                for right_at, n_parts, right_width in rights:
                    total = None
                    per = n_blocks // n_parts
                    for b in range(n_blocks):
                        right = refs[right_at + b // per][(b % per) * count : (b % per + 1) * count, :]
                        term = dot_first(refs[left_at + b][:, pl.ds(at, 128)], right)
                        total = term if total is None else total + term
                    target[pl.ds(pl.multiple_of(index * 128, 128), 128), column : column + right_width] = (
                        total.astype(target.dtype)
                    )
                    column += right_width

        @pl.loop(0, steps // 2)
        def _(index):
            one(index, sent, steps // 2)

        @pl.loop(0, steps // 2)
        def _(index):
            one(index, keep, 0)

    flops = 2 * dim * sum(p[1] * p[2] * r[2] for p in plan for r in p[3])
    keep, sent = local_kernel(body, "outer_sums", ins, outs, smem=(len(ins) - 1,), flops=flops)
    if not aligned:
        whole = jnp.concatenate([keep, sent.astype(F32)]).reshape(n_dp, chunk, width)
        whole = whole[jnp.asarray(turn) ^ place].reshape(dim, width)
        keep, sent = whole[:rows], whole[rows:].astype(LOW)
    return scatter_sum(keep, sent, dp_bits)


def rows_of(source, row_start, row_count):
    return lax.dynamic_slice_in_dim(source, row_start, row_count, 0)


def body(
    block_input,
    latent_table,
    latent_segments,
    input_segments,
    ln_gain,
    ln_bias,
    cross_query,
    cross_key,
    cross_value,
    cross_out,
    self_query,
    self_key,
    self_value,
    self_out,
    up_proj,
    down_proj,
    out_grad,
):
    count, dim = block_input.shape
    member = lax.axis_index("mp")
    n_mp, n_dp = lax.axis_size("mp"), lax.axis_size("dp")
    place = member + n_mp * lax.axis_index("dp")
    slots = latent_table.shape[0]
    order = [member ^ k for k in range(n_mp)]
    bits = axis_bits()
    dp_bits = [b for b in bits if b[0] == "dp"]
    gains = [ln_gain[i : i + 1] for i in range(4)]
    offsets = [ln_bias[i : i + 1] for i in range(4)]

    def relative(ids):
        return jnp.concatenate([rows_of(ids, k * count, count) for k in order])

    normed_input = layer_norm(block_input.astype(F32), gains[1], offsets[1]).astype(LOW)
    near_input, far_input, across_input = share_rows(normed_input)
    near_out, far_out, across_out = share_rows(out_grad)

    row_total = latent_segments.shape[1]
    latent_abs = latent_segments[0]
    latent_ids = relative(latent_abs)
    input_ids = relative(input_segments[0])
    positions = relative(jnp.arange(row_total, dtype=jnp.int32))

    def ends(ids):
        blocks = ids.reshape(n_mp, count)
        return [blocks[:, 0], blocks[:, -1]]

    def id_set(query_ids, key_ids):
        return (
            query_ids.reshape(1, row_total),
            key_ids.reshape(row_total, 1),
            jnp.stack(ends(query_ids) + ends(key_ids)),
        )

    cross_ids = id_set(latent_ids, input_ids)
    self_ids = id_set(latent_ids, latent_ids)
    earlier = jnp.sum(
        (latent_abs[None, :] < latent_ids[:, None]).astype(jnp.int32), axis=1, dtype=jnp.int32
    )
    slot_index = positions - earlier
    slot_range = jnp.arange(slots, dtype=jnp.int32)
    table_pick = (slot_index[:, None] == slot_range[None, :]).astype(LOW)
    own_pick = table_pick[:count]
    start_rows = dot(own_pick, latent_table)
    table_rows = latent_table.astype(F32)
    normed_table = layer_norm(table_rows, gains[0], offsets[0]).astype(LOW)
    table_queries = dot(normed_table, cross_query).astype(LOW)
    cross_queries = dot(table_pick, table_queries).astype(LOW)
    queries_near, queries_far = cross_queries[: 2 * count], cross_queries[2 * count :]

    keys_near, values_near, key_ts_near, value_ts_near = project_pair(
        (normed_input, near_input), (cross_key, cross_value), [0, 1]
    )
    (keys_far, values_far, key_ts_far, value_ts_far, mixed_far, logs_far, part_far, part_across) = attend_far(
        far_input, across_input, (cross_key, cross_value), queries_far,
        (keys_near, key_ts_near, value_ts_near), cross_out, cross_ids,
    )
    got_far = send_far(part_far, part_across)
    mixed_near, logs_near, part_own, part_near = attend_near(
        queries_near, (keys_near, value_ts_near), (keys_far, value_ts_far), cross_out, cross_ids
    )
    cross_kept = (keys_near, keys_far, key_ts_near, key_ts_far, values_near, values_far)
    cross_queries_set = (queries_near, queries_far)
    cross_logs = (logs_near, logs_far)
    cross_mixed = (mixed_near, mixed_far)
    after_cross, normed_self = norm_rows(
        (start_rows, part_own, swap(part_near, "mp", 1), got_far), gains[2], offsets[2]
    )

    near_self, far_self, across_self = share_rows(normed_self)
    self_weights = (self_key, self_value, self_query)
    keys_near, values_near, queries_near, key_ts_near, value_ts_near = project_pair(
        (normed_self, near_self), self_weights, [0, 1]
    )
    (keys_far, values_far, queries_far, key_ts_far, value_ts_far, mixed_far, logs_far, part_far,
     part_across) = attend_far(
        far_self, across_self, self_weights, None,
        (keys_near, key_ts_near, value_ts_near), self_out, self_ids,
    )
    got_far = send_far(part_far, part_across)
    mixed_near, logs_near, part_own, part_near = attend_near(
        queries_near, (keys_near, value_ts_near), (keys_far, value_ts_far), self_out, self_ids
    )
    self_kept = (keys_near, keys_far, key_ts_near, key_ts_far, values_near, values_far)
    self_queries_set = (queries_near, queries_far)
    self_logs = (logs_near, logs_far)
    self_mixed = (mixed_near, mixed_far)
    after_self, normed_mlp = norm_rows(
        (after_cross, part_own, swap(part_near, "mp", 1), got_far), gains[3], offsets[3]
    )

    near_mlp, far_mlp, across_mlp = share_rows(normed_mlp)
    active_near, hidden_near, part_own, part_near = mlp_pair(
        (normed_mlp, near_mlp), (out_grad, near_out), up_proj, down_proj
    )
    active_far, hidden_far, part_far, part_across = mlp_pair(
        (far_mlp, across_mlp), (far_out, across_out), up_proj, down_proj
    )
    got_far = send_far(part_far, part_across)
    grad_self, dy_own, mlp_sums = norm_rows_back(
        after_self, gains[3], (part_own, swap(part_near, "mp", 1), got_far), out_grad
    )
    near_dy, far_dy, across_dy = share_rows(dy_own)
    part_far, part_across = pull_pair(active_far, down_proj)
    got_far = send_far(part_far, part_across)
    part_own, part_near = pull_pair(active_near, down_proj)
    block_output = (
        after_self + part_own + swap(part_near, "mp", 1).astype(F32) + got_far.astype(F32)
    )
    mlp_sum = outer_sums(
        [
            ((normed_mlp, near_mlp, far_mlp, across_mlp), [(hidden_near, hidden_far)]),
            ((out_grad, near_out, far_out, across_out), [(active_near, active_far)]),
        ],
        dp_bits,
    )

    query_near, key_sum, value_sum = back_near(
        (dy_own, near_dy), self_out, self_queries_set[0], self_logs[0], self_kept, self_ids
    )
    query_far, key_grads, value_grads, part_far, part_across = back_far(
        (far_dy, across_dy), self_out, self_queries_set[1], self_logs[1], self_kept, self_ids,
        (key_sum, value_sum), self_weights,
    )
    got_far = send_far(part_far, part_across)
    part_own, part_near = pull_near(
        [(key_grads, self_key, count), (value_grads, self_value, count), (query_near, self_query, count)]
    )
    grad_cross, dy_cross, self_sums = norm_rows_back(
        after_cross, gains[2], (part_own, swap(part_near, "mp", 1), got_far), grad_self
    )
    near_dyc, far_dyc, across_dyc = share_rows(dy_cross)
    self_sum = outer_sums(
        [
            (
                (normed_self, near_self, far_self, across_self),
                [(query_near, query_far), (key_grads,), (value_grads,)],
            ),
            ((dy_own, near_dy, far_dy, across_dy), [self_mixed]),
        ],
        dp_bits,
    )

    query_near, key_sum, value_sum = back_near(
        (dy_cross, near_dyc), cross_out, cross_queries_set[0], cross_logs[0], cross_kept, cross_ids
    )
    query_far, key_grads, value_grads, part_far, part_across = back_far(
        (far_dyc, across_dyc), cross_out, cross_queries_set[1], cross_logs[1], cross_kept, cross_ids,
        (key_sum, value_sum), (cross_key, cross_value),
    )
    got_far = send_far(part_far, part_across)
    part_own, part_near = pull_near([(key_grads, cross_key, count), (value_grads, cross_value, count)])
    grad_input, input_sums = norm_rows_back(
        block_input, gains[1], (part_own, swap(part_near, "mp", 1), got_far), None
    )

    slot_grads = (
        dot_first(table_pick[: 2 * count], query_near) + dot_first(table_pick[2 * count :], query_far)
    ).astype(LOW)
    n_all = n_mp * n_dp
    per = slots // n_all
    turn = jnp.asarray(reversed_bits(n_all))
    slot_of = ((turn ^ place)[:, None] * per + jnp.arange(per, dtype=jnp.int32)[None, :]).reshape(slots)
    turned = (slot_of[:, None] == slot_range[None, :]).astype(LOW)
    slot_terms = jnp.concatenate(
        [
            dot_last(dot(turned, slot_grads).astype(LOW), cross_query),
            dot(turned, dot_first(own_pick, dy_cross).astype(LOW)),
        ],
        axis=1,
    )
    half = slots // 2
    slot_terms = scatter_sum(slot_terms[:half], slot_terms[half:].astype(LOW), bits)
    grad_rows, gain_latent, offset_latent = layer_norm_back(
        rows_of(table_rows, place * per, per), gains[0], slot_terms[:, :dim]
    )
    table_own = (slot_terms[:, dim:] + grad_rows).astype(LOW)
    table_grad = dot_first(turned, gather_back(table_own, bits))
    small = sum_everywhere(
        jnp.concatenate([gain_latent, offset_latent, input_sums, self_sums, mlp_sums]), bits
    )
    ln_gain_grad = jnp.concatenate([small[0:1], small[2:3], small[4:5], small[6:7]])
    ln_bias_grad = jnp.concatenate([small[1:2], small[3:4], small[5:6]])

    query_blocks = tuple(normed_table[i : i + count] for i in range(0, slots, count))
    cross_sum = outer_sums(
        [
            ((normed_table,), [(slot_grads,)]),
            ((normed_input, near_input, far_input, across_input), [(key_grads,), (value_grads,)]),
            ((dy_cross, near_dyc, far_dyc, across_dyc), [cross_mixed]),
        ],
        dp_bits,
    )
    up_width = up_proj.shape[1]
    heads_width = cross_query.shape[1]

    def column(whole, index):
        return whole[:, index * heads_width : (index + 1) * heads_width]

    return (
        block_output,
        grad_input,
        table_grad,
        ln_gain_grad,
        ln_bias_grad,
        small[7],
        column(cross_sum, 0),
        column(cross_sum, 1),
        column(cross_sum, 2),
        column(cross_sum, 3),
        column(self_sum, 0),
        column(self_sum, 1),
        column(self_sum, 2),
        column(self_sum, 3),
        mlp_sum[:, :up_width],
        mlp_sum[:, up_width:],
    )


def solution(mesh):
    placed = (
        P(("dp", "mp"), None),
        P(),
        P("dp", None),
        P("dp", None),
        P(),
        P(),
        P(None, "mp"),
        P(None, "mp"),
        P(None, "mp"),
        P(None, "mp"),
        P(None, "mp"),
        P(None, "mp"),
        P(None, "mp"),
        P(None, "mp"),
        P(None, "mp"),
        P(None, "mp"),
        P(("dp", "mp"), None),
    )
    return jax.shard_map(
        body,
        mesh=mesh,
        in_specs=placed,
        out_specs=(
            P(("dp", "mp"), None),
            P(("dp", "mp"), None),
            P(),
            P(),
            P(),
            P(),
            P("dp", "mp"),
            P("dp", "mp"),
            P("dp", "mp"),
            P("dp", "mp"),
            P("dp", "mp"),
            P("dp", "mp"),
            P("dp", "mp"),
            P("dp", "mp"),
            P("dp", "mp"),
            P("dp", "mp"),
        ),
        check_vma=False,
    )
```

```python
import jax
import jax.numpy as jnp
import numpy as np
from jax import lax
from jax.experimental import pallas as pl
from jax.experimental.pallas import tpu as pltpu
from jax.sharding import PartitionSpec as P

HEAD = 128
images = 16
norm_eps = 1e-05
masked_score = -1e30
gelu_coeff = 0.7978845608028654
gelu_cubic = 0.044715
log2_e = 1.4426950408889634
score_scale = HEAD ** (-0.5)
exp2_scale = score_scale * log2_e
LOW = jnp.bfloat16
F32 = jnp.float32
VMEM_BYTES = 32 * 1024 * 1024


def layer_norm(values, gain, offset):
    average = jnp.mean(values, axis=-1, keepdims=True)
    centred = values - average
    spread = jnp.mean(centred * centred, axis=-1, keepdims=True)
    return centred * lax.rsqrt(spread + norm_eps) * gain + offset


def layer_norm_back(values, gain, grad):
    average = jnp.mean(values, axis=-1, keepdims=True)
    centred = values - average
    spread = jnp.mean(centred * centred, axis=-1, keepdims=True)
    inverse = lax.rsqrt(spread + norm_eps)
    normal = centred * inverse
    scaled = grad * gain
    inner = jnp.mean(scaled * normal, axis=-1, keepdims=True)
    back = inverse * (scaled - jnp.mean(scaled, axis=-1, keepdims=True) - normal * inner)
    return (
        back,
        jnp.sum(grad * normal, axis=0, keepdims=True),
        jnp.sum(grad, axis=0, keepdims=True),
    )


def dot(left, right):
    return jnp.dot(left, right, preferred_element_type=F32)


def dot_last(left, right):
    return lax.dot_general(left, right, (((1,), (1,)), ((), ())), preferred_element_type=F32)


def dot_first(left, right):
    return lax.dot_general(left, right, (((0,), (0,)), ((), ())), preferred_element_type=F32)


def shape(dims, kind=F32):
    return jax.ShapeDtypeStruct(dims, kind)


def local_kernel(body, name, ins, outs, scratch=(), smem=(), cold=None, cold_outs=(), smem_outs=(), after=()):
    n_in, n_after, n_out = len(ins), len(after), len(outs)
    groups = [list(g) for g in (cold or [])]
    moved = [i for g in groups for i in g]
    held = [pltpu.VMEM(ins[i].shape, ins[i].dtype) for i in moved]
    held += [pltpu.VMEM(outs[o].shape, outs[o].dtype) for o in cold_outs]
    sems = []
    if moved:
        sems.append(pltpu.SemaphoreType.DMA((len(moved),)))
    if cold_outs:
        sems.append(pltpu.SemaphoreType.DMA((len(cold_outs),)))

    def run(*refs):
        inside = list(refs[:n_in])
        results = list(refs[n_in + n_after : n_in + n_after + n_out])
        rest = list(refs[n_in + n_after + n_out :])
        buffers, rest = rest[: len(held)], rest[len(held) :]
        in_sem = rest.pop(0) if moved else None
        out_sem = rest.pop(0) if cold_outs else None
        copies, waited, sent = {}, set(), {}
        for place, i in enumerate(moved):
            copies[i] = pltpu.make_async_copy(refs[i], buffers[place], in_sem.at[place])
            copies[i].start()
            inside[i] = buffers[place]
        made = list(results)
        for place, o in enumerate(cold_outs):
            made[o] = buffers[len(moved) + place]

        def need(*which):
            for k in which:
                for i in groups[k]:
                    copies[i].wait()
                waited.add(k)

        def emit(*given):
            for ref in given:
                for place, o in enumerate(cold_outs):
                    if made[o] is ref and o not in sent:
                        sent[o] = pltpu.make_async_copy(made[o], results[o], out_sem.at[place])
                        sent[o].start()

        body(need, emit, *inside, *made, *rest)
        for k in range(len(groups)):
            if k not in waited:
                need(k)
        emit(*[made[o] for o in cold_outs])
        for o in cold_outs:
            sent[o].wait()

    spaces = [pltpu.VMEM] * n_in + [pl.ANY] * n_after
    for i in smem:
        spaces[i] = pltpu.SMEM
    for i in moved:
        spaces[i] = pl.ANY
    return pl.pallas_call(
        run,
        name=name,
        out_shape=list(outs),
        in_specs=[pl.BlockSpec(memory_space=s) for s in spaces],
        out_specs=[
            pl.BlockSpec(memory_space=pl.ANY if o in cold_outs else pltpu.SMEM if o in smem_outs else pltpu.VMEM)
            for o in range(n_out)
        ],
        scratch_shapes=held + sems + list(scratch),
        compiler_params=pltpu.CompilerParams(vmem_limit_bytes=VMEM_BYTES),
        cost_estimate=pl.CostEstimate(flops=1000, bytes_accessed=1000, transcendentals=0),
    )(*ins, *after)


def tie(values, *others):
    return lax.optimization_barrier((values, *others))[0]


def swap(values, axis, bit):
    return lax.ppermute(values, axis, [(i, i ^ bit) for i in range(lax.axis_size(axis))])


def send_far(far_part, got, *others):
    sent = tie((far_part + got[: far_part.shape[0]].astype(F32)).astype(LOW), *others)
    return swap(sent, "mp", 2), sent


def axis_bits(axis):
    return [1 << i for i in range(lax.axis_size(axis).bit_length() - 1)]


def halving_order(bits):
    order = [0]
    for bit in reversed(bits):
        order = order + [r ^ bit for r in order]
    return np.array(order, np.int32)


def scatter_sum(values, axis, bits):
    for bit in bits:
        half = values.shape[0] // 2
        got = swap(values[half:].astype(LOW), axis, bit)
        values = values[:half] + got.astype(F32)
    return values


def gather_back(values, axis, bits):
    for bit in reversed(bits):
        values = jnp.concatenate([values, swap(values, axis, bit)])
    return values


def sum_low(values, axis, bits):
    values = values.astype(LOW)
    for bit in bits:
        values = (values.astype(F32) + swap(values, axis, bit).astype(F32)).astype(LOW)
    return values


def sum_exact(values, axis, bits):
    for bit in bits:
        values = values + swap(values, axis, bit)
    return values


def tile_active(bounds, block, tile):
    return (bounds[2, tile] <= bounds[1, block]) & (bounds[3, tile] >= bounds[0, block])


def attend_block(block, queries, keys, value_ts, q_ids, k_ids, bounds, mixed, row, out_row, logs, scratch):
    scores, peak, total, acc = scratch
    count = queries.shape[0] // 2
    heads = queries.shape[1] // HEAD
    query_rows = queries[row : row + count, :]
    ids = q_ids[:, block * count : (block + 1) * count]
    peak[...] = jnp.full(peak.shape, masked_score, F32)
    total[...] = jnp.zeros(total.shape, F32)
    acc[...] = jnp.zeros(acc.shape, F32)
    for tile in range(4):
        inner = (tile % 2) * count

        @pl.when(tile_active(bounds, block, tile))
        def _(tile=tile, inner=inner):
            allowed = k_ids[tile * count : (tile + 1) * count, :] == ids
            for h in range(heads):
                cols = slice(h * HEAD, (h + 1) * HEAD)
                part = dot_last(keys[tile // 2][inner : inner + count, cols], query_rows[:, cols])
                part = jnp.where(allowed, part, masked_score)
                scores[h, tile] = part
                peak[h : h + 1, :] = jnp.maximum(
                    peak[h : h + 1, :], jnp.max(part, axis=0, keepdims=True)
                )

    for tile in range(4):
        inner = (tile % 2) * count

        @pl.when(tile_active(bounds, block, tile))
        def _(tile=tile, inner=inner):
            for h in range(heads):
                weights = jnp.exp2((scores[h, tile] - peak[h : h + 1, :]) * exp2_scale)
                total[h : h + 1, :] += jnp.sum(weights, axis=0, keepdims=True)
                acc[h] += dot(
                    value_ts[tile // 2][h * HEAD : (h + 1) * HEAD, inner : inner + count],
                    weights.astype(LOW),
                )

    for h in range(heads):
        sums = total[h : h + 1, :]
        mixed[out_row : out_row + count, h * HEAD : (h + 1) * HEAD] = (acc[h] / sums).T.astype(LOW)
        logs[h : h + 1, out_row : out_row + count] = peak[h : h + 1, :] * exp2_scale + jnp.log2(sums)


def attend_scratch(count, heads):
    return [
        pltpu.VMEM((heads, 4, count, count), F32),
        pltpu.VMEM((8, count), F32),
        pltpu.VMEM((8, count), F32),
        pltpu.VMEM((heads, HEAD, count), F32),
    ]


def project_pair(blocks, weights, norm=None):
    count, width = blocks[0].shape[0], weights[0].shape[1]
    dim = blocks[0].shape[1]
    outs = [shape((2 * count, width), LOW) for w in weights] + [shape((width, 2 * count), LOW)] * 2
    ins = list(blocks) + list(weights)
    if norm is not None:
        outs.append(shape((2 * count, dim), LOW))
        ins += list(norm[:2])
    n_weights = len(weights)

    def body(need, emit, *refs):
        rows, ws = refs[:2], refs[2 : 2 + n_weights]
        res = refs[len(ins) :]
        if norm is not None:
            norm_into(rows, refs[2 + n_weights], refs[3 + n_weights], norm[2], res[-1])
            rows = [res[-1].at[:count], res[-1].at[count:]]
        need(0)
        project_into(rows, ws, res)

    return local_kernel(
        body, "project_pair", ins, outs, cold=[range(2, 2 + n_weights)], cold_outs=range(len(outs))
    )


def norm_into(blocks, gain, offset, index, out):
    count = blocks[0].shape[0]
    at = slice(index, index + 1)
    for b in range(2):
        rows = layer_norm(blocks[b][...].astype(F32), gain[at, :], offset[at, :])
        out[b * count : (b + 1) * count, :] = rows.astype(LOW)


def project_into(blocks, weights, res):
    count = blocks[0].shape[0]
    for i, weight in enumerate(weights):
        for b in range(2):
            part = dot(blocks[b][...], weight[...])
            res[i][b * count : (b + 1) * count, :] = part.astype(LOW)
            if i < 2:
                res[len(weights) + i][:, b * count : (b + 1) * count] = part.T.astype(LOW)


def attend_first(far, across, weights, queries_far, near_set, out_weight, ids, norm=None):
    count, dim = far.shape
    width = out_weight.shape[1]
    heads = width // HEAD
    with_query = len(weights) == 3
    q_ids, k_ids, bounds = ids
    n_weights = len(weights)
    first = [far, across, *weights, *(norm[:2] if norm else ())]
    second = [near_set[0], near_set[2], near_set[3], out_weight, q_ids, k_ids]
    if not with_query:
        second.append(queries_far)
    n_first, n_all = len(first), len(first) + len(second)
    ins = first + second + [bounds]
    pair = shape((2 * count, width), LOW)
    turned = shape((width, 2 * count), LOW)
    outs = [pair] * n_weights + [turned, turned]
    if norm is not None:
        outs.append(shape((2 * count, dim), LOW))
    n_project = len(outs)
    outs += [pair, shape((8, 2 * count)), shape((2 * count, dim), LOW)]

    def body(need, emit, *refs):
        res, scratch = refs[len(ins) : len(ins) + len(outs)], refs[len(ins) + len(outs) :]
        rows, ws = refs[:2], refs[2 : 2 + n_weights]
        near_keys, near_values, near_queries, wo, qi, ki = refs[n_first : n_first + 6]
        bnd = refs[n_all]
        if norm is not None:
            norm_into(rows, refs[2 + n_weights], refs[3 + n_weights], norm[2], res[n_project - 1])
            rows = [res[n_project - 1].at[:count], res[n_project - 1].at[count:]]
        need(0)
        project_into(rows, ws, res)
        emit(*res[:n_project])
        need(1)
        far_queries = res[2] if with_query else refs[n_first + 6]
        mixed, logs, hop = res[n_project:]
        for place, (block, source) in enumerate(((3, far_queries), (1, near_queries))):
            attend_block(
                block, source, (near_keys, res[0]), (near_values, res[n_weights + 1]),
                qi, ki, bnd, mixed, (block % 2) * count, place * count, logs, scratch,
            )
            rows_of_mixed = mixed[place * count : (place + 1) * count, :]
            hop[place * count : (place + 1) * count, :] = dot_last(rows_of_mixed, wo[...]).astype(LOW)

    return local_kernel(
        body, "attend_first", ins, outs, attend_scratch(count, heads), smem=(n_all,),
        cold=[range(2, 2 + n_weights), range(n_first, n_all)], cold_outs=range(n_project + 2),
    )


def attend_one(block, queries, near_set, far_set, out_weight, ids, after):
    width = out_weight.shape[1]
    heads = width // HEAD
    count = queries.shape[0] // 2
    dim = out_weight.shape[0]
    q_ids, k_ids, bounds = ids
    ins = [queries, near_set[0], far_set[0], near_set[1], far_set[1], out_weight, q_ids, k_ids, bounds]
    outs = [shape((count, width), LOW), shape((8, count)), shape((count, dim))]

    def body(need, emit, q, k0, k1, v0, v1, wo, qi, ki, bnd, mixed, logs, part, *scratch):
        need(0)
        attend_block(block, q, (k0, k1), (v0, v1), qi, ki, bnd, mixed, 0, 0, logs, scratch)
        part[...] = dot_last(mixed[...], wo[...])

    return local_kernel(
        body, "attend_one", ins, outs, attend_scratch(count, heads), smem=(8,),
        cold=[range(8)], cold_outs=(0, 1), after=after,
    )


def back_block(block, row, grads, queries, logs, keys, key_ts, values, q_ids, k_ids, bounds,
               query_grads, key_acc, value_acc, scratch):
    probs, grad_probs, inner_sum, acc = scratch
    count = queries.shape[0] // 2
    heads = queries.shape[1] // HEAD
    query_rows = queries[row : row + count, :]
    ids = q_ids[:, block * count : (block + 1) * count]
    inner_sum[...] = jnp.zeros(inner_sum.shape, F32)
    acc[...] = jnp.zeros(acc.shape, F32)
    for tile in range(4):
        inner = (tile % 2) * count

        @pl.when(tile_active(bounds, block, tile))
        def _(tile=tile, inner=inner):
            allowed = k_ids[tile * count : (tile + 1) * count, :] == ids
            for h in range(heads):
                cols = slice(h * HEAD, (h + 1) * HEAD)
                part = dot_last(keys[tile // 2][inner : inner + count, cols], query_rows[:, cols])
                exact = jnp.where(
                    allowed,
                    jnp.exp2(part * exp2_scale - logs[0][h : h + 1, logs[1] : logs[1] + count]),
                    0.0,
                )
                pulled = dot_last(values[tile // 2][inner : inner + count, cols], grads[:, cols])
                probs[h, tile] = exact
                grad_probs[h, tile] = pulled
                inner_sum[h : h + 1, :] += jnp.sum(exact * pulled, axis=0, keepdims=True)
                value_acc[tile * count : (tile + 1) * count, cols] += dot(
                    exact.astype(LOW), grads[:, cols]
                )

    for tile in range(4):
        inner = (tile % 2) * count

        @pl.when(tile_active(bounds, block, tile))
        def _(tile=tile, inner=inner):
            for h in range(heads):
                cols = slice(h * HEAD, (h + 1) * HEAD)
                score_grads = (
                    probs[h, tile] * (grad_probs[h, tile] - inner_sum[h : h + 1, :])
                ).astype(LOW)
                key_acc[tile * count : (tile + 1) * count, cols] += dot(
                    score_grads, query_rows[:, cols]
                )
                acc[h] += dot(key_ts[tile // 2][cols, inner : inner + count], score_grads)

    for h in range(heads):
        query_grads[row : row + count, h * HEAD : (h + 1) * HEAD] = (
            (acc[h] * score_scale).T.astype(LOW)
        )


def back_scratch(count, heads):
    return [
        pltpu.VMEM((heads, 4, count, count), F32),
        pltpu.VMEM((heads, 4, count, count), F32),
        pltpu.VMEM((8, count), F32),
        pltpu.VMEM((heads, HEAD, count), F32),
    ]


def back_near(grads, out_weight, queries, logs, kept, ids):
    count = queries.shape[0] // 2
    width = queries.shape[1]
    q_ids, k_ids, bounds = ids
    ins = [*grads, out_weight, queries, *logs, *kept, q_ids, k_ids, bounds]
    outs = [shape((2 * count, width), LOW), shape((4 * count, width)), shape((4 * count, width))]

    def body(need, emit, g0, g1, wo, q, lg, lo, k0, k1, t0, t1, v0, v1, qi, ki, bnd, dq, dk, dv, *scratch):
        need(0)
        dk[...] = jnp.zeros(dk.shape, F32)
        dv[...] = jnp.zeros(dv.shape, F32)
        for b, g in enumerate((g0, g1)):
            mixed_grads = dot(g[...], wo[...]).astype(LOW)
            logs_at = (lg, count) if b else (lo, 0)
            back_block(b, b * count, mixed_grads, q, logs_at, (k0, k1), (t0, t1), (v0, v1), qi, ki, bnd,
                       dq, dk, dv, scratch)

    return local_kernel(body, "back_near", ins, outs, back_scratch(count, width // HEAD), smem=(14,),
        cold=[range(2, 14)], cold_outs=(0,),
    )


def back_far(grads, out_weight, queries, logs, kept, ids, sums, weights, after=()):
    count = queries.shape[0] // 2
    width = queries.shape[1]
    dim = out_weight.shape[0]
    q_ids, k_ids, bounds = ids
    ins = [*grads, out_weight, queries, *logs, *kept, q_ids, k_ids, bounds, *sums, *weights]
    whole = shape((4 * count, width), LOW)
    outs = [shape((2 * count, width), LOW), whole, whole, shape((count, dim)), shape((count, dim), LOW)]

    def body(need, emit, *refs):
        g0, g1, wo, q, lg, lo, k0, k1, t0, t1, v0, v1, qi, ki, bnd, dk_in, dv_in = refs[:17]
        ws = refs[17 : 17 + len(weights)]
        dq, dk, dv, far_out, across_out, key_acc, value_acc, *scratch = refs[17 + len(weights) :]
        need(0)
        key_acc[...] = dk_in[...]
        value_acc[...] = dv_in[...]
        for b, g in enumerate((g0, g1)):
            mixed_grads = dot(g[...], wo[...]).astype(LOW)
            logs_at = (lg, 0) if b else (lo, 0)
            back_block(2 + b, b * count, mixed_grads, q, logs_at, (k0, k1), (t0, t1), (v0, v1), qi, ki, bnd,
                       dq, key_acc, value_acc, scratch)
        dk[...] = (key_acc[...] * score_scale).astype(LOW)
        dv[...] = value_acc[...].astype(LOW)
        need(1)
        for b in (1, 0):
            rows = slice((2 + b) * count, (3 + b) * count)
            part = dot_last(dk[rows, :], ws[0][...]) + dot_last(dv[rows, :], ws[1][...])
            if len(ws) == 3:
                part = part + dot_last(dq[b * count : (b + 1) * count, :], ws[2][...])
            if b:
                across_out[...] = part.astype(LOW)
            else:
                far_out[...] = part

    scratch = [pltpu.VMEM((4 * count, width), F32)] * 2 + back_scratch(count, width // HEAD)
    return local_kernel(
        body, "back_far", ins, outs, scratch, smem=(14,),
        cold=[range(2, 14), range(17, 17 + len(weights))], after=after,
    )


def pull_near(pairs, after):
    dim = pairs[0][1].shape[0]
    count = pairs[0][2]
    ins = [p[0] for p in pairs] + [p[1] for p in pairs]
    outs = [shape((count, dim)), shape((count, dim), LOW)]

    def body(need, emit, *refs):
        n = len(pairs)
        need(0)
        own_out, near_out = refs[2 * n :]
        for b in range(2):
            part = None
            for i in range(n):
                term = dot_last(refs[i][b * count : (b + 1) * count, :], refs[n + i][...])
                part = term if part is None else part + term
            if b:
                near_out[...] = part.astype(LOW)
            else:
                own_out[...] = part

    return local_kernel(
        body, "pull_near", ins, outs, cold=[range(len(pairs), 2 * len(pairs))], after=after
    )


def mlp_pair(rows, grads, up_proj, down_proj, after=()):
    count, dim = rows[0].shape
    units = up_proj.shape[1]
    step = 256
    outs = [
        shape((2 * count, units), LOW), shape((2 * count, units), LOW),
        shape((count, dim)), shape((count, dim), LOW),
    ]

    def body(need, emit, x0, x1, g0, g1, up, down, active, grad_hidden, first_out, second_out):
        need(0)
        for b, (x, g) in enumerate(((x0, g0), (x1, g1))):
            for at in range(0, units, step):
                hidden = dot(x[...], up[:, at : at + step])
                pulled = dot(g[...], down[:, at : at + step])
                square = hidden * hidden
                bent = jnp.tanh(gelu_coeff * (hidden + gelu_cubic * hidden * square))
                half = 0.5 * (1.0 + bent)
                slope = half + 0.5 * hidden * (1.0 - bent * bent) * (
                    gelu_coeff * (1.0 + 3.0 * gelu_cubic * square)
                )
                active[b * count : (b + 1) * count, at : at + step] = (hidden * half).astype(LOW)
                grad_hidden[b * count : (b + 1) * count, at : at + step] = (pulled * slope).astype(LOW)
        emit(active, grad_hidden)
        for b in (1, 0):
            part = dot_last(grad_hidden[b * count : (b + 1) * count, :], up[...])
            if b:
                second_out[...] = part.astype(LOW)
            else:
                first_out[...] = part

    return local_kernel(
        body, "mlp_pair", [*rows, *grads, up_proj, down_proj], outs, cold=[range(2, 6)], cold_outs=(0, 1),
        after=after,
    )


def pull_four(near_rows, far_rows, weight, after):
    count, dim = near_rows.shape[0] // 2, weight.shape[0]
    outs = [shape((count, dim)), shape((count, dim)), shape((2 * count, dim), LOW)]

    def body(need, emit, x, y, w, own_out, far_out, hop):
        need(0)
        own_out[...] = dot_last(x[:count, :], w[...])
        far_out[...] = dot_last(y[:count, :], w[...])
        hop[:count, :] = dot_last(y[count:, :], w[...]).astype(LOW)
        hop[count:, :] = dot_last(x[count:, :], w[...]).astype(LOW)

    return local_kernel(
        body, "pull_four", [near_rows, far_rows, weight], outs, cold=[range(3)], cold_outs=(0, 1, 2), after=after
    )


def norm_rows(terms, gain, offset, index):
    kept = terms[0]

    def body(need, emit, k, p, n, f, g, o, after, normed):
        total = p[...] + n[n.shape[0] - p.shape[0] :, :].astype(F32) + f[...].astype(F32)
        need(0)
        total = total + k[...]
        after[...] = total
        emit(after)
        normed[...] = layer_norm(total, g[index : index + 1, :], o[index : index + 1, :]).astype(LOW)

    return local_kernel(
        body, "norm_rows", [*terms, gain, offset], [shape(kept.shape), shape(kept.shape, LOW)],
        cold=[[0]], cold_outs=(0,),
    )


def norm_rows_back(values, gain, index, terms, grads, after=()):
    added = grads is not None

    def body(need, emit, v, g, p, n, f, *refs):
        total = p[...] + n[...].astype(F32) + f[...].astype(F32)
        need(0)
        back, gain_sum, offset_sum = layer_norm_back(v[...].astype(F32), g[index : index + 1, :], total)
        if added:
            back = back + refs[0][...].astype(F32)
            out, out_low, sums = refs[1:]
            out_low[...] = back.astype(LOW)
            sums[0:1, :] = gain_sum
            sums[1:2, :] = offset_sum
        else:
            out = refs[0]
        out[...] = back

    ins = [values, gain, *terms]
    outs = [shape(values.shape)]
    if added:
        ins.append(grads)
        outs += [shape(values.shape, LOW), shape((2, values.shape[1]))]
    return local_kernel(
        body, "norm_back", ins, outs, cold=[[0, 5] if added else [0]], cold_outs=(0,), after=after
    )


def dp_orders():
    bits = axis_bits("dp")
    return [bits, bits[1:2] + bits[:1] + bits[2:]]


def outer_sums(sets, after):
    n_dp = lax.axis_size("dp")
    place = lax.axis_index("dp")
    ins, plans, places, outs = [], [], [], []
    seen = {}

    def take(array):
        if id(array) not in seen:
            seen[id(array)] = len(ins)
            ins.append(array)
        return seen[id(array)]

    for groups, bits in zip(sets, dp_orders()):
        plan = []
        for blocks, parts in groups:
            terms = []
            if len(parts) == 3:
                count = blocks[0].shape[0]
                terms = [
                    (take(blocks[0]), take(parts[0]), 0, count),
                    (take(blocks[1][1]), take(parts[1]), 0, count),
                    (take(blocks[1][0]), take(parts[1]), count, count),
                    (take(blocks[2]), take(parts[2]), 0, count),
                ]
            else:
                per = len(blocks) // len(parts)
                for b, block in enumerate(blocks):
                    count = block.shape[0]
                    terms.append((take(block), take(parts[b // per]), (b % per) * count, count))
            plan.append((terms, parts[0].shape[1]))
        plans.append(plan)
        dim = groups[0][0][0].shape[1]
        chunk = dim // n_dp
        aligned = chunk % 128 == 0
        steps = dim // 128
        width = sum(p[1] for p in plan)
        if aligned:
            repeat = chunk // 128
            spots = (jnp.asarray(halving_order(bits)) ^ place)[:, None] * repeat
            spots = (spots + jnp.arange(repeat, dtype=jnp.int32)[None, :]).reshape(steps)
        else:
            spots = jnp.arange(steps, dtype=jnp.int32)
        places.append(spots.astype(jnp.int32))
        outs += [shape((dim // 2, width)), shape((dim // 2, width), LOW)]
    ins.append(jnp.stack(places))

    def body(need, emit, *refs):
        need(0)
        spots = refs[len(ins) - 1]
        results = refs[len(ins) :]

        def one(order, index, target, base):
            at = pl.multiple_of(spots[order, base + index] * 128, 128)
            column = 0
            for terms, right_width in plans[order]:
                total = None
                for left, right, row, count in terms:
                    term = dot_first(refs[left][:, pl.ds(at, 128)], refs[right][row : row + count, :])
                    total = term if total is None else total + term
                target[pl.ds(pl.multiple_of(index * 128, 128), 128), column : column + right_width] = (
                    total.astype(target.dtype)
                )
                column += right_width

        for half in (1, 0):
            for order in range(len(plans)):
                @pl.loop(0, steps // 2)
                def _(index, order=order, half=half):
                    one(order, index, results[2 * order + half], half * (steps // 2))

    results = local_kernel(
        body, "outer_sums", ins, outs, smem=(len(ins) - 1,), cold=[range(len(ins) - 1)],
        cold_outs=range(len(outs)), after=after,
    )
    pairs = []
    for order, bits in enumerate(dp_orders()[: len(plans)]):
        keep, sent = results[2 * order : 2 * order + 2]
        if not aligned:
            whole = jnp.concatenate([keep, sent.astype(F32)]).reshape(n_dp, chunk, keep.shape[1])
            whole = whole[jnp.asarray(halving_order(bits)) ^ place].reshape(dim, keep.shape[1])
            keep, sent = whole[: dim // 2], whole[dim // 2 :].astype(LOW)
        pairs.append((keep, sent))
    return pairs


def outer_whole(groups, after):
    ins = [a for blocks, parts in groups for a in (*blocks, *parts)]
    dim = groups[0][0][0].shape[1]
    width = groups[0][1][0].shape[1]
    step = 256

    def body(need, emit, *refs):
        out = refs[len(ins)]
        for k in range(len(groups)):
            need(k)
            lefts, rights = refs[6 * k : 6 * k + 4], refs[6 * k + 4 : 6 * k + 6]
            count = lefts[0].shape[0]

            @pl.loop(0, dim // step)
            def _(index, k=k, lefts=lefts, rights=rights, count=count):
                at = pl.multiple_of(index * step, step)
                total = None
                for b in range(4):
                    right = rights[b // 2][(b % 2) * count : (b % 2 + 1) * count, :]
                    term = dot_first(lefts[b][:, pl.ds(at, step)], right)
                    total = term if total is None else total + term
                out[pl.ds(at, step), k * width : (k + 1) * width] = total.astype(LOW)

    return local_kernel(
        body, "outer_whole", ins, [shape((dim, width * len(groups)), LOW)],
        cold=[range(6 * k, 6 * k + 6) for k in range(len(groups))], cold_outs=(0,), after=after,
    )[0]


def fold(pairs, step, after=(), widths=None):
    orders = dp_orders()
    ins, outs = [], []
    last = step == len(orders[0]) - 1
    for order, (keep, sent) in enumerate(pairs):
        ins += [keep, swap(sent, "dp", orders[order][step])]
        rows, width = keep.shape
        if last:
            outs += [shape((rows, w)) for w in widths[order]]
        else:
            outs += [shape((rows // 2, width)), shape((rows // 2, width), LOW)]

    def body(need, emit, *refs):
        results = list(refs[len(ins) :])
        for order in range(len(pairs)):
            keep, got = refs[2 * order], refs[2 * order + 1]
            if last:
                column = 0
                for w in widths[order]:
                    cols = slice(column, column + w)
                    results.pop(0)[...] = keep[:, cols] + got[:, cols].astype(F32)
                    column += w
            else:
                half = keep.shape[0] // 2
                results.pop(0)[...] = keep[:half, :] + got[:half, :].astype(F32)
                results.pop(0)[...] = (keep[half:, :] + got[half:, :].astype(F32)).astype(LOW)

    results = local_kernel(body, "fold", ins, outs, after=after)
    if last:
        return results
    return [(results[2 * i], results[2 * i + 1]) for i in range(len(pairs))]


def rows_of(source, row_start, row_count):
    return lax.dynamic_slice_in_dim(source, row_start, row_count, 0)


def turn_row(row):
    columns = []
    for at in range(0, row.shape[1], 128):
        columns.append(jnp.broadcast_to(row[:, at : at + 128], (128, 128)).T[:, 0:1])
    return jnp.concatenate(columns, axis=0)


def prepare(latent_row, input_row, member, table, gain, offset, query_weight, images):
    total = latent_row.shape[1]
    count = total // 4
    slots, dim = table.shape
    width = query_weight.shape[1]
    whole = jnp.int32
    outs = [
        shape((1, total), whole), shape((total, 1), whole), shape((total, 1), whole),
        shape((4, 4), whole), shape((4, 4), whole),
        shape((total, slots), LOW), shape((slots, dim), LOW),
        shape((2 * count, width), LOW), shape((2 * count, width), LOW), shape((count, dim)),
    ]

    def body(need, emit, lat, inp, lat_s, inp_s, who, tb, g, o, wq,
             lat_out, lat_col, inp_col, cross_ends, self_ends, pick, normed, near_q, far_q, start):
        order = [who[0, 0] ^ k for k in range(4)]
        for k in range(4):
            first = order[k] * count
            last = first + count - 1
            cross_ends[0, k] = lat_s[0, first]
            cross_ends[1, k] = lat_s[0, last]
            cross_ends[2, k] = inp_s[0, first]
            cross_ends[3, k] = inp_s[0, last]
            for r in range(2):
                self_ends[2 * r, k] = lat_s[0, first]
                self_ends[2 * r + 1, k] = lat_s[0, last]
        starts = [pl.multiple_of(at * count, count) for at in order]
        lat_rel = jnp.concatenate([lat[:, pl.ds(at, count)] for at in starts], axis=1)
        inp_rel = jnp.concatenate([inp[:, pl.ds(at, count)] for at in starts], axis=1)
        lane = lax.broadcasted_iota(whole, (1, count), 1)
        place = jnp.concatenate([lane + at for at in starts], axis=1)
        lat_all = lat[...]
        for image in range(images):
            before = jnp.sum((lat_all < image).astype(F32), axis=1, keepdims=True).astype(whole)
            place = place - jnp.where(lat_rel == image, before, 0)
        lat_out[...] = lat_rel
        lat_col[...] = turn_row(lat_rel)
        inp_col[...] = turn_row(inp_rel)
        slot = turn_row(place)
        slot_lane = lax.broadcasted_iota(whole, (total, slots), 1)
        pick[...] = jnp.where(slot == slot_lane, 1.0, 0.0).astype(LOW)
        normed[...] = layer_norm(tb[...].astype(F32), g[0:1, :], o[0:1, :]).astype(LOW)
        start[...] = dot(pick[:count, :], tb[...])
        need(0)
        queries = dot(normed[...], wq[...]).astype(LOW)
        near_q[...] = dot(pick[: 2 * count, :], queries).astype(LOW)
        far_q[...] = dot(pick[2 * count :, :], queries).astype(LOW)

    return local_kernel(
        body, "prepare",
        [latent_row, input_row, latent_row, input_row, member, table, gain, offset, query_weight],
        outs, smem=(2, 3, 4), smem_outs=(3, 4), cold=[[8]],
    )


def slot_stack(pick, query_pairs, raw_blocks, parts, grads, sums, member, after):
    count, dim = raw_blocks[0].shape
    slots, width = pick.shape[1], query_pairs[0].shape[1]
    cut = dim // (2 * width)
    ins = [pick, *query_pairs, *raw_blocks, *parts, *grads, *sums, member]

    def body(need, emit, pk, q0, q1, x0, x1, x2, x3, p0, p1, p2, p3, r0, r1, r2, r3, s0, s1, who, out):
        need(0)
        total = dot_first(pk[: 2 * count, :], q0[...]) + dot_first(pk[2 * count :, :], q1[...])
        out[:slots, :width] = total.astype(LOW)
        at = pl.multiple_of(who[0, 0] * width, width)
        total = None
        for b, r in enumerate((r0, r1, r2, r3)):
            term = dot_first(pk[b * count : (b + 1) * count, :], r[:, pl.ds(at, width)])
            total = term if total is None else total + term
        out[:slots, width:] = total.astype(LOW)
        gain_sum = offset_sum = None
        for x, p in ((x0, p0), (x1, p1), (x2, p2), (x3, p3)):
            values = x[...].astype(F32)
            centred = values - jnp.mean(values, axis=-1, keepdims=True)
            spread = jnp.mean(centred * centred, axis=-1, keepdims=True)
            back = p[...].astype(F32)
            gains = jnp.sum(back * (centred * lax.rsqrt(spread + norm_eps)), axis=0, keepdims=True)
            offsets = jnp.sum(back, axis=0, keepdims=True)
            gain_sum = gains if gain_sum is None else gain_sum + gains
            offset_sum = offsets if offset_sum is None else offset_sum + offsets
        rows = [gain_sum, offset_sum, s0[0:1, :], s0[1:2, :], s1[0:1, :], s1[1:2, :]]
        rows += [jnp.zeros((1, dim), F32)] * 2
        whole = jnp.concatenate(rows, axis=0)
        for q in range(cut):
            out[slots + 8 * q : slots + 8 * (q + 1), :] = (
                whole[:, 2 * q * width : 2 * (q + 1) * width].astype(LOW)
            )

    return local_kernel(
        body, "slot_stack", ins, [shape((slots + 8 * cut, 2 * width), LOW)],
        smem=(len(ins) - 1,), cold=[range(7)], after=after,
    )[0]


def table_end(stacks, weights, gain, table, member):
    slots, dim = table.shape
    width = stacks[0].shape[1] // 2
    cut = dim // (2 * width)
    ins = [*stacks, *weights, gain, table, member]

    def body(need, emit, *refs):
        st, ws = refs[:4], refs[4:8]
        g, tb, who = refs[8:11]
        table_out, gain_out, offset_out, last_out, residual, grads, weight = refs[11:]
        need(0)
        for k in range(4):
            at = pl.multiple_of((who[0, 0] ^ k) * width, width)
            grads[:, pl.ds(at, width)] = st[k][:slots, :width]
            residual[:, pl.ds(at, width)] = st[k][:slots, width:]
            weight[:, pl.ds(at, width)] = ws[k][...]
        total = dot_last(grads[...], weight[...])
        back, gain_sum, offset_sum = layer_norm_back(tb[...].astype(F32), g[0:1, :], total)
        table_out[...] = residual[...].astype(F32) + back
        small = [st[k][slots:, :].astype(F32) for k in range(4)]
        small = (small[0] + small[1]) + (small[2] + small[3])
        small = jnp.concatenate([small[8 * q : 8 * (q + 1), :] for q in range(cut)], axis=1)
        gain_out[0:1, :] = gain_sum
        offset_out[0:1, :] = offset_sum
        for k in range(3):
            gain_out[k + 1 : k + 2, :] = small[2 * k : 2 * k + 1, :]
            target = last_out if k == 2 else offset_out
            at = 0 if k == 2 else k + 1
            target[at : at + 1, :] = small[2 * k + 1 : 2 * k + 2, :]

    outs = [shape((slots, dim)), shape((4, dim)), shape((3, dim)), shape((1, dim))]
    return local_kernel(
        body, "table_end", ins, outs,
        [pltpu.VMEM((slots, dim), LOW), pltpu.VMEM((slots, dim), LOW), pltpu.VMEM((dim, dim), LOW)],
        smem=(10,), cold=[range(4, 8)],
    )


def body(
    block_input,
    latent_table,
    latent_segments,
    input_segments,
    ln_gain,
    ln_bias,
    cross_query,
    cross_key,
    cross_value,
    cross_out,
    self_query,
    self_key,
    self_value,
    self_out,
    up_proj,
    down_proj,
    out_grad,
):
    count, dim = block_input.shape
    member = lax.axis_index("mp")
    n_mp, n_dp = lax.axis_size("mp"), lax.axis_size("dp")
    slots = latent_table.shape[0]
    mp_bits, dp_bits = axis_bits("mp"), axis_bits("dp")
    dp_steps = len(dp_bits)

    far_raw = swap(block_input, "mp", 2)
    near_raw = swap(block_input, "mp", 1)
    near_out = swap(out_grad, "mp", 1)

    who = member.astype(jnp.int32).reshape(1, 1)
    (latent_rel, latent_col, input_col, cross_ends, self_ends, table_pick, normed_table, queries_near,
     queries_far, start_rows) = prepare(
        latent_segments, input_segments, who, latent_table, ln_gain, ln_bias, cross_query, images
    )
    cross_ids = (latent_rel, input_col, cross_ends)
    self_ids = (latent_rel, latent_col, self_ends)

    half = count // 2
    input_norm = (ln_gain, ln_bias, 1)
    keys_near, values_near, key_ts_near, value_ts_near, normed_near = project_pair(
        (block_input, near_raw), (cross_key, cross_value), input_norm
    )
    far_raw = tie(far_raw, keys_near)
    across_raw = swap(far_raw, "mp", 1)
    far_out_1 = swap(tie(out_grad[:half], far_raw), "mp", 2)
    (keys_far, values_far, key_ts_far, value_ts_far, normed_far, mixed_two, logs_two, hop) = attend_first(
        far_raw, across_raw, (cross_key, cross_value), queries_far,
        (keys_near, key_ts_near, value_ts_near, queries_near), cross_out, cross_ids, input_norm,
    )
    got = swap(tie(hop, far_out_1), "mp", 1)
    key_values = ((keys_near, value_ts_near), (keys_far, value_ts_far))
    mixed_far, logs_far, part_far = attend_one(2, queries_far, *key_values, cross_out, cross_ids, ())
    got_far, sent = send_far(part_far, got)
    mixed_own, logs_own, part_own = attend_one(0, queries_near, *key_values, cross_out, cross_ids, (sent,))
    cross_kept = (keys_near, keys_far, key_ts_near, key_ts_far, values_near, values_far)
    cross_queries_set = (queries_near, queries_far)
    cross_logs = ((logs_two, logs_own), (logs_two, logs_far))
    cross_mixed = (mixed_own, mixed_two, mixed_far)
    after_cross, normed_self = norm_rows((start_rows, part_own, got, got_far), ln_gain, ln_bias, 2)

    self_weights = (self_key, self_value, self_query)
    far_self = swap(normed_self, "mp", 2)
    near_self = swap(normed_self, "mp", 1)
    keys_near, values_near, queries_near, key_ts_near, value_ts_near = project_pair(
        (normed_self, near_self), self_weights
    )
    far_self = tie(far_self, keys_near)
    across_self = swap(far_self, "mp", 1)
    far_out_2 = swap(tie(out_grad[half:], far_self), "mp", 2)
    (keys_far, values_far, queries_far, key_ts_far, value_ts_far, mixed_two, logs_two, hop) = attend_first(
        far_self, across_self, self_weights, None,
        (keys_near, key_ts_near, value_ts_near, queries_near), self_out, self_ids,
    )
    got = swap(tie(hop, far_out_2), "mp", 1)
    key_values = ((keys_near, value_ts_near), (keys_far, value_ts_far))
    mixed_far, logs_far, part_far = attend_one(2, queries_far, *key_values, self_out, self_ids, ())
    got_far, sent = send_far(part_far, got)
    mixed_own, logs_own, part_own = attend_one(0, queries_near, *key_values, self_out, self_ids, (sent,))
    far_out = tie(jnp.concatenate([far_out_1, far_out_2]), part_own)
    across_out = swap(far_out, "mp", 1)
    self_kept = (keys_near, keys_far, key_ts_near, key_ts_far, values_near, values_far)
    self_queries_set = (queries_near, queries_far)
    self_logs = ((logs_two, logs_own), (logs_two, logs_far))
    self_mixed = (mixed_own, mixed_two, mixed_far)
    after_self, normed_mlp = norm_rows((after_cross, part_own, got, got_far), ln_gain, ln_bias, 3)

    far_mlp = swap(normed_mlp, "mp", 2)
    near_mlp = swap(normed_mlp, "mp", 1)
    active_near, hidden_near, part_own, part_near = mlp_pair(
        (normed_mlp, near_mlp), (out_grad, near_out), up_proj, down_proj, (across_out,)
    )
    far_mlp = tie(far_mlp, part_near)
    across_mlp = swap(far_mlp, "mp", 1)
    query_rows = cross_query.shape[0] // 2
    far_query_1 = swap(tie(cross_query[:query_rows], far_mlp), "mp", 2)
    active_far, hidden_far, part_far, part_across = mlp_pair(
        (far_mlp, across_mlp), (far_out, across_out), up_proj, down_proj
    )
    got = swap(tie(part_across, far_query_1), "mp", 1)
    got_far, sent = send_far(part_far, got)
    mlp_grads = outer_whole(
        [
            ((normed_mlp, near_mlp, far_mlp, across_mlp), (hidden_near, hidden_far)),
            ((out_grad, near_out, far_out, across_out), (active_near, active_far)),
        ],
        (sent,),
    )
    mlp_sum = lax.psum_scatter(tie(mlp_grads, got_far), "dp", scatter_dimension=0, tiled=True)
    grad_self, dy_own, mlp_sums = norm_rows_back(
        after_self, ln_gain, 3, (part_own, swap(part_near, "mp", 1), got_far), out_grad,
        (mlp_grads,),
    )

    far_dy = swap(dy_own, "mp", 2)
    near_dy = swap(dy_own, "mp", 1)

    query_near, key_sum, value_sum = back_near(
        (dy_own, near_dy), self_out, self_queries_set[0], self_logs[0], self_kept, self_ids
    )
    far_dy = tie(far_dy, key_sum)
    across_dy = swap(far_dy, "mp", 1)
    far_query_2 = swap(tie(cross_query[query_rows:], far_dy), "mp", 2)
    query_far, key_grads, value_grads, part_far, part_across = back_far(
        (far_dy, across_dy), self_out, self_queries_set[1], self_logs[1], self_kept, self_ids,
        (key_sum, value_sum), self_weights,
    )
    got = swap(tie(part_across, far_query_2), "mp", 1)
    got_far, sent = send_far(part_far, got)
    part_own, part_near = pull_near(
        [(key_grads, self_key, count), (value_grads, self_value, count), (query_near, self_query, count)],
        (sent,),
    )
    normed_blocks = (normed_self, near_self, far_self, across_self)
    self_pairs = outer_sums(
        [
            [
                (normed_blocks, (query_near, query_far)), (normed_blocks, (key_grads,)),
                (normed_blocks, (value_grads,)), ((dy_own, (near_dy, across_dy), far_dy), self_mixed),
            ],
        ],
        (part_near,),
    )
    grad_cross, dy_cross, self_sums = norm_rows_back(
        after_cross, ln_gain, 2, (part_own, swap(part_near, "mp", 1), got_far), grad_self,
        (self_pairs[0][1],),
    )

    far_dyc = swap(dy_cross, "mp", 2)
    near_dyc = swap(dy_cross, "mp", 1)
    query_near, key_sum, value_sum = back_near(
        (dy_cross, near_dyc), cross_out, cross_queries_set[0], cross_logs[0], cross_kept, cross_ids
    )
    part_own_out, part_far_out, hop_out = pull_four(active_near, active_far, down_proj, (key_sum,))
    far_dyc = tie(far_dyc, part_own_out)
    across_dyc = swap(far_dyc, "mp", 1)
    query_far, key_grads, value_grads, part_far, part_across = back_far(
        (far_dyc, across_dyc), cross_out, cross_queries_set[1], cross_logs[1], cross_kept, cross_ids,
        (key_sum, value_sum), (cross_key, cross_value),
    )
    dyc_blocks = (dy_cross, near_dyc, far_dyc, across_dyc)
    part_own, part_near = pull_near([(key_grads, cross_key, count), (value_grads, cross_value, count)], ())
    got = swap(part_across, "mp", 1)
    got_far, sent = send_far(part_far, got, part_own)

    up_width = up_proj.shape[1]
    heads_width = cross_query.shape[1]
    stack = slot_stack(
        table_pick, (query_near, query_far), (block_input, near_raw, far_raw, across_raw),
        (part_own, part_near, part_far, part_across), dyc_blocks, (self_sums, mlp_sums), who, (sent,),
    )
    stack_got = swap(stack, "dp", dp_bits[0])
    input_blocks = (normed_near, normed_far)
    cross_pairs = outer_sums(
        [
            [(input_blocks, (key_grads,))],
            [
                (input_blocks, (value_grads,)),
                ((dy_cross, (near_dyc, across_dyc), far_dyc), cross_mixed),
            ],
        ],
        (stack,),
    )
    got_near = swap(tie(part_near, cross_pairs[0][1]), "mp", 1)
    cross_pairs = [(keep, tie(away, got_far)) for keep, away in cross_pairs]
    (grad_input,) = norm_rows_back(block_input, ln_gain, 1, (part_own, got_near, got_far), None)
    for step in range(dp_steps):
        last = step == dp_steps - 1
        stack = (stack.astype(F32) + stack_got.astype(F32)).astype(LOW)
        if step == 0:
            got_out = swap(tie(hop_out, grad_input), "mp", 1)
            sent_out = (part_far_out + got_out[:count].astype(F32)).astype(LOW)
            got_far_out = swap(sent_out, "mp", 2)
        if not last:
            stack_got = swap(tie(stack, grad_input), "dp", dp_bits[step + 1])
        self_pairs = fold(self_pairs, step, (), [[heads_width] * 4])
        cross_pairs = fold(cross_pairs, step, (), [[heads_width], [heads_width] * 2])
    mlp_sum = mlp_sum.astype(F32)
    block_output = (
        after_self + part_own_out + got_out[count:].astype(F32) + got_far_out.astype(F32)
    )
    far_query = jnp.concatenate([far_query_1, far_query_2])
    query_weights = (cross_query, swap(cross_query, "mp", 1), far_query, swap(far_query, "mp", 1))
    far_stack = swap(stack, "mp", 2)
    stacks = (stack, swap(stack, "mp", 1), far_stack, swap(far_stack, "mp", 1))
    table_grad, ln_gain_grad, ln_bias_grad, last_bias = table_end(
        stacks, query_weights, ln_gain, latent_table, who
    )
    chunk = dim // n_dp
    own_features = lax.dynamic_slice_in_dim(normed_table, lax.axis_index("dp") * chunk, chunk, 1)
    query_sum = dot_first(own_features, stack[:slots, :heads_width])

    return (
        block_output,
        grad_input,
        table_grad,
        ln_gain_grad,
        ln_bias_grad,
        last_bias[0],
        query_sum,
        *cross_pairs,
        *self_pairs,
        mlp_sum[:, :up_width],
        mlp_sum[:, up_width:],
    )


def solution(mesh):
    placed = (
        P(("dp", "mp"), None),
        P(),
        P("dp", None),
        P("dp", None),
        P(),
        P(),
        P(None, "mp"),
        P(None, "mp"),
        P(None, "mp"),
        P(None, "mp"),
        P(None, "mp"),
        P(None, "mp"),
        P(None, "mp"),
        P(None, "mp"),
        P(None, "mp"),
        P(None, "mp"),
        P(("dp", "mp"), None),
    )
    return jax.shard_map(
        body,
        mesh=mesh,
        in_specs=placed,
        out_specs=(
            P(("dp", "mp"), None),
            P(("dp", "mp"), None),
            P(),
            P(),
            P(),
            P(),
            P("dp", "mp"),
            P("dp", "mp"),
            P("dp", "mp"),
            P("dp", "mp"),
            P("dp", "mp"),
            P("dp", "mp"),
            P("dp", "mp"),
            P("dp", "mp"),
            P("dp", "mp"),
            P("dp", "mp"),
        ),
        check_vma=False,
    )
```

```python
import jax
import jax.numpy as jnp
import numpy as np
from jax import lax
from jax.experimental import pallas as pl
from jax.experimental.pallas import tpu as pltpu
from jax.sharding import PartitionSpec as P

HEAD = 128
images = 16
norm_eps = 1e-05
masked_score = -1e30
gelu_coeff = 0.7978845608028654
gelu_cubic = 0.044715
log2_e = 1.4426950408889634
score_scale = HEAD ** (-0.5)
exp2_scale = score_scale * log2_e
LOW = jnp.bfloat16
F32 = jnp.float32
VMEM_BYTES = 32 * 1024 * 1024
VMEM_LARGE = 56 * 1024 * 1024


def layer_norm(values, gain, offset):
    average = jnp.mean(values, axis=-1, keepdims=True)
    centred = values - average
    spread = jnp.mean(centred * centred, axis=-1, keepdims=True)
    return centred * lax.rsqrt(spread + norm_eps) * gain + offset


def layer_norm_back(values, gain, grad):
    average = jnp.mean(values, axis=-1, keepdims=True)
    centred = values - average
    spread = jnp.mean(centred * centred, axis=-1, keepdims=True)
    inverse = lax.rsqrt(spread + norm_eps)
    normal = centred * inverse
    scaled = grad * gain
    inner = jnp.mean(scaled * normal, axis=-1, keepdims=True)
    back = inverse * (scaled - jnp.mean(scaled, axis=-1, keepdims=True) - normal * inner)
    return (
        back,
        jnp.sum(grad * normal, axis=0, keepdims=True),
        jnp.sum(grad, axis=0, keepdims=True),
    )


def dot(left, right):
    return jnp.dot(left, right, preferred_element_type=F32)


def dot_last(left, right):
    return lax.dot_general(left, right, (((1,), (1,)), ((), ())), preferred_element_type=F32)


def dot_first(left, right):
    return lax.dot_general(left, right, (((0,), (0,)), ((), ())), preferred_element_type=F32)


def shape(dims, kind=F32):
    return jax.ShapeDtypeStruct(dims, kind)


def local_kernel(body, name, ins, outs, scratch=(), smem=(), cold=None, cold_outs=(), smem_outs=(), vmem=VMEM_BYTES, after=()):
    if after:
        ins = [tie(ins[0], *after), *ins[1:]]
    n_in, n_out = len(ins), len(outs)
    groups = [list(g) for g in (cold or [])]
    moved = [i for g in groups for i in g]
    held = [pltpu.VMEM(ins[i].shape, ins[i].dtype) for i in moved]
    held += [pltpu.VMEM(outs[o].shape, outs[o].dtype) for o in cold_outs]
    sems = []
    if moved:
        sems.append(pltpu.SemaphoreType.DMA((len(moved),)))
    if cold_outs:
        sems.append(pltpu.SemaphoreType.DMA((len(cold_outs),)))

    def run(*refs):
        inside = list(refs[:n_in])
        results = list(refs[n_in : n_in + n_out])
        rest = list(refs[n_in + n_out :])
        buffers, rest = rest[: len(held)], rest[len(held) :]
        in_sem = rest.pop(0) if moved else None
        out_sem = rest.pop(0) if cold_outs else None
        copies, waited, sent = {}, set(), {}
        for place, i in enumerate(moved):
            copies[i] = pltpu.make_async_copy(refs[i], buffers[place], in_sem.at[place])
            copies[i].start()
            inside[i] = buffers[place]
        made = list(results)
        for place, o in enumerate(cold_outs):
            made[o] = buffers[len(moved) + place]

        def need(*which):
            for k in which:
                for i in groups[k]:
                    copies[i].wait()
                waited.add(k)

        def emit(*given):
            for ref in given:
                for place, o in enumerate(cold_outs):
                    if made[o] is ref and o not in sent:
                        sent[o] = pltpu.make_async_copy(made[o], results[o], out_sem.at[place])
                        sent[o].start()

        body(need, emit, *inside, *made, *rest)
        for k in range(len(groups)):
            if k not in waited:
                need(k)
        emit(*[made[o] for o in cold_outs])
        for o in cold_outs:
            sent[o].wait()

    spaces = [pltpu.VMEM] * n_in
    for i in smem:
        spaces[i] = pltpu.SMEM
    for i in moved:
        spaces[i] = pl.ANY
    return pl.pallas_call(
        run,
        name=name,
        out_shape=list(outs),
        in_specs=[pl.BlockSpec(memory_space=s) for s in spaces],
        out_specs=[
            pl.BlockSpec(memory_space=pl.ANY if o in cold_outs else pltpu.SMEM if o in smem_outs else pltpu.VMEM)
            for o in range(n_out)
        ],
        scratch_shapes=held + sems + list(scratch),
        compiler_params=pltpu.CompilerParams(vmem_limit_bytes=vmem),
        cost_estimate=pl.CostEstimate(flops=1000, bytes_accessed=1000, transcendentals=0),
    )(*ins)


def wait(*arrays):
    return lax.optimization_barrier(arrays)


def tie(values, *others):
    return lax.optimization_barrier((values, *others))[0]


def swap(values, axis, bit):
    return lax.ppermute(values, axis, [(i, i ^ bit) for i in range(lax.axis_size(axis))])


def send_far(far_part, got, *others):
    sent = tie((far_part + got[: far_part.shape[0]].astype(F32)).astype(LOW), *others)
    return swap(sent, "mp", 2), sent


def axis_bits(axis):
    return [1 << i for i in range(lax.axis_size(axis).bit_length() - 1)]


def halving_order(bits):
    order = [0]
    for bit in reversed(bits):
        order = order + [r ^ bit for r in order]
    return np.array(order, np.int32)


def scatter_sum(values, axis, bits):
    for bit in bits:
        half = values.shape[0] // 2
        got = swap(values[half:].astype(LOW), axis, bit)
        values = values[:half] + got.astype(F32)
    return values


def gather_back(values, axis, bits):
    for bit in reversed(bits):
        values = jnp.concatenate([values, swap(values, axis, bit)])
    return values


def sum_low(values, axis, bits):
    values = values.astype(LOW)
    for bit in bits:
        values = (values.astype(F32) + swap(values, axis, bit).astype(F32)).astype(LOW)
    return values


def sum_exact(values, axis, bits):
    for bit in bits:
        values = values + swap(values, axis, bit)
    return values


def tile_active(bounds, block, tile):
    return (bounds[2, tile] <= bounds[1, block]) & (bounds[3, tile] >= bounds[0, block])


def attend_block(block, queries, keys, value_ts, q_ids, k_ids, bounds, mixed, row, out_row, logs, scratch):
    scores, peak, total, acc = scratch
    count = queries.shape[0] // 2
    heads = queries.shape[1] // HEAD
    query_rows = queries[row : row + count, :]
    ids = q_ids[:, block * count : (block + 1) * count]
    peak[...] = jnp.full(peak.shape, masked_score, F32)
    total[...] = jnp.zeros(total.shape, F32)
    acc[...] = jnp.zeros(acc.shape, F32)
    for tile in range(4):
        inner = (tile % 2) * count

        @pl.when(tile_active(bounds, block, tile))
        def _(tile=tile, inner=inner):
            allowed = k_ids[tile * count : (tile + 1) * count, :] == ids
            for h in range(heads):
                cols = slice(h * HEAD, (h + 1) * HEAD)
                part = dot_last(keys[tile // 2][inner : inner + count, cols], query_rows[:, cols])
                part = jnp.where(allowed, part, masked_score)
                scores[h, tile] = part
                peak[h : h + 1, :] = jnp.maximum(
                    peak[h : h + 1, :], jnp.max(part, axis=0, keepdims=True)
                )

    for tile in range(4):
        inner = (tile % 2) * count

        @pl.when(tile_active(bounds, block, tile))
        def _(tile=tile, inner=inner):
            for h in range(heads):
                weights = jnp.exp2((scores[h, tile] - peak[h : h + 1, :]) * exp2_scale)
                total[h : h + 1, :] += jnp.sum(weights, axis=0, keepdims=True)
                acc[h] += dot(
                    value_ts[tile // 2][h * HEAD : (h + 1) * HEAD, inner : inner + count],
                    weights.astype(LOW),
                )

    for h in range(heads):
        sums = total[h : h + 1, :]
        mixed[out_row : out_row + count, h * HEAD : (h + 1) * HEAD] = (acc[h] / sums).T.astype(LOW)
        logs[h : h + 1, out_row : out_row + count] = peak[h : h + 1, :] * exp2_scale + jnp.log2(sums)


def attend_scratch(count, heads):
    return [
        pltpu.VMEM((heads, 4, count, count), F32),
        pltpu.VMEM((8, count), F32),
        pltpu.VMEM((8, count), F32),
        pltpu.VMEM((heads, HEAD, count), F32),
    ]


def project_pair(blocks, weights, norm=None):
    count, width = blocks[0].shape[0], weights[0].shape[1]
    dim = blocks[0].shape[1]
    outs = [shape((2 * count, width), LOW) for w in weights] + [shape((width, 2 * count), LOW)] * 2
    ins = list(blocks) + list(weights)
    if norm is not None:
        outs.append(shape((2 * count, dim), LOW))
        ins += list(norm[:2])
    n_weights = len(weights)

    def body(need, emit, *refs):
        rows, ws = refs[:2], refs[2 : 2 + n_weights]
        res = refs[len(ins) :]
        if norm is not None:
            norm_into(rows, refs[2 + n_weights], refs[3 + n_weights], norm[2], res[-1])
            rows = [res[-1].at[:count], res[-1].at[count:]]
        need(0)
        project_into(rows, ws, res)

    return local_kernel(
        body, "project_pair", ins, outs, cold=[range(2, 2 + n_weights)], cold_outs=range(len(outs))
    )


def norm_into(blocks, gain, offset, index, out):
    count = blocks[0].shape[0]
    at = slice(index, index + 1)
    for b in range(2):
        rows = layer_norm(blocks[b][...].astype(F32), gain[at, :], offset[at, :])
        out[b * count : (b + 1) * count, :] = rows.astype(LOW)


def project_into(blocks, weights, res):
    count = blocks[0].shape[0]
    for i, weight in enumerate(weights):
        for b in range(2):
            part = dot(blocks[b][...], weight[...])
            res[i][b * count : (b + 1) * count, :] = part.astype(LOW)
            if i < 2:
                res[len(weights) + i][:, b * count : (b + 1) * count] = part.T.astype(LOW)


def attend_first(far, across, weights, queries_far, near_set, out_weight, ids, norm=None):
    count, dim = far.shape
    width = out_weight.shape[1]
    heads = width // HEAD
    with_query = len(weights) == 3
    q_ids, k_ids, bounds = ids
    n_weights = len(weights)
    first = [far, across, *weights, *(norm[:2] if norm else ())]
    second = [near_set[0], near_set[2], near_set[3], out_weight, q_ids, k_ids]
    if not with_query:
        second.append(queries_far)
    n_first, n_all = len(first), len(first) + len(second)
    ins = first + second + [bounds]
    pair = shape((2 * count, width), LOW)
    turned = shape((width, 2 * count), LOW)
    outs = [pair] * n_weights + [turned, turned]
    if norm is not None:
        outs.append(shape((2 * count, dim), LOW))
    n_project = len(outs)
    outs += [pair, shape((8, 2 * count)), shape((2 * count, dim), LOW)]

    def body(need, emit, *refs):
        res, scratch = refs[len(ins) : len(ins) + len(outs)], refs[len(ins) + len(outs) :]
        rows, ws = refs[:2], refs[2 : 2 + n_weights]
        near_keys, near_values, near_queries, wo, qi, ki = refs[n_first : n_first + 6]
        bnd = refs[n_all]
        if norm is not None:
            norm_into(rows, refs[2 + n_weights], refs[3 + n_weights], norm[2], res[n_project - 1])
            rows = [res[n_project - 1].at[:count], res[n_project - 1].at[count:]]
        need(0)
        project_into(rows, ws, res)
        emit(*res[:n_project])
        need(1)
        far_queries = res[2] if with_query else refs[n_first + 6]
        mixed, logs, hop = res[n_project:]
        for place, (block, source) in enumerate(((3, far_queries), (1, near_queries))):
            attend_block(
                block, source, (near_keys, res[0]), (near_values, res[n_weights + 1]),
                qi, ki, bnd, mixed, (block % 2) * count, place * count, logs, scratch,
            )
            rows_of_mixed = mixed[place * count : (place + 1) * count, :]
            hop[place * count : (place + 1) * count, :] = dot_last(rows_of_mixed, wo[...]).astype(LOW)

    return local_kernel(
        body, "attend_first", ins, outs, attend_scratch(count, heads), smem=(n_all,),
        cold=[range(2, 2 + n_weights), range(n_first, n_all)], cold_outs=range(n_project + 2),
    )


def attend_one(block, queries, near_set, far_set, out_weight, ids, after):
    width = out_weight.shape[1]
    heads = width // HEAD
    count = queries.shape[0] // 2
    dim = out_weight.shape[0]
    q_ids, k_ids, bounds = ids
    ins = [queries, near_set[0], far_set[0], near_set[1], far_set[1], out_weight, q_ids, k_ids, bounds]
    outs = [shape((count, width), LOW), shape((8, count)), shape((count, dim))]

    def body(need, emit, q, k0, k1, v0, v1, wo, qi, ki, bnd, mixed, logs, part, *scratch):
        need(0)
        attend_block(block, q, (k0, k1), (v0, v1), qi, ki, bnd, mixed, 0, 0, logs, scratch)
        part[...] = dot_last(mixed[...], wo[...])

    return local_kernel(
        body, "attend_one", ins, outs, attend_scratch(count, heads), smem=(8,),
        cold=[range(8)], cold_outs=(0, 1), after=after,
    )


def back_block(block, row, grads, queries, logs, keys, key_ts, values, q_ids, k_ids, bounds,
               query_grads, key_acc, value_acc, scratch):
    probs, grad_probs, inner_sum, acc = scratch
    count = queries.shape[0] // 2
    heads = queries.shape[1] // HEAD
    query_rows = queries[row : row + count, :]
    ids = q_ids[:, block * count : (block + 1) * count]
    inner_sum[...] = jnp.zeros(inner_sum.shape, F32)
    acc[...] = jnp.zeros(acc.shape, F32)
    for tile in range(4):
        inner = (tile % 2) * count

        @pl.when(tile_active(bounds, block, tile))
        def _(tile=tile, inner=inner):
            allowed = k_ids[tile * count : (tile + 1) * count, :] == ids
            for h in range(heads):
                cols = slice(h * HEAD, (h + 1) * HEAD)
                part = dot_last(keys[tile // 2][inner : inner + count, cols], query_rows[:, cols])
                exact = jnp.where(
                    allowed,
                    jnp.exp2(part * exp2_scale - logs[0][h : h + 1, logs[1] : logs[1] + count]),
                    0.0,
                )
                pulled = dot_last(values[tile // 2][inner : inner + count, cols], grads[:, cols])
                probs[h, tile] = exact
                grad_probs[h, tile] = pulled
                inner_sum[h : h + 1, :] += jnp.sum(exact * pulled, axis=0, keepdims=True)
                value_acc[tile * count : (tile + 1) * count, cols] += dot(
                    exact.astype(LOW), grads[:, cols]
                )

    for tile in range(4):
        inner = (tile % 2) * count

        @pl.when(tile_active(bounds, block, tile))
        def _(tile=tile, inner=inner):
            for h in range(heads):
                cols = slice(h * HEAD, (h + 1) * HEAD)
                score_grads = (
                    probs[h, tile] * (grad_probs[h, tile] - inner_sum[h : h + 1, :])
                ).astype(LOW)
                key_acc[tile * count : (tile + 1) * count, cols] += dot(
                    score_grads, query_rows[:, cols]
                )
                acc[h] += dot(key_ts[tile // 2][cols, inner : inner + count], score_grads)

    for h in range(heads):
        query_grads[row : row + count, h * HEAD : (h + 1) * HEAD] = (
            (acc[h] * score_scale).T.astype(LOW)
        )


def back_scratch(count, heads):
    return [
        pltpu.VMEM((heads, 4, count, count), F32),
        pltpu.VMEM((heads, 4, count, count), F32),
        pltpu.VMEM((8, count), F32),
        pltpu.VMEM((heads, HEAD, count), F32),
    ]


def back_near(grads, out_weight, queries, logs, kept, ids):
    count = queries.shape[0] // 2
    width = queries.shape[1]
    q_ids, k_ids, bounds = ids
    ins = [*grads, out_weight, queries, *logs, *kept, q_ids, k_ids, bounds]
    outs = [shape((2 * count, width), LOW), shape((4 * count, width)), shape((4 * count, width))]

    def body(need, emit, g0, g1, wo, q, lg, lo, k0, k1, t0, t1, v0, v1, qi, ki, bnd, dq, dk, dv, *scratch):
        need(0)
        dk[...] = jnp.zeros(dk.shape, F32)
        dv[...] = jnp.zeros(dv.shape, F32)
        for b, g in enumerate((g0, g1)):
            mixed_grads = dot(g[...], wo[...]).astype(LOW)
            logs_at = (lg, count) if b else (lo, 0)
            back_block(b, b * count, mixed_grads, q, logs_at, (k0, k1), (t0, t1), (v0, v1), qi, ki, bnd,
                       dq, dk, dv, scratch)

    return local_kernel(body, "back_near", ins, outs, back_scratch(count, width // HEAD), smem=(14,),
        cold=[range(2, 14)], cold_outs=(0,),
    )


def back_far(grads, out_weight, queries, logs, kept, ids, sums, weights, after=()):
    count = queries.shape[0] // 2
    width = queries.shape[1]
    dim = out_weight.shape[0]
    q_ids, k_ids, bounds = ids
    ins = [*grads, out_weight, queries, *logs, *kept, q_ids, k_ids, bounds, *sums, *weights]
    whole = shape((4 * count, width), LOW)
    outs = [shape((2 * count, width), LOW), whole, whole, shape((count, dim)), shape((count, dim), LOW)]

    def body(need, emit, *refs):
        g0, g1, wo, q, lg, lo, k0, k1, t0, t1, v0, v1, qi, ki, bnd, dk_in, dv_in = refs[:17]
        ws = refs[17 : 17 + len(weights)]
        dq, dk, dv, far_out, across_out, key_acc, value_acc, *scratch = refs[17 + len(weights) :]
        need(0)
        key_acc[...] = dk_in[...]
        value_acc[...] = dv_in[...]
        for b, g in enumerate((g0, g1)):
            mixed_grads = dot(g[...], wo[...]).astype(LOW)
            logs_at = (lg, 0) if b else (lo, 0)
            back_block(2 + b, b * count, mixed_grads, q, logs_at, (k0, k1), (t0, t1), (v0, v1), qi, ki, bnd,
                       dq, key_acc, value_acc, scratch)
        dk[...] = (key_acc[...] * score_scale).astype(LOW)
        dv[...] = value_acc[...].astype(LOW)
        need(1)
        for b in (1, 0):
            rows = slice((2 + b) * count, (3 + b) * count)
            part = dot_last(dk[rows, :], ws[0][...]) + dot_last(dv[rows, :], ws[1][...])
            if len(ws) == 3:
                part = part + dot_last(dq[b * count : (b + 1) * count, :], ws[2][...])
            if b:
                across_out[...] = part.astype(LOW)
            else:
                far_out[...] = part

    scratch = [pltpu.VMEM((4 * count, width), F32)] * 2 + back_scratch(count, width // HEAD)
    return local_kernel(
        body, "back_far", ins, outs, scratch, smem=(14,),
        cold=[range(2, 14), range(17, 17 + len(weights))], after=after,
    )


def pull_near(pairs, after):
    dim = pairs[0][1].shape[0]
    count = pairs[0][2]
    ins = [p[0] for p in pairs] + [p[1] for p in pairs]
    outs = [shape((count, dim)), shape((count, dim), LOW)]

    def body(need, emit, *refs):
        n = len(pairs)
        need(0)
        own_out, near_out = refs[2 * n :]
        for b in range(2):
            part = None
            for i in range(n):
                term = dot_last(refs[i][b * count : (b + 1) * count, :], refs[n + i][...])
                part = term if part is None else part + term
            if b:
                near_out[...] = part.astype(LOW)
            else:
                own_out[...] = part

    return local_kernel(
        body, "pull_near", ins, outs, cold=[range(len(pairs), 2 * len(pairs))], after=after
    )


def mlp_pair(rows, grads, up_proj, down_proj, after=()):
    count, dim = rows[0].shape
    units = up_proj.shape[1]
    step = 256
    outs = [
        shape((2 * count, units), LOW), shape((2 * count, units), LOW),
        shape((count, dim)), shape((count, dim), LOW),
    ]

    def body(need, emit, x0, x1, g0, g1, up, down, active, grad_hidden, first_out, second_out):
        need(0)
        for b, (x, g) in enumerate(((x0, g0), (x1, g1))):
            for at in range(0, units, step):
                hidden = dot(x[...], up[:, at : at + step])
                pulled = dot(g[...], down[:, at : at + step])
                square = hidden * hidden
                bent = jnp.tanh(gelu_coeff * (hidden + gelu_cubic * hidden * square))
                half = 0.5 * (1.0 + bent)
                slope = half + 0.5 * hidden * (1.0 - bent * bent) * (
                    gelu_coeff * (1.0 + 3.0 * gelu_cubic * square)
                )
                active[b * count : (b + 1) * count, at : at + step] = (hidden * half).astype(LOW)
                grad_hidden[b * count : (b + 1) * count, at : at + step] = (pulled * slope).astype(LOW)
        emit(active, grad_hidden)
        for b in (1, 0):
            part = dot_last(grad_hidden[b * count : (b + 1) * count, :], up[...])
            if b:
                second_out[...] = part.astype(LOW)
            else:
                first_out[...] = part

    return local_kernel(
        body, "mlp_pair", [*rows, *grads, up_proj, down_proj], outs, cold=[range(2, 6)], cold_outs=(0, 1),
        after=after,
    )


def pull_four(near_rows, far_rows, weight, after):
    count, dim = near_rows.shape[0] // 2, weight.shape[0]
    outs = [shape((count, dim)), shape((count, dim)), shape((2 * count, dim), LOW)]

    def body(need, emit, x, y, w, own_out, far_out, hop):
        need(0)
        own_out[...] = dot_last(x[:count, :], w[...])
        far_out[...] = dot_last(y[:count, :], w[...])
        hop[:count, :] = dot_last(y[count:, :], w[...]).astype(LOW)
        hop[count:, :] = dot_last(x[count:, :], w[...]).astype(LOW)

    return local_kernel(
        body, "pull_four", [near_rows, far_rows, weight], outs, cold=[range(3)], cold_outs=(0, 1, 2), after=after
    )


def norm_rows(terms, gain, offset, index):
    kept = terms[0]

    def body(need, emit, k, p, n, f, g, o, after, normed):
        total = p[...] + n[n.shape[0] - p.shape[0] :, :].astype(F32) + f[...].astype(F32)
        need(0)
        total = total + k[...]
        after[...] = total
        emit(after)
        normed[...] = layer_norm(total, g[index : index + 1, :], o[index : index + 1, :]).astype(LOW)

    return local_kernel(
        body, "norm_rows", [*terms, gain, offset], [shape(kept.shape), shape(kept.shape, LOW)],
        cold=[[0]], cold_outs=(0,),
    )


def norm_rows_back(values, gain, index, terms, grads, after=()):
    added = grads is not None

    def body(need, emit, v, g, p, n, f, *refs):
        total = p[...] + n[...].astype(F32) + f[...].astype(F32)
        need(0)
        back, gain_sum, offset_sum = layer_norm_back(v[...].astype(F32), g[index : index + 1, :], total)
        if added:
            back = back + refs[0][...].astype(F32)
            out, out_low, sums = refs[1:]
            out_low[...] = back.astype(LOW)
            sums[0:1, :] = gain_sum
            sums[1:2, :] = offset_sum
        else:
            out = refs[0]
        out[...] = back

    ins = [values, gain, *terms]
    outs = [shape(values.shape)]
    if added:
        ins.append(grads)
        outs += [shape(values.shape, LOW), shape((2, values.shape[1]))]
    return local_kernel(
        body, "norm_back", ins, outs, cold=[[0, 5] if added else [0]], cold_outs=(0,), after=after
    )


def dp_orders():
    bits = axis_bits("dp")
    return [bits, bits[1:2] + bits[:1] + bits[2:]]


def outer_sums(sets, after, parts_sent=1):
    n_dp = lax.axis_size("dp")
    place = lax.axis_index("dp")
    ins, plans, places, outs = [], [], [], []
    seen = {}

    def take(array):
        if id(array) not in seen:
            seen[id(array)] = len(ins)
            ins.append(array)
        return seen[id(array)]

    for groups, bits in zip(sets, dp_orders()):
        plan = []
        for blocks, parts in groups:
            terms = []
            if len(parts) == 3:
                count = blocks[0].shape[0]
                terms = [
                    (take(blocks[0]), take(parts[0]), 0, count),
                    (take(blocks[1][1]), take(parts[1]), 0, count),
                    (take(blocks[1][0]), take(parts[1]), count, count),
                    (take(blocks[2]), take(parts[2]), 0, count),
                ]
            else:
                per = len(blocks) // len(parts)
                for b, block in enumerate(blocks):
                    count = block.shape[0]
                    terms.append((take(block), take(parts[b // per]), (b % per) * count, count))
            plan.append((terms, parts[0].shape[1]))
        plans.append(plan)
        dim = groups[0][0][0].shape[1]
        chunk = dim // n_dp
        aligned = chunk % 128 == 0
        steps = dim // 128
        width = sum(p[1] for p in plan)
        if aligned:
            repeat = chunk // 128
            spots = (jnp.asarray(halving_order(bits)) ^ place)[:, None] * repeat
            spots = (spots + jnp.arange(repeat, dtype=jnp.int32)[None, :]).reshape(steps)
        else:
            spots = jnp.arange(steps, dtype=jnp.int32)
        places.append(spots.astype(jnp.int32))
        outs += [shape((dim // 2, width))] + [shape((dim // 2 // parts_sent, width), LOW)] * parts_sent
    ins.append(jnp.stack(places))

    def body(need, emit, *refs):
        need(0)
        spots = refs[len(ins) - 1]
        results = refs[len(ins) :]

        def one(order, index, target, base):
            at = pl.multiple_of(spots[order, base + index] * 128, 128)
            column = 0
            for terms, right_width in plans[order]:
                total = None
                for left, right, row, count in terms:
                    term = dot_first(refs[left][:, pl.ds(at, 128)], refs[right][row : row + count, :])
                    total = term if total is None else total + term
                target[pl.ds(pl.multiple_of(index * 128, 128), 128), column : column + right_width] = (
                    total.astype(target.dtype)
                )
                column += right_width

        per = 1 + parts_sent
        half = steps // 2
        for piece in [*range(1, per), 0]:
            for order in range(len(plans)):
                run = half if piece == 0 else half // parts_sent
                base = 0 if piece == 0 else half + (piece - 1) * run

                @pl.loop(0, run)
                def _(index, target=results[per * order + piece], order=order, base=base):
                    one(order, index, target, base)

    results = local_kernel(
        body, "outer_sums", ins, outs, smem=(len(ins) - 1,), cold=[range(len(ins) - 1)],
        cold_outs=range(len(outs)), vmem=VMEM_LARGE, after=after,
    )
    pairs = []
    for order, bits in enumerate(dp_orders()[: len(plans)]):
        keep, *sent = results[(1 + parts_sent) * order : (1 + parts_sent) * (order + 1)]
        if not aligned:
            whole = jnp.concatenate([keep, *[part.astype(F32) for part in sent]])
            whole = whole.reshape(n_dp, chunk, keep.shape[1])
            whole = whole[jnp.asarray(halving_order(bits)) ^ place].reshape(dim, keep.shape[1])
            keep, whole = whole[: dim // 2], whole[dim // 2 :].astype(LOW)
            sent = [part for part in whole.reshape(parts_sent, dim // 2 // parts_sent, keep.shape[1])]
        pairs.append((keep, *sent))
    return pairs


def outer_whole(groups, after):
    ins = [a for blocks, parts in groups for a in (*blocks, *parts)]
    dim = groups[0][0][0].shape[1]
    width = groups[0][1][0].shape[1]
    step = 256

    def body(need, emit, *refs):
        out = refs[len(ins)]
        for k in range(len(groups)):
            need(k)
            lefts, rights = refs[6 * k : 6 * k + 4], refs[6 * k + 4 : 6 * k + 6]
            count = lefts[0].shape[0]

            @pl.loop(0, dim // step)
            def _(index, k=k, lefts=lefts, rights=rights, count=count):
                at = pl.multiple_of(index * step, step)
                total = None
                for b in range(4):
                    right = rights[b // 2][(b % 2) * count : (b % 2 + 1) * count, :]
                    term = dot_first(lefts[b][:, pl.ds(at, step)], right)
                    total = term if total is None else total + term
                out[pl.ds(at, step), k * width : (k + 1) * width] = total.astype(LOW)

    return local_kernel(
        body, "outer_whole", ins, [shape((dim, width * len(groups)), LOW)],
        cold=[range(6 * k, 6 * k + 6) for k in range(len(groups))], cold_outs=(0,), vmem=VMEM_LARGE, after=after,
    )[0]


def merge(pairs, last, widths, after=()):
    ins, outs, firsts = [], [], []
    for order, (keep, *came) in enumerate(pairs):
        firsts.append(len(ins))
        ins += [keep, *came]
        rows, width = keep.shape
        if last:
            outs += [shape((rows, w)) for w in widths[order]]
        else:
            outs += [shape((rows // 2, width)), shape((rows // 2, width), LOW)]

    def body(need, emit, *refs):
        results = list(refs[len(ins) :])
        for order in range(len(pairs)):
            keep, got = refs[firsts[order]], refs[firsts[order] + 1]
            if last:
                column = 0
                for w in widths[order]:
                    cols = slice(column, column + w)
                    results.pop(0)[...] = keep[:, cols] + got[:, cols].astype(F32)
                    column += w
            else:
                half = keep.shape[0] // 2
                later = got[half:, :] if len(pairs[order]) == 2 else refs[firsts[order] + 2][...]
                results.pop(0)[...] = keep[:half, :] + got[:half, :].astype(F32)
                results.pop(0)[...] = (keep[half:, :] + later.astype(F32)).astype(LOW)

    results = local_kernel(body, "merge", ins, outs, after=after)
    if last:
        return results
    return [(results[2 * i], results[2 * i + 1]) for i in range(len(pairs))]


def rows_of(source, row_start, row_count):
    return lax.dynamic_slice_in_dim(source, row_start, row_count, 0)


def turn_row(row):
    columns = []
    for at in range(0, row.shape[1], 128):
        columns.append(jnp.broadcast_to(row[:, at : at + 128], (128, 128)).T[:, 0:1])
    return jnp.concatenate(columns, axis=0)


def prepare(latent_row, input_row, member, table, gain, offset, query_weight, images):
    total = latent_row.shape[1]
    count = total // 4
    slots, dim = table.shape
    width = query_weight.shape[1]
    whole = jnp.int32
    outs = [
        shape((1, total), whole), shape((total, 1), whole), shape((total, 1), whole),
        shape((4, 4), whole), shape((4, 4), whole),
        shape((total, slots), LOW), shape((slots, dim), LOW),
        shape((2 * count, width), LOW), shape((2 * count, width), LOW), shape((count, dim)),
    ]

    def body(need, emit, lat, inp, lat_s, inp_s, who, tb, g, o, wq,
             lat_out, lat_col, inp_col, cross_ends, self_ends, pick, normed, near_q, far_q, start):
        order = [who[0, 0] ^ k for k in range(4)]
        for k in range(4):
            first = order[k] * count
            last = first + count - 1
            cross_ends[0, k] = lat_s[0, first]
            cross_ends[1, k] = lat_s[0, last]
            cross_ends[2, k] = inp_s[0, first]
            cross_ends[3, k] = inp_s[0, last]
            for r in range(2):
                self_ends[2 * r, k] = lat_s[0, first]
                self_ends[2 * r + 1, k] = lat_s[0, last]
        starts = [pl.multiple_of(at * count, count) for at in order]
        lat_rel = jnp.concatenate([lat[:, pl.ds(at, count)] for at in starts], axis=1)
        inp_rel = jnp.concatenate([inp[:, pl.ds(at, count)] for at in starts], axis=1)
        lane = lax.broadcasted_iota(whole, (1, count), 1)
        place = jnp.concatenate([lane + at for at in starts], axis=1)
        lat_all = lat[...]
        for image in range(images):
            before = jnp.sum((lat_all < image).astype(F32), axis=1, keepdims=True).astype(whole)
            place = place - jnp.where(lat_rel == image, before, 0)
        lat_out[...] = lat_rel
        lat_col[...] = turn_row(lat_rel)
        inp_col[...] = turn_row(inp_rel)
        slot = turn_row(place)
        slot_lane = lax.broadcasted_iota(whole, (total, slots), 1)
        pick[...] = jnp.where(slot == slot_lane, 1.0, 0.0).astype(LOW)
        normed[...] = layer_norm(tb[...].astype(F32), g[0:1, :], o[0:1, :]).astype(LOW)
        start[...] = dot(pick[:count, :], tb[...])
        need(0)
        queries = dot(normed[...], wq[...]).astype(LOW)
        near_q[...] = dot(pick[: 2 * count, :], queries).astype(LOW)
        far_q[...] = dot(pick[2 * count :, :], queries).astype(LOW)

    return local_kernel(
        body, "prepare",
        [latent_row, input_row, latent_row, input_row, member, table, gain, offset, query_weight],
        outs, smem=(2, 3, 4), smem_outs=(3, 4), cold=[[8]],
    )


def slot_stack(pick, query_pairs, raw_blocks, parts, grads, sums, member, after):
    count, dim = raw_blocks[0].shape
    slots, width = pick.shape[1], query_pairs[0].shape[1]
    cut = dim // (2 * width)
    ins = [pick, *query_pairs, *raw_blocks, *parts, *grads, *sums, member]

    def body(need, emit, pk, q0, q1, x0, x1, x2, x3, p0, p1, p2, p3, r0, r1, r2, r3, s0, s1, who, out):
        need(0)
        total = dot_first(pk[: 2 * count, :], q0[...]) + dot_first(pk[2 * count :, :], q1[...])
        out[:slots, :width] = total.astype(LOW)
        at = pl.multiple_of(who[0, 0] * width, width)
        total = None
        for b, r in enumerate((r0, r1, r2, r3)):
            term = dot_first(pk[b * count : (b + 1) * count, :], r[:, pl.ds(at, width)])
            total = term if total is None else total + term
        out[:slots, width:] = total.astype(LOW)
        gain_sum = offset_sum = None
        for x, p in ((x0, p0), (x1, p1), (x2, p2), (x3, p3)):
            values = x[...].astype(F32)
            centred = values - jnp.mean(values, axis=-1, keepdims=True)
            spread = jnp.mean(centred * centred, axis=-1, keepdims=True)
            back = p[...].astype(F32)
            gains = jnp.sum(back * (centred * lax.rsqrt(spread + norm_eps)), axis=0, keepdims=True)
            offsets = jnp.sum(back, axis=0, keepdims=True)
            gain_sum = gains if gain_sum is None else gain_sum + gains
            offset_sum = offsets if offset_sum is None else offset_sum + offsets
        rows = [gain_sum, offset_sum, s0[0:1, :], s0[1:2, :], s1[0:1, :], s1[1:2, :]]
        rows += [jnp.zeros((1, dim), F32)] * 2
        whole = jnp.concatenate(rows, axis=0)
        for q in range(cut):
            out[slots + 8 * q : slots + 8 * (q + 1), :] = (
                whole[:, 2 * q * width : 2 * (q + 1) * width].astype(LOW)
            )

    return local_kernel(
        body, "slot_stack", ins, [shape((slots + 8 * cut, 2 * width), LOW)],
        smem=(len(ins) - 1,), cold=[range(7)], after=after,
    )[0]


def table_end(stacks, weights, gain, table, member):
    slots, dim = table.shape
    width = stacks[0].shape[1] // 2
    cut = dim // (2 * width)
    ins = [*stacks, *weights, gain, table, member]

    def body(need, emit, *refs):
        st, ws = refs[:4], refs[4:8]
        g, tb, who = refs[8:11]
        table_out, gain_out, offset_out, last_out, residual, grads, weight = refs[11:]
        need(0)
        for k in range(4):
            at = pl.multiple_of((who[0, 0] ^ k) * width, width)
            grads[:, pl.ds(at, width)] = st[k][:slots, :width]
            residual[:, pl.ds(at, width)] = st[k][:slots, width:]
            weight[:, pl.ds(at, width)] = ws[k][...]
        total = dot_last(grads[...], weight[...])
        back, gain_sum, offset_sum = layer_norm_back(tb[...].astype(F32), g[0:1, :], total)
        table_out[...] = residual[...].astype(F32) + back
        small = [st[k][slots:, :].astype(F32) for k in range(4)]
        small = (small[0] + small[1]) + (small[2] + small[3])
        small = jnp.concatenate([small[8 * q : 8 * (q + 1), :] for q in range(cut)], axis=1)
        gain_out[0:1, :] = gain_sum
        offset_out[0:1, :] = offset_sum
        for k in range(3):
            gain_out[k + 1 : k + 2, :] = small[2 * k : 2 * k + 1, :]
            target = last_out if k == 2 else offset_out
            at = 0 if k == 2 else k + 1
            target[at : at + 1, :] = small[2 * k + 1 : 2 * k + 2, :]

    outs = [shape((slots, dim)), shape((4, dim)), shape((3, dim)), shape((1, dim))]
    return local_kernel(
        body, "table_end", ins, outs,
        [pltpu.VMEM((slots, dim), LOW), pltpu.VMEM((slots, dim), LOW), pltpu.VMEM((dim, dim), LOW)],
        smem=(10,), cold=[range(4, 8)],
    )


def body(
    block_input,
    latent_table,
    latent_segments,
    input_segments,
    ln_gain,
    ln_bias,
    cross_query,
    cross_key,
    cross_value,
    cross_out,
    self_query,
    self_key,
    self_value,
    self_out,
    up_proj,
    down_proj,
    out_grad,
):
    count, dim = block_input.shape
    member = lax.axis_index("mp")
    n_mp, n_dp = lax.axis_size("mp"), lax.axis_size("dp")
    slots = latent_table.shape[0]
    mp_bits, dp_bits = axis_bits("mp"), axis_bits("dp")
    dp_steps = len(dp_bits)

    far_raw = swap(block_input, "mp", 2)
    near_raw = swap(block_input, "mp", 1)
    near_out = swap(out_grad, "mp", 1)
    half = count // 2
    near_raw, out_1, out_2 = lax.optimization_barrier((near_raw, out_grad[:half], out_grad[half:]))

    who = member.astype(jnp.int32).reshape(1, 1)
    (latent_rel, latent_col, input_col, cross_ends, self_ends, table_pick, normed_table, queries_near,
     queries_far, start_rows) = prepare(
        latent_segments, input_segments, who, latent_table, ln_gain, ln_bias, cross_query, images
    )
    cross_ids = (latent_rel, input_col, cross_ends)
    self_ids = (latent_rel, latent_col, self_ends)

    input_norm = (ln_gain, ln_bias, 1)
    keys_near, values_near, key_ts_near, value_ts_near, normed_near = project_pair(
        (block_input, near_raw), (cross_key, cross_value), input_norm
    )
    far_raw = tie(far_raw, keys_near, queries_far)
    across_raw = swap(far_raw, "mp", 1)
    far_out_1 = swap(tie(out_1, far_raw), "mp", 2)
    (keys_far, values_far, key_ts_far, value_ts_far, normed_far, mixed_two, logs_two, hop) = attend_first(
        far_raw, across_raw, (cross_key, cross_value), queries_far,
        (keys_near, key_ts_near, value_ts_near, queries_near), cross_out, cross_ids, input_norm,
    )
    got = swap(tie(hop, far_out_1), "mp", 1)
    key_values = ((keys_near, value_ts_near), (keys_far, value_ts_far))
    mixed_far, logs_far, part_far = attend_one(2, queries_far, *key_values, cross_out, cross_ids, ())
    got_far, sent = send_far(part_far, got)
    mixed_own, logs_own, part_own = attend_one(0, queries_near, *key_values, cross_out, cross_ids, (sent,))
    cross_kept = (keys_near, keys_far, key_ts_near, key_ts_far, values_near, values_far)
    cross_queries_set = (queries_near, queries_far)
    cross_logs = ((logs_two, logs_own), (logs_two, logs_far))
    cross_mixed = (mixed_own, mixed_two, mixed_far)
    after_cross, normed_self = norm_rows((start_rows, part_own, got, got_far), ln_gain, ln_bias, 2)

    self_weights = (self_key, self_value, self_query)
    far_self = swap(normed_self, "mp", 2)
    near_self = swap(normed_self, "mp", 1)
    keys_near, values_near, queries_near, key_ts_near, value_ts_near = project_pair(
        (normed_self, near_self), self_weights
    )
    far_self = tie(far_self, keys_near)
    across_self = swap(far_self, "mp", 1)
    far_out_2 = swap(tie(out_2, far_self), "mp", 2)
    (keys_far, values_far, queries_far, key_ts_far, value_ts_far, mixed_two, logs_two, hop) = attend_first(
        far_self, across_self, self_weights, None,
        (keys_near, key_ts_near, value_ts_near, queries_near), self_out, self_ids,
    )
    got = swap(tie(hop, far_out_2), "mp", 1)
    key_values = ((keys_near, value_ts_near), (keys_far, value_ts_far))
    mixed_far, logs_far, part_far = attend_one(2, queries_far, *key_values, self_out, self_ids, ())
    got_far, sent = send_far(part_far, got)
    mixed_own, logs_own, part_own = attend_one(0, queries_near, *key_values, self_out, self_ids, (sent,))
    far_out = tie(jnp.concatenate([far_out_1, far_out_2]), part_own)
    across_out = swap(far_out, "mp", 1)
    self_kept = (keys_near, keys_far, key_ts_near, key_ts_far, values_near, values_far)
    self_queries_set = (queries_near, queries_far)
    self_logs = ((logs_two, logs_own), (logs_two, logs_far))
    self_mixed = (mixed_own, mixed_two, mixed_far)
    after_self, normed_mlp = norm_rows((after_cross, part_own, got, got_far), ln_gain, ln_bias, 3)

    far_mlp = swap(normed_mlp, "mp", 2)
    near_mlp = swap(normed_mlp, "mp", 1)
    active_near, hidden_near, part_own, part_near = mlp_pair(
        (normed_mlp, near_mlp), (out_grad, near_out), up_proj, down_proj, (across_out,)
    )
    far_mlp = tie(far_mlp, part_near)
    across_mlp = swap(far_mlp, "mp", 1)
    active_far, hidden_far, part_far, part_across = mlp_pair(
        (far_mlp, across_mlp), (far_out, across_out), up_proj, down_proj
    )
    got = swap(part_across, "mp", 1)
    got_far, sent = send_far(part_far, got)
    mlp_grads = outer_whole(
        [
            ((normed_mlp, near_mlp, far_mlp, across_mlp), (hidden_near, hidden_far)),
            ((out_grad, near_out, far_out, across_out), (active_near, active_far)),
        ],
        (sent,),
    )
    mlp_sum = lax.psum_scatter(tie(mlp_grads, got_far), "dp", scatter_dimension=0, tiled=True)
    grad_self, dy_own, mlp_sums = norm_rows_back(
        after_self, ln_gain, 3, (part_own, swap(part_near, "mp", 1), got_far), out_grad,
        (mlp_grads,),
    )

    far_dy = swap(dy_own, "mp", 2)
    near_dy = swap(dy_own, "mp", 1)

    query_near, key_sum, value_sum = back_near(
        (dy_own, near_dy), self_out, self_queries_set[0], self_logs[0], self_kept, self_ids
    )
    far_dy = tie(far_dy, key_sum)
    across_dy = swap(far_dy, "mp", 1)
    query_far, key_grads, value_grads, part_far, part_across = back_far(
        (far_dy, across_dy), self_out, self_queries_set[1], self_logs[1], self_kept, self_ids,
        (key_sum, value_sum), self_weights,
    )
    got = swap(part_across, "mp", 1)
    part_own, part_near = pull_near(
        [(key_grads, self_key, count), (value_grads, self_value, count), (query_near, self_query, count)], ()
    )
    got_far, sent = send_far(part_far, got, part_own)
    got_near = swap(part_near, "mp", 1)
    normed_blocks = (normed_self, near_self, far_self, across_self)
    self_pairs = outer_sums(
        [
            [
                (normed_blocks, (query_near, query_far)), (normed_blocks, (key_grads,)),
                (normed_blocks, (value_grads,)), ((dy_own, (near_dy, across_dy), far_dy), self_mixed),
            ],
        ],
        (sent,), 2,
    )
    grad_cross, dy_cross, self_sums = norm_rows_back(
        after_cross, ln_gain, 2, (part_own, got_near, got_far), grad_self,
        (self_pairs[0][1],),
    )

    far_dyc = swap(dy_cross, "mp", 2)
    near_dyc = swap(dy_cross, "mp", 1)
    query_near, key_sum, value_sum = back_near(
        (dy_cross, near_dyc), cross_out, cross_queries_set[0], cross_logs[0], cross_kept, cross_ids
    )
    part_own_out, part_far_out, hop_out = pull_four(active_near, active_far, down_proj, (key_sum,))
    self_half = swap(self_pairs[0][1], "dp", dp_bits[0])
    far_dyc = tie(far_dyc, part_own_out, self_half)
    across_dyc = swap(far_dyc, "mp", 1)
    query_far, key_grads, value_grads, part_far, part_across = back_far(
        (far_dyc, across_dyc), cross_out, cross_queries_set[1], cross_logs[1], cross_kept, cross_ids,
        (key_sum, value_sum), (cross_key, cross_value),
    )
    dyc_blocks = (dy_cross, near_dyc, far_dyc, across_dyc)
    part_own, part_near = pull_near([(key_grads, cross_key, count), (value_grads, cross_value, count)], ())
    got = swap(part_across, "mp", 1)
    got_near = swap(part_near, "mp", 1)
    got_far, sent = send_far(part_far, got, part_own)

    up_width = up_proj.shape[1]
    heads_width = cross_query.shape[1]
    stack = slot_stack(
        table_pick, (query_near, query_far), (block_input, near_raw, far_raw, across_raw),
        (part_own, part_near, part_far, part_across), dyc_blocks, (self_sums, mlp_sums), who,
        (sent,),
    )
    input_blocks = (normed_near, normed_far)
    cross_sets = [
        [
            (input_blocks, (key_grads,)),
            (input_blocks, (value_grads,)),
            ((dy_cross, (near_dyc, across_dyc), far_dyc), cross_mixed),
        ],
    ]
    self_keep, _, self_sent = self_pairs[0]

    def dp_swap(values, step):
        return swap(values, "dp", dp_bits[step])

    def joined(mine, came):
        return (mine.astype(F32) + came.astype(F32)).astype(LOW)

    def halved(keep, *came):
        return merge([(keep, *came)], False, None)[0]

    stack_got, self_got = dp_swap(stack, 0), dp_swap(self_sent, 0)
    ((cross_keep, cross_sent),) = outer_sums(cross_sets, (stack,))
    got_far, got_near, stack, stack_got, self_got, cross_sent, hop_out, query_sent = wait(
        got_far, got_near, stack, stack_got, self_got, cross_sent, hop_out, cross_query
    )
    stack = joined(stack, stack_got)

    stack_got, cross_got = dp_swap(stack, 1), dp_swap(cross_sent, 0)
    far_query, near_query = swap(query_sent, "mp", 2), swap(query_sent, "mp", 1)
    got_out = swap(hop_out, "mp", 1)
    self_keep, self_sent = halved(self_keep, self_half, self_got)
    (grad_input,) = norm_rows_back(block_input, ln_gain, 1, (part_own, got_near, got_far), None)
    stack, stack_got, got_out, grad_input, self_sent = wait(stack, stack_got, got_out, grad_input, self_sent)
    stack = joined(stack, stack_got)
    sent_out = (part_far_out + got_out[:count].astype(F32)).astype(LOW)

    stack_got, self_got = dp_swap(stack, 2), dp_swap(self_sent, 1)
    got_far_out = swap(sent_out, "mp", 2)
    mlp_parts = [mlp_sum[:, :up_width].astype(F32), mlp_sum[:, up_width:].astype(F32)]
    stack, stack_got, self_got, cross_got, mlp_parts = wait(stack, stack_got, self_got, cross_got, mlp_parts)
    stack = joined(stack, stack_got)

    for step in range(3, dp_steps):
        self_keep, self_sent = halved(self_keep, self_got)
        cross_keep, cross_sent = halved(cross_keep, cross_got)
        stack_got, cross_got, self_got = wait(
            dp_swap(stack, step), dp_swap(cross_sent, step - 2), dp_swap(self_sent, step - 1)
        )
        stack = joined(stack, stack_got)

    far_stack, near_stack = swap(stack, "mp", 2), swap(stack, "mp", 1)
    cross_keep, cross_sent = halved(cross_keep, cross_got)
    cross_got = dp_swap(cross_sent, dp_steps - 2)
    self_keep, self_sent = halved(self_keep, self_got)
    self_got = dp_swap(self_sent, dp_steps - 1)
    far_stack, cross_got, far_query, near_query = wait(far_stack, cross_got, far_query, near_query)

    across_stack = swap(far_stack, "mp", 1)
    across_query = swap(far_query, "mp", 1)
    cross_keep, cross_sent = halved(cross_keep, cross_got)
    cross_got = dp_swap(cross_sent, dp_steps - 1)
    self_keep, self_got, across_stack, cross_sent = wait(self_keep, self_got, across_stack, cross_sent)
    self_pair = merge([(self_keep, self_got)], True, [[heads_width] * 4])
    chunk = dim // n_dp
    own_features = lax.dynamic_slice_in_dim(normed_table, lax.axis_index("dp") * chunk, chunk, 1)
    query_sum = dot_first(own_features, stack[:slots, :heads_width])
    table_grad, ln_gain_grad, ln_bias_grad, last_bias = table_end(
        (stack, near_stack, far_stack, across_stack),
        (cross_query, near_query, far_query, across_query), ln_gain, latent_table, who,
    )
    block_output = (
        after_self + part_own_out + got_out[count:].astype(F32) + got_far_out.astype(F32)
    )
    cross_keep, table_grad, block_output, query_sum, self_pair = wait(
        cross_keep, table_grad, block_output, query_sum, self_pair
    )
    cross_pair = merge([(cross_keep, cross_got)], True, [[heads_width] * 3])

    return (
        block_output,
        grad_input,
        table_grad,
        ln_gain_grad,
        ln_bias_grad,
        last_bias[0],
        query_sum,
        *cross_pair,
        *self_pair,
        *mlp_parts,
    )


def solution(mesh):
    placed = (
        P(("dp", "mp"), None),
        P(),
        P("dp", None),
        P("dp", None),
        P(),
        P(),
        P(None, "mp"),
        P(None, "mp"),
        P(None, "mp"),
        P(None, "mp"),
        P(None, "mp"),
        P(None, "mp"),
        P(None, "mp"),
        P(None, "mp"),
        P(None, "mp"),
        P(None, "mp"),
        P(("dp", "mp"), None),
    )
    return jax.shard_map(
        body,
        mesh=mesh,
        in_specs=placed,
        out_specs=(
            P(("dp", "mp"), None),
            P(("dp", "mp"), None),
            P(),
            P(),
            P(),
            P(),
            P("dp", "mp"),
            P("dp", "mp"),
            P("dp", "mp"),
            P("dp", "mp"),
            P("dp", "mp"),
            P("dp", "mp"),
            P("dp", "mp"),
            P("dp", "mp"),
            P("dp", "mp"),
            P("dp", "mp"),
        ),
        check_vma=False,
    )
```

```python
import jax
import jax.numpy as jnp
import numpy as np
from jax import lax
from jax.experimental import pallas as pl
from jax.experimental.pallas import tpu as pltpu
from jax.sharding import PartitionSpec as P

HEAD = 128
images = 16
norm_eps = 1e-05
masked_score = -1e30
gelu_coeff = 0.7978845608028654
gelu_cubic = 0.044715
log2_e = 1.4426950408889634
score_scale = HEAD ** (-0.5)
exp2_scale = score_scale * log2_e
LOW = jnp.bfloat16
F32 = jnp.float32
VMEM_BYTES = 32 * 1024 * 1024
VMEM_LARGE = 56 * 1024 * 1024


def layer_norm(values, gain, offset):
    average = jnp.mean(values, axis=-1, keepdims=True)
    centred = values - average
    spread = jnp.mean(centred * centred, axis=-1, keepdims=True)
    return centred * lax.rsqrt(spread + norm_eps) * gain + offset


def layer_norm_back(values, gain, grad):
    average = jnp.mean(values, axis=-1, keepdims=True)
    centred = values - average
    spread = jnp.mean(centred * centred, axis=-1, keepdims=True)
    inverse = lax.rsqrt(spread + norm_eps)
    normal = centred * inverse
    scaled = grad * gain
    inner = jnp.mean(scaled * normal, axis=-1, keepdims=True)
    back = inverse * (scaled - jnp.mean(scaled, axis=-1, keepdims=True) - normal * inner)
    return (
        back,
        jnp.sum(grad * normal, axis=0, keepdims=True),
        jnp.sum(grad, axis=0, keepdims=True),
    )


def dot(left, right):
    return jnp.dot(left, right, preferred_element_type=F32)


def dot_last(left, right):
    return lax.dot_general(left, right, (((1,), (1,)), ((), ())), preferred_element_type=F32)


def dot_first(left, right):
    return lax.dot_general(left, right, (((0,), (0,)), ((), ())), preferred_element_type=F32)


def shape(dims, kind=F32):
    return jax.ShapeDtypeStruct(dims, kind)


def local_kernel(body, name, ins, outs, scratch=(), smem=(), cold=None, cold_outs=(), smem_outs=(), vmem=VMEM_BYTES, after=()):
    if after:
        ins = [tie(ins[0], *after), *ins[1:]]
    n_in, n_out = len(ins), len(outs)
    groups = [list(g) for g in (cold or [])]
    moved = [i for g in groups for i in g]
    held = [pltpu.VMEM(ins[i].shape, ins[i].dtype) for i in moved]
    held += [pltpu.VMEM(outs[o].shape, outs[o].dtype) for o in cold_outs]
    sems = []
    if moved:
        sems.append(pltpu.SemaphoreType.DMA((len(moved),)))
    if cold_outs:
        sems.append(pltpu.SemaphoreType.DMA((len(cold_outs),)))

    def run(*refs):
        inside = list(refs[:n_in])
        results = list(refs[n_in : n_in + n_out])
        rest = list(refs[n_in + n_out :])
        buffers, rest = rest[: len(held)], rest[len(held) :]
        in_sem = rest.pop(0) if moved else None
        out_sem = rest.pop(0) if cold_outs else None
        copies, waited, sent = {}, set(), {}
        for place, i in enumerate(moved):
            copies[i] = pltpu.make_async_copy(refs[i], buffers[place], in_sem.at[place])
            copies[i].start()
            inside[i] = buffers[place]
        made = list(results)
        for place, o in enumerate(cold_outs):
            made[o] = buffers[len(moved) + place]

        def need(*which):
            for k in which:
                for i in groups[k]:
                    copies[i].wait()
                waited.add(k)

        def emit(*given):
            for ref in given:
                for place, o in enumerate(cold_outs):
                    if made[o] is ref and o not in sent:
                        sent[o] = pltpu.make_async_copy(made[o], results[o], out_sem.at[place])
                        sent[o].start()

        body(need, emit, *inside, *made, *rest)
        for k in range(len(groups)):
            if k not in waited:
                need(k)
        emit(*[made[o] for o in cold_outs])
        for o in cold_outs:
            sent[o].wait()

    spaces = [pltpu.VMEM] * n_in
    for i in smem:
        spaces[i] = pltpu.SMEM
    for i in moved:
        spaces[i] = pl.ANY
    return pl.pallas_call(
        run,
        name=name,
        out_shape=list(outs),
        in_specs=[pl.BlockSpec(memory_space=s) for s in spaces],
        out_specs=[
            pl.BlockSpec(memory_space=pl.ANY if o in cold_outs else pltpu.SMEM if o in smem_outs else pltpu.VMEM)
            for o in range(n_out)
        ],
        scratch_shapes=held + sems + list(scratch),
        compiler_params=pltpu.CompilerParams(vmem_limit_bytes=vmem),
        cost_estimate=pl.CostEstimate(flops=1000, bytes_accessed=1000, transcendentals=0),
    )(*ins)


def wait(*arrays):
    return lax.optimization_barrier(arrays)


def tie(values, *others):
    return lax.optimization_barrier((values, *others))[0]


def swap(values, axis, bit):
    return lax.ppermute(values, axis, [(i, i ^ bit) for i in range(lax.axis_size(axis))])


def send_far(far_part, got, *others):
    sent = tie((far_part + got[: far_part.shape[0]].astype(F32)).astype(LOW), *others)
    return swap(sent, "mp", 2), sent


def axis_bits(axis):
    return [1 << i for i in range(lax.axis_size(axis).bit_length() - 1)]


def halving_order(bits):
    order = [0]
    for bit in reversed(bits):
        order = order + [r ^ bit for r in order]
    return np.array(order, np.int32)


def scatter_sum(values, axis, bits):
    for bit in bits:
        half = values.shape[0] // 2
        got = swap(values[half:].astype(LOW), axis, bit)
        values = values[:half] + got.astype(F32)
    return values


def gather_back(values, axis, bits):
    for bit in reversed(bits):
        values = jnp.concatenate([values, swap(values, axis, bit)])
    return values


def sum_low(values, axis, bits):
    values = values.astype(LOW)
    for bit in bits:
        values = (values.astype(F32) + swap(values, axis, bit).astype(F32)).astype(LOW)
    return values


def sum_exact(values, axis, bits):
    for bit in bits:
        values = values + swap(values, axis, bit)
    return values


def tile_active(bounds, block, tile):
    return (bounds[2, tile] <= bounds[1, block]) & (bounds[3, tile] >= bounds[0, block])


def attend_block(block, queries, keys, value_ts, q_ids, k_ids, bounds, mixed, row, out_row, logs, scratch):
    scores, peak, total, acc = scratch
    count = queries.shape[0] // 2
    heads = queries.shape[1] // HEAD
    query_rows = queries[row : row + count, :]
    ids = q_ids[:, block * count : (block + 1) * count]
    peak[...] = jnp.full(peak.shape, masked_score, F32)
    total[...] = jnp.zeros(total.shape, F32)
    acc[...] = jnp.zeros(acc.shape, F32)
    for tile in range(4):
        inner = (tile % 2) * count

        @pl.when(tile_active(bounds, block, tile))
        def _(tile=tile, inner=inner):
            allowed = k_ids[tile * count : (tile + 1) * count, :] == ids
            for h in range(heads):
                cols = slice(h * HEAD, (h + 1) * HEAD)
                part = dot_last(keys[tile // 2][inner : inner + count, cols], query_rows[:, cols])
                part = jnp.where(allowed, part, masked_score)
                scores[h, tile] = part
                peak[h : h + 1, :] = jnp.maximum(
                    peak[h : h + 1, :], jnp.max(part, axis=0, keepdims=True)
                )

    for tile in range(4):
        inner = (tile % 2) * count

        @pl.when(tile_active(bounds, block, tile))
        def _(tile=tile, inner=inner):
            for h in range(heads):
                weights = jnp.exp2((scores[h, tile] - peak[h : h + 1, :]) * exp2_scale)
                total[h : h + 1, :] += jnp.sum(weights, axis=0, keepdims=True)
                acc[h] += dot(
                    value_ts[tile // 2][h * HEAD : (h + 1) * HEAD, inner : inner + count],
                    weights.astype(LOW),
                )

    for h in range(heads):
        sums = total[h : h + 1, :]
        mixed[out_row : out_row + count, h * HEAD : (h + 1) * HEAD] = (acc[h] / sums).T.astype(LOW)
        logs[h : h + 1, out_row : out_row + count] = peak[h : h + 1, :] * exp2_scale + jnp.log2(sums)


def attend_scratch(count, heads):
    return [
        pltpu.VMEM((heads, 4, count, count), F32),
        pltpu.VMEM((8, count), F32),
        pltpu.VMEM((8, count), F32),
        pltpu.VMEM((heads, HEAD, count), F32),
    ]


def project_pair(blocks, weights, norm=None):
    count, width = blocks[0].shape[0], weights[0].shape[1]
    dim = blocks[0].shape[1]
    outs = [shape((2 * count, width), LOW) for w in weights] + [shape((width, 2 * count), LOW)] * 2
    ins = list(blocks) + list(weights)
    if norm is not None:
        outs.append(shape((2 * count, dim), LOW))
        ins += list(norm[:2])
    n_weights = len(weights)

    def body(need, emit, *refs):
        rows, ws = refs[:2], refs[2 : 2 + n_weights]
        res = refs[len(ins) :]
        if norm is not None:
            norm_into(rows, refs[2 + n_weights], refs[3 + n_weights], norm[2], res[-1])
            rows = [res[-1].at[:count], res[-1].at[count:]]
        need(0)
        project_into(rows, ws, res)

    return local_kernel(
        body, "project_pair", ins, outs, cold=[range(2, 2 + n_weights)], cold_outs=range(len(outs))
    )


def norm_into(blocks, gain, offset, index, out):
    count = blocks[0].shape[0]
    at = slice(index, index + 1)
    for b in range(2):
        rows = layer_norm(blocks[b][...].astype(F32), gain[at, :], offset[at, :])
        out[b * count : (b + 1) * count, :] = rows.astype(LOW)


def project_into(blocks, weights, res):
    count = blocks[0].shape[0]
    for i, weight in enumerate(weights):
        for b in range(2):
            part = dot(blocks[b][...], weight[...])
            res[i][b * count : (b + 1) * count, :] = part.astype(LOW)
            if i < 2:
                res[len(weights) + i][:, b * count : (b + 1) * count] = part.T.astype(LOW)


def attend_first(far, across, weights, queries_far, near_set, out_weight, ids, norm=None):
    count, dim = far.shape
    width = out_weight.shape[1]
    heads = width // HEAD
    with_query = len(weights) == 3
    q_ids, k_ids, bounds = ids
    n_weights = len(weights)
    first = [far, across, *weights, *(norm[:2] if norm else ())]
    second = [near_set[0], near_set[2], near_set[3], out_weight, q_ids, k_ids]
    if not with_query:
        second.append(queries_far)
    n_first, n_all = len(first), len(first) + len(second)
    ins = first + second + [bounds]
    pair = shape((2 * count, width), LOW)
    turned = shape((width, 2 * count), LOW)
    outs = [pair] * n_weights + [turned, turned]
    if norm is not None:
        outs.append(shape((2 * count, dim), LOW))
    n_project = len(outs)
    outs += [pair, shape((8, 2 * count)), shape((2 * count, dim), LOW)]

    def body(need, emit, *refs):
        res, scratch = refs[len(ins) : len(ins) + len(outs)], refs[len(ins) + len(outs) :]
        rows, ws = refs[:2], refs[2 : 2 + n_weights]
        near_keys, near_values, near_queries, wo, qi, ki = refs[n_first : n_first + 6]
        bnd = refs[n_all]
        if norm is not None:
            norm_into(rows, refs[2 + n_weights], refs[3 + n_weights], norm[2], res[n_project - 1])
            rows = [res[n_project - 1].at[:count], res[n_project - 1].at[count:]]
        need(0)
        project_into(rows, ws, res)
        emit(*res[:n_project])
        need(1)
        far_queries = res[2] if with_query else refs[n_first + 6]
        mixed, logs, hop = res[n_project:]
        for place, (block, source) in enumerate(((3, far_queries), (1, near_queries))):
            attend_block(
                block, source, (near_keys, res[0]), (near_values, res[n_weights + 1]),
                qi, ki, bnd, mixed, (block % 2) * count, place * count, logs, scratch,
            )
            rows_of_mixed = mixed[place * count : (place + 1) * count, :]
            hop[place * count : (place + 1) * count, :] = dot_last(rows_of_mixed, wo[...]).astype(LOW)

    return local_kernel(
        body, "attend_first", ins, outs, attend_scratch(count, heads), smem=(n_all,),
        cold=[range(2, 2 + n_weights), range(n_first, n_all)], cold_outs=range(n_project + 2),
    )


def attend_one(block, queries, near_set, far_set, out_weight, ids, after):
    width = out_weight.shape[1]
    heads = width // HEAD
    count = queries.shape[0] // 2
    dim = out_weight.shape[0]
    q_ids, k_ids, bounds = ids
    ins = [queries, near_set[0], far_set[0], near_set[1], far_set[1], out_weight, q_ids, k_ids, bounds]
    outs = [shape((count, width), LOW), shape((8, count)), shape((count, dim))]

    def body(need, emit, q, k0, k1, v0, v1, wo, qi, ki, bnd, mixed, logs, part, *scratch):
        need(0)
        attend_block(block, q, (k0, k1), (v0, v1), qi, ki, bnd, mixed, 0, 0, logs, scratch)
        part[...] = dot_last(mixed[...], wo[...])

    return local_kernel(
        body, "attend_one", ins, outs, attend_scratch(count, heads), smem=(8,),
        cold=[range(8)], cold_outs=(0, 1), after=after,
    )


def back_block(block, row, grads, queries, logs, keys, key_ts, values, q_ids, k_ids, bounds,
               query_grads, key_acc, value_acc, scratch):
    probs, grad_probs, inner_sum, acc = scratch
    count = queries.shape[0] // 2
    heads = queries.shape[1] // HEAD
    query_rows = queries[row : row + count, :]
    ids = q_ids[:, block * count : (block + 1) * count]
    inner_sum[...] = jnp.zeros(inner_sum.shape, F32)
    acc[...] = jnp.zeros(acc.shape, F32)
    for tile in range(4):
        inner = (tile % 2) * count

        @pl.when(tile_active(bounds, block, tile))
        def _(tile=tile, inner=inner):
            allowed = k_ids[tile * count : (tile + 1) * count, :] == ids
            for h in range(heads):
                cols = slice(h * HEAD, (h + 1) * HEAD)
                part = dot_last(keys[tile // 2][inner : inner + count, cols], query_rows[:, cols])
                exact = jnp.where(
                    allowed,
                    jnp.exp2(part * exp2_scale - logs[0][h : h + 1, logs[1] : logs[1] + count]),
                    0.0,
                )
                pulled = dot_last(values[tile // 2][inner : inner + count, cols], grads[:, cols])
                probs[h, tile] = exact
                grad_probs[h, tile] = pulled
                inner_sum[h : h + 1, :] += jnp.sum(exact * pulled, axis=0, keepdims=True)
                value_acc[tile * count : (tile + 1) * count, cols] += dot(
                    exact.astype(LOW), grads[:, cols]
                )

    for tile in range(4):
        inner = (tile % 2) * count

        @pl.when(tile_active(bounds, block, tile))
        def _(tile=tile, inner=inner):
            for h in range(heads):
                cols = slice(h * HEAD, (h + 1) * HEAD)
                score_grads = (
                    probs[h, tile] * (grad_probs[h, tile] - inner_sum[h : h + 1, :])
                ).astype(LOW)
                key_acc[tile * count : (tile + 1) * count, cols] += dot(
                    score_grads, query_rows[:, cols]
                )
                acc[h] += dot(key_ts[tile // 2][cols, inner : inner + count], score_grads)

    for h in range(heads):
        query_grads[row : row + count, h * HEAD : (h + 1) * HEAD] = (
            (acc[h] * score_scale).T.astype(LOW)
        )


def back_scratch(count, heads):
    return [
        pltpu.VMEM((heads, 4, count, count), F32),
        pltpu.VMEM((heads, 4, count, count), F32),
        pltpu.VMEM((8, count), F32),
        pltpu.VMEM((heads, HEAD, count), F32),
    ]


def back_near(grads, out_weight, queries, logs, kept, ids):
    count = queries.shape[0] // 2
    width = queries.shape[1]
    q_ids, k_ids, bounds = ids
    ins = [*grads, out_weight, queries, *logs, *kept, q_ids, k_ids, bounds]
    outs = [shape((2 * count, width), LOW), shape((4 * count, width)), shape((4 * count, width))]

    def body(need, emit, g0, g1, wo, q, lg, lo, k0, k1, t0, t1, v0, v1, qi, ki, bnd, dq, dk, dv, *scratch):
        need(0)
        dk[...] = jnp.zeros(dk.shape, F32)
        dv[...] = jnp.zeros(dv.shape, F32)
        for b, g in enumerate((g0, g1)):
            mixed_grads = dot(g[...], wo[...]).astype(LOW)
            logs_at = (lg, count) if b else (lo, 0)
            back_block(b, b * count, mixed_grads, q, logs_at, (k0, k1), (t0, t1), (v0, v1), qi, ki, bnd,
                       dq, dk, dv, scratch)

    return local_kernel(body, "back_near", ins, outs, back_scratch(count, width // HEAD), smem=(14,),
        cold=[range(2, 14)], cold_outs=(0,),
    )


def back_far(grads, out_weight, queries, logs, kept, ids, sums, weights, after=()):
    count = queries.shape[0] // 2
    width = queries.shape[1]
    dim = out_weight.shape[0]
    q_ids, k_ids, bounds = ids
    ins = [*grads, out_weight, queries, *logs, *kept, q_ids, k_ids, bounds, *sums, *weights]
    whole = shape((4 * count, width), LOW)
    outs = [shape((2 * count, width), LOW), whole, whole, shape((count, dim)), shape((count, dim), LOW)]

    def body(need, emit, *refs):
        g0, g1, wo, q, lg, lo, k0, k1, t0, t1, v0, v1, qi, ki, bnd, dk_in, dv_in = refs[:17]
        ws = refs[17 : 17 + len(weights)]
        dq, dk, dv, far_out, across_out, key_acc, value_acc, *scratch = refs[17 + len(weights) :]
        need(0)
        key_acc[...] = dk_in[...]
        value_acc[...] = dv_in[...]
        for b, g in enumerate((g0, g1)):
            mixed_grads = dot(g[...], wo[...]).astype(LOW)
            logs_at = (lg, 0) if b else (lo, 0)
            back_block(2 + b, b * count, mixed_grads, q, logs_at, (k0, k1), (t0, t1), (v0, v1), qi, ki, bnd,
                       dq, key_acc, value_acc, scratch)
        dk[...] = (key_acc[...] * score_scale).astype(LOW)
        dv[...] = value_acc[...].astype(LOW)
        need(1)
        for b in (1, 0):
            rows = slice((2 + b) * count, (3 + b) * count)
            part = dot_last(dk[rows, :], ws[0][...]) + dot_last(dv[rows, :], ws[1][...])
            if len(ws) == 3:
                part = part + dot_last(dq[b * count : (b + 1) * count, :], ws[2][...])
            if b:
                across_out[...] = part.astype(LOW)
            else:
                far_out[...] = part

    scratch = [pltpu.VMEM((4 * count, width), F32)] * 2 + back_scratch(count, width // HEAD)
    return local_kernel(
        body, "back_far", ins, outs, scratch, smem=(14,),
        cold=[range(2, 14), range(17, 17 + len(weights))], after=after,
    )


def pull_near(pairs, after):
    dim = pairs[0][1].shape[0]
    count = pairs[0][2]
    ins = [p[0] for p in pairs] + [p[1] for p in pairs]
    outs = [shape((count, dim)), shape((count, dim), LOW)]

    def body(need, emit, *refs):
        n = len(pairs)
        need(0)
        own_out, near_out = refs[2 * n :]
        for b in range(2):
            part = None
            for i in range(n):
                term = dot_last(refs[i][b * count : (b + 1) * count, :], refs[n + i][...])
                part = term if part is None else part + term
            if b:
                near_out[...] = part.astype(LOW)
            else:
                own_out[...] = part

    return local_kernel(
        body, "pull_near", ins, outs, cold=[range(len(pairs), 2 * len(pairs))], after=after
    )


def pull_active(grads, down_proj, after):
    count, units = grads[0].shape[0], down_proj.shape[1]

    def body(need, emit, g0, g1, down, out):
        need(0)
        for b, g in enumerate((g0, g1)):
            out[b * count : (b + 1) * count, :] = dot(g[...], down[...]).astype(LOW)

    return local_kernel(
        body, "pull_active", [*grads, down_proj], [shape((2 * count, units), LOW)], cold=[range(3)], after=after
    )[0]


def mlp_pair(rows, grads, up_proj, down_proj, after=(), pulled=None):
    count, dim = rows[0].shape
    units = up_proj.shape[1]
    step = 256
    outs = [
        shape((2 * count, units), LOW), shape((2 * count, units), LOW),
        shape((count, dim)), shape((count, dim), LOW),
    ]
    ready = pulled is not None
    ins = [*rows, up_proj, pulled] if ready else [*rows, up_proj, down_proj, *grads]

    def body(need, emit, x0, x1, up, *refs):
        active, grad_hidden, first_out, second_out = refs[-4:]
        need(0)
        for b, x in enumerate((x0, x1)):
            band = slice(b * count, (b + 1) * count)
            for at in range(0, units, step):
                hidden = dot(x[...], up[:, at : at + step])
                if ready:
                    back = refs[0][band, at : at + step].astype(F32)
                else:
                    back = dot(refs[1 + b][...], refs[0][:, at : at + step])
                square = hidden * hidden
                bent = jnp.tanh(gelu_coeff * (hidden + gelu_cubic * hidden * square))
                half = 0.5 * (1.0 + bent)
                slope = half + 0.5 * hidden * (1.0 - bent * bent) * (
                    gelu_coeff * (1.0 + 3.0 * gelu_cubic * square)
                )
                active[band, at : at + step] = (hidden * half).astype(LOW)
                grad_hidden[band, at : at + step] = (back * slope).astype(LOW)
        emit(active, grad_hidden)
        for b in (1, 0):
            part = dot_last(grad_hidden[b * count : (b + 1) * count, :], up[...])
            if b:
                second_out[...] = part.astype(LOW)
            else:
                first_out[...] = part

    return local_kernel(
        body, "mlp_pair", ins, outs, cold=[[2] if ready else range(2, 6)], cold_outs=(0, 1), after=after,
    )


def pull_four(near_rows, far_rows, weight, after):
    count, dim = near_rows.shape[0] // 2, weight.shape[0]
    outs = [shape((count, dim)), shape((count, dim)), shape((2 * count, dim), LOW)]

    def body(need, emit, x, y, w, own_out, far_out, hop):
        need(0)
        own_out[...] = dot_last(x[:count, :], w[...])
        far_out[...] = dot_last(y[:count, :], w[...])
        hop[:count, :] = dot_last(y[count:, :], w[...]).astype(LOW)
        hop[count:, :] = dot_last(x[count:, :], w[...]).astype(LOW)

    return local_kernel(
        body, "pull_four", [near_rows, far_rows, weight], outs, cold=[range(3)], cold_outs=(0, 1, 2), after=after
    )


def norm_rows(terms, gain, offset, index):
    kept = terms[0]

    def body(need, emit, k, p, n, f, g, o, after, normed):
        total = p[...] + n[n.shape[0] - p.shape[0] :, :].astype(F32) + f[...].astype(F32)
        need(0)
        total = total + k[...]
        after[...] = total
        emit(after)
        normed[...] = layer_norm(total, g[index : index + 1, :], o[index : index + 1, :]).astype(LOW)

    return local_kernel(
        body, "norm_rows", [*terms, gain, offset], [shape(kept.shape), shape(kept.shape, LOW)],
        cold=[[0]], cold_outs=(0,),
    )


def norm_rows_back(values, gain, index, terms, grads, after=(), inside=False):
    added = grads is not None

    def body(need, emit, v, g, p, n, f, *refs):
        if inside:
            need(0)
        total = p[...] + n[...].astype(F32) + f[...].astype(F32)
        if not inside:
            need(0)
        back, gain_sum, offset_sum = layer_norm_back(v[...].astype(F32), g[index : index + 1, :], total)
        if added:
            back = back + refs[0][...].astype(F32)
            out, sums = refs[1:]
            sums[0:1, :] = gain_sum
            sums[1:2, :] = offset_sum
        else:
            out = refs[0]
        out[...] = back.astype(out.dtype)

    ins = [values, gain, *terms]
    outs = [shape(values.shape, LOW if added else F32)]
    if added:
        ins.append(grads)
        outs.append(shape((2, values.shape[1])))
    return local_kernel(
        body, "norm_back", ins, outs, cold=[[0, 2, 5] if inside else [0, 5] if added else [0]], cold_outs=() if added else (0,),
        vmem=VMEM_LARGE if inside else VMEM_BYTES, after=after,
    )


def dp_orders():
    bits = axis_bits("dp")
    return [bits, bits[1:2] + bits[:1] + bits[2:]]


def outer_sums(sets, after, parts_sent=1):
    n_dp = lax.axis_size("dp")
    place = lax.axis_index("dp")
    ins, plans, places, outs = [], [], [], []
    seen = {}

    def take(array):
        if id(array) not in seen:
            seen[id(array)] = len(ins)
            ins.append(array)
        return seen[id(array)]

    for groups, bits in zip(sets, dp_orders()):
        plan = []
        for blocks, parts in groups:
            terms = []
            if len(parts) == 3:
                count = blocks[0].shape[0]
                terms = [
                    (take(blocks[0]), take(parts[0]), 0, count),
                    (take(blocks[1][1]), take(parts[1]), 0, count),
                    (take(blocks[1][0]), take(parts[1]), count, count),
                    (take(blocks[2]), take(parts[2]), 0, count),
                ]
            else:
                per = len(blocks) // len(parts)
                for b, block in enumerate(blocks):
                    count = block.shape[0]
                    terms.append((take(block), take(parts[b // per]), (b % per) * count, count))
            plan.append((terms, parts[0].shape[1]))
        plans.append(plan)
        dim = groups[0][0][0].shape[1]
        chunk = dim // n_dp
        aligned = chunk % 128 == 0
        steps = dim // 128
        width = sum(p[1] for p in plan)
        if aligned:
            repeat = chunk // 128
            spots = (jnp.asarray(halving_order(bits)) ^ place)[:, None] * repeat
            spots = (spots + jnp.arange(repeat, dtype=jnp.int32)[None, :]).reshape(steps)
        else:
            spots = jnp.arange(steps, dtype=jnp.int32)
        places.append(spots.astype(jnp.int32))
        outs += [shape((dim // 2, width))] + [shape((dim // 2 // parts_sent, width), LOW)] * parts_sent
    ins.append(jnp.stack(places))

    def body(need, emit, *refs):
        need(0)
        spots = refs[len(ins) - 1]
        results = refs[len(ins) :]

        def one(order, index, target, base):
            at = pl.multiple_of(spots[order, base + index] * 128, 128)
            column = 0
            for terms, right_width in plans[order]:
                total = None
                for left, right, row, count in terms:
                    term = dot_first(refs[left][:, pl.ds(at, 128)], refs[right][row : row + count, :])
                    total = term if total is None else total + term
                target[pl.ds(pl.multiple_of(index * 128, 128), 128), column : column + right_width] = (
                    total.astype(target.dtype)
                )
                column += right_width

        per = 1 + parts_sent
        half = steps // 2
        for piece in [*range(1, per), 0]:
            for order in range(len(plans)):
                run = half if piece == 0 else half // parts_sent
                base = 0 if piece == 0 else half + (piece - 1) * run

                @pl.loop(0, run)
                def _(index, target=results[per * order + piece], order=order, base=base):
                    one(order, index, target, base)

    results = local_kernel(
        body, "outer_sums", ins, outs, smem=(len(ins) - 1,), cold=[range(len(ins) - 1)],
        cold_outs=range(len(outs)), vmem=VMEM_LARGE, after=after,
    )
    pairs = []
    for order, bits in enumerate(dp_orders()[: len(plans)]):
        keep, *sent = results[(1 + parts_sent) * order : (1 + parts_sent) * (order + 1)]
        if not aligned:
            whole = jnp.concatenate([keep, *[part.astype(F32) for part in sent]])
            whole = whole.reshape(n_dp, chunk, keep.shape[1])
            whole = whole[jnp.asarray(halving_order(bits)) ^ place].reshape(dim, keep.shape[1])
            keep, whole = whole[: dim // 2], whole[dim // 2 :].astype(LOW)
            sent = [part for part in whole.reshape(parts_sent, dim // 2 // parts_sent, keep.shape[1])]
        pairs.append((keep, *sent))
    return pairs


def outer_whole(groups, after):
    ins = [a for blocks, parts in groups for a in (*blocks, *parts)]
    dim = groups[0][0][0].shape[1]
    width = groups[0][1][0].shape[1]
    step = 256

    def body(need, emit, *refs):
        out = refs[len(ins)]
        for k in range(len(groups)):
            need(k)
            lefts, rights = refs[6 * k : 6 * k + 4], refs[6 * k + 4 : 6 * k + 6]
            count = lefts[0].shape[0]

            @pl.loop(0, dim // step)
            def _(index, k=k, lefts=lefts, rights=rights, count=count):
                at = pl.multiple_of(index * step, step)
                total = None
                for b in range(4):
                    right = rights[b // 2][(b % 2) * count : (b % 2 + 1) * count, :]
                    term = dot_first(lefts[b][:, pl.ds(at, step)], right)
                    total = term if total is None else total + term
                out[pl.ds(at, step), k * width : (k + 1) * width] = total.astype(LOW)

    return local_kernel(
        body, "outer_whole", ins, [shape((dim, width * len(groups)), LOW)],
        cold=[range(6 * k, 6 * k + 6) for k in range(len(groups))], cold_outs=(0,), vmem=VMEM_LARGE, after=after,
    )[0]


def merge(pairs, last, widths, after=()):
    ins, outs, firsts = [], [], []
    for order, (keep, *came) in enumerate(pairs):
        firsts.append(len(ins))
        ins += [keep, *came]
        rows, width = keep.shape
        if last:
            outs += [shape((rows, w)) for w in widths[order]]
        else:
            outs += [shape((rows // 2, width)), shape((rows // 2, width), LOW)]

    def body(need, emit, *refs):
        results = list(refs[len(ins) :])
        for order in range(len(pairs)):
            keep, got = refs[firsts[order]], refs[firsts[order] + 1]
            if last:
                column = 0
                for w in widths[order]:
                    cols = slice(column, column + w)
                    results.pop(0)[...] = keep[:, cols] + got[:, cols].astype(F32)
                    column += w
            else:
                half = keep.shape[0] // 2
                later = got[half:, :] if len(pairs[order]) == 2 else refs[firsts[order] + 2][...]
                results.pop(0)[...] = keep[:half, :] + got[:half, :].astype(F32)
                results.pop(0)[...] = (keep[half:, :] + later.astype(F32)).astype(LOW)

    results = local_kernel(body, "merge", ins, outs, after=after)
    if last:
        return results
    return [(results[2 * i], results[2 * i + 1]) for i in range(len(pairs))]


def rows_of(source, row_start, row_count):
    return lax.dynamic_slice_in_dim(source, row_start, row_count, 0)


def turn_row(row):
    columns = []
    for at in range(0, row.shape[1], 128):
        columns.append(jnp.broadcast_to(row[:, at : at + 128], (128, 128)).T[:, 0:1])
    return jnp.concatenate(columns, axis=0)


def prepare(latent_row, input_row, member, table, gain, offset, query_weight, images):
    total = latent_row.shape[1]
    count = total // 4
    slots, dim = table.shape
    width = query_weight.shape[1]
    whole = jnp.int32
    outs = [
        shape((1, total), whole), shape((total, 1), whole), shape((total, 1), whole),
        shape((4, 4), whole), shape((4, 4), whole),
        shape((total, slots), LOW), shape((slots, dim), LOW),
        shape((2 * count, width), LOW), shape((2 * count, width), LOW), shape((count, dim)),
    ]

    def body(need, emit, lat, inp, lat_s, inp_s, who, tb, g, o, wq,
             lat_out, lat_col, inp_col, cross_ends, self_ends, pick, normed, near_q, far_q, start):
        order = [who[0, 0] ^ k for k in range(4)]
        for k in range(4):
            first = order[k] * count
            last = first + count - 1
            cross_ends[0, k] = lat_s[0, first]
            cross_ends[1, k] = lat_s[0, last]
            cross_ends[2, k] = inp_s[0, first]
            cross_ends[3, k] = inp_s[0, last]
            for r in range(2):
                self_ends[2 * r, k] = lat_s[0, first]
                self_ends[2 * r + 1, k] = lat_s[0, last]
        starts = [pl.multiple_of(at * count, count) for at in order]
        lat_rel = jnp.concatenate([lat[:, pl.ds(at, count)] for at in starts], axis=1)
        inp_rel = jnp.concatenate([inp[:, pl.ds(at, count)] for at in starts], axis=1)
        lane = lax.broadcasted_iota(whole, (1, count), 1)
        place = jnp.concatenate([lane + at for at in starts], axis=1)
        lat_all = lat[...]
        for image in range(images):
            before = jnp.sum((lat_all < image).astype(F32), axis=1, keepdims=True).astype(whole)
            place = place - jnp.where(lat_rel == image, before, 0)
        lat_out[...] = lat_rel
        lat_col[...] = turn_row(lat_rel)
        inp_col[...] = turn_row(inp_rel)
        slot = turn_row(place)
        slot_lane = lax.broadcasted_iota(whole, (total, slots), 1)
        pick[...] = jnp.where(slot == slot_lane, 1.0, 0.0).astype(LOW)
        normed[...] = layer_norm(tb[...].astype(F32), g[0:1, :], o[0:1, :]).astype(LOW)
        start[...] = dot(pick[:count, :], tb[...])
        need(0)
        queries = dot(normed[...], wq[...]).astype(LOW)
        near_q[...] = dot(pick[: 2 * count, :], queries).astype(LOW)
        far_q[...] = dot(pick[2 * count :, :], queries).astype(LOW)

    return local_kernel(
        body, "prepare",
        [latent_row, input_row, latent_row, input_row, member, table, gain, offset, query_weight],
        outs, smem=(2, 3, 4), smem_outs=(3, 4), cold=[[8]],
    )


def slot_stack(pick, query_pairs, raw_blocks, parts, grads, sums, member, after):
    count, dim = raw_blocks[0].shape
    slots, width = pick.shape[1], query_pairs[0].shape[1]
    cut = dim // (2 * width)
    ins = [pick, *query_pairs, *raw_blocks, *parts, *grads, *sums, member]

    def body(need, emit, pk, q0, q1, x0, x1, x2, x3, p0, p1, p2, p3, r0, r1, r2, r3, s0, s1, who, out):
        need(0)
        total = dot_first(pk[: 2 * count, :], q0[...]) + dot_first(pk[2 * count :, :], q1[...])
        out[:slots, :width] = total.astype(LOW)
        at = pl.multiple_of(who[0, 0] * width, width)
        total = None
        for b, r in enumerate((r0, r1, r2, r3)):
            term = dot_first(pk[b * count : (b + 1) * count, :], r[:, pl.ds(at, width)])
            total = term if total is None else total + term
        out[:slots, width:] = total.astype(LOW)
        gain_sum = offset_sum = None
        for x, p in ((x0, p0), (x1, p1), (x2, p2), (x3, p3)):
            values = x[...].astype(F32)
            centred = values - jnp.mean(values, axis=-1, keepdims=True)
            spread = jnp.mean(centred * centred, axis=-1, keepdims=True)
            back = p[...].astype(F32)
            gains = jnp.sum(back * (centred * lax.rsqrt(spread + norm_eps)), axis=0, keepdims=True)
            offsets = jnp.sum(back, axis=0, keepdims=True)
            gain_sum = gains if gain_sum is None else gain_sum + gains
            offset_sum = offsets if offset_sum is None else offset_sum + offsets
        rows = [gain_sum, offset_sum, s0[0:1, :], s0[1:2, :], s1[0:1, :], s1[1:2, :]]
        rows += [jnp.zeros((1, dim), F32)] * 2
        whole = jnp.concatenate(rows, axis=0)
        for q in range(cut):
            out[slots + 8 * q : slots + 8 * (q + 1), :] = (
                whole[:, 2 * q * width : 2 * (q + 1) * width].astype(LOW)
            )

    return local_kernel(
        body, "slot_stack", ins, [shape((slots + 8 * cut, 2 * width), LOW)],
        smem=(len(ins) - 1,), cold=[range(7)], after=after,
    )[0]


def table_end(stacks, weights, gain, table, member):
    slots, dim = table.shape
    width = stacks[0].shape[1] // 2
    cut = dim // (2 * width)
    ins = [*stacks, *weights, gain, table, member]

    def body(need, emit, *refs):
        st, ws = refs[:4], refs[4:8]
        g, tb, who = refs[8:11]
        table_out, gain_out, offset_out, last_out, residual, grads, weight = refs[11:]
        need(0)
        for k in range(4):
            at = pl.multiple_of((who[0, 0] ^ k) * width, width)
            grads[:, pl.ds(at, width)] = st[k][:slots, :width]
            residual[:, pl.ds(at, width)] = st[k][:slots, width:]
            weight[:, pl.ds(at, width)] = ws[k][...]
        total = dot_last(grads[...], weight[...])
        back, gain_sum, offset_sum = layer_norm_back(tb[...].astype(F32), g[0:1, :], total)
        table_out[...] = residual[...].astype(F32) + back
        small = [st[k][slots:, :].astype(F32) for k in range(4)]
        small = (small[0] + small[1]) + (small[2] + small[3])
        small = jnp.concatenate([small[8 * q : 8 * (q + 1), :] for q in range(cut)], axis=1)
        gain_out[0:1, :] = gain_sum
        offset_out[0:1, :] = offset_sum
        for k in range(3):
            gain_out[k + 1 : k + 2, :] = small[2 * k : 2 * k + 1, :]
            target = last_out if k == 2 else offset_out
            at = 0 if k == 2 else k + 1
            target[at : at + 1, :] = small[2 * k + 1 : 2 * k + 2, :]

    outs = [shape((slots, dim)), shape((4, dim)), shape((3, dim)), shape((1, dim))]
    return local_kernel(
        body, "table_end", ins, outs,
        [pltpu.VMEM((slots, dim), LOW), pltpu.VMEM((slots, dim), LOW), pltpu.VMEM((dim, dim), LOW)],
        smem=(10,), cold=[range(4, 8)],
    )


def body(
    block_input,
    latent_table,
    latent_segments,
    input_segments,
    ln_gain,
    ln_bias,
    cross_query,
    cross_key,
    cross_value,
    cross_out,
    self_query,
    self_key,
    self_value,
    self_out,
    up_proj,
    down_proj,
    out_grad,
):
    count, dim = block_input.shape
    member = lax.axis_index("mp")
    n_mp, n_dp = lax.axis_size("mp"), lax.axis_size("dp")
    slots = latent_table.shape[0]
    mp_bits, dp_bits = axis_bits("mp"), axis_bits("dp")
    dp_steps = len(dp_bits)

    far_raw = swap(block_input, "mp", 2)
    near_raw = swap(block_input, "mp", 1)
    near_out = swap(out_grad, "mp", 1)
    half = count // 2
    near_raw, out_1, out_2 = lax.optimization_barrier((near_raw, out_grad[:half], out_grad[half:]))

    who = member.astype(jnp.int32).reshape(1, 1)
    (latent_rel, latent_col, input_col, cross_ends, self_ends, table_pick, normed_table, queries_near,
     queries_far, start_rows) = prepare(
        latent_segments, input_segments, who, latent_table, ln_gain, ln_bias, cross_query, images
    )
    cross_ids = (latent_rel, input_col, cross_ends)
    self_ids = (latent_rel, latent_col, self_ends)

    input_norm = (ln_gain, ln_bias, 1)
    keys_near, values_near, key_ts_near, value_ts_near, normed_near = project_pair(
        (block_input, near_raw), (cross_key, cross_value), input_norm
    )
    far_raw = tie(far_raw, keys_near, queries_far)
    across_raw = swap(far_raw, "mp", 1)
    far_out_1 = swap(tie(out_1, far_raw), "mp", 2)
    (keys_far, values_far, key_ts_far, value_ts_far, normed_far, mixed_two, logs_two, hop) = attend_first(
        far_raw, across_raw, (cross_key, cross_value), queries_far,
        (keys_near, key_ts_near, value_ts_near, queries_near), cross_out, cross_ids, input_norm,
    )
    got = swap(tie(hop, far_out_1), "mp", 1)
    key_values = ((keys_near, value_ts_near), (keys_far, value_ts_far))
    mixed_far, logs_far, part_far = attend_one(2, queries_far, *key_values, cross_out, cross_ids, ())
    got_far, sent = send_far(part_far, got)
    mixed_own, logs_own, part_own = attend_one(0, queries_near, *key_values, cross_out, cross_ids, (sent,))
    cross_kept = (keys_near, keys_far, key_ts_near, key_ts_far, values_near, values_far)
    cross_queries_set = (queries_near, queries_far)
    cross_logs = ((logs_two, logs_own), (logs_two, logs_far))
    cross_mixed = (mixed_own, mixed_two, mixed_far)
    after_cross, normed_self = norm_rows((start_rows, part_own, got, got_far), ln_gain, ln_bias, 2)

    self_weights = (self_key, self_value, self_query)
    far_self = swap(normed_self, "mp", 2)
    near_self = swap(normed_self, "mp", 1)
    keys_near, values_near, queries_near, key_ts_near, value_ts_near = project_pair(
        (normed_self, near_self), self_weights
    )
    far_self = tie(far_self, keys_near)
    across_self = swap(far_self, "mp", 1)
    far_out_2 = swap(tie(out_2, far_self), "mp", 2)
    (keys_far, values_far, queries_far, key_ts_far, value_ts_far, mixed_two, logs_two, hop) = attend_first(
        far_self, across_self, self_weights, None,
        (keys_near, key_ts_near, value_ts_near, queries_near), self_out, self_ids,
    )
    got = swap(tie(hop, far_out_2), "mp", 1)
    key_values = ((keys_near, value_ts_near), (keys_far, value_ts_far))
    mixed_far, logs_far, part_far = attend_one(2, queries_far, *key_values, self_out, self_ids, ())
    got_far, sent = send_far(part_far, got)
    mixed_own, logs_own, part_own = attend_one(0, queries_near, *key_values, self_out, self_ids, (sent,))
    far_out = tie(jnp.concatenate([far_out_1, far_out_2]), part_own)
    across_out = swap(far_out, "mp", 1)
    self_kept = (keys_near, keys_far, key_ts_near, key_ts_far, values_near, values_far)
    self_queries_set = (queries_near, queries_far)
    self_logs = ((logs_two, logs_own), (logs_two, logs_far))
    self_mixed = (mixed_own, mixed_two, mixed_far)
    after_self, normed_mlp = norm_rows((after_cross, part_own, got, got_far), ln_gain, ln_bias, 3)

    far_mlp = swap(normed_mlp, "mp", 2)
    near_mlp = swap(normed_mlp, "mp", 1)
    active_near, hidden_near, part_own, part_near = mlp_pair(
        (normed_mlp, near_mlp), (out_grad, near_out), up_proj, down_proj, (across_out,)
    )
    pulled_far = pull_active((far_out, across_out), down_proj, (part_near,))
    far_mlp = tie(far_mlp, pulled_far)
    across_mlp = swap(far_mlp, "mp", 1)
    active_far, hidden_far, part_far, part_across = mlp_pair(
        (far_mlp, across_mlp), None, up_proj, None, (), pulled_far
    )
    got = swap(part_across, "mp", 1)
    got_far, sent = send_far(part_far, got)
    got_near = swap(part_near, "mp", 1)
    mlp_grads = outer_whole(
        [
            ((normed_mlp, near_mlp, far_mlp, across_mlp), (hidden_near, hidden_far)),
            ((out_grad, near_out, far_out, across_out), (active_near, active_far)),
        ],
        (sent, got_near),
    )
    mlp_sum = lax.psum_scatter(tie(mlp_grads, got_far), "dp", scatter_dimension=0, tiled=True)
    dy_own, mlp_sums = norm_rows_back(
        after_self, ln_gain, 3, (part_own, got_near, got_far), out_grad,
        (mlp_grads,), True,
    )

    far_dy = swap(dy_own, "mp", 2)
    near_dy = swap(dy_own, "mp", 1)

    query_near, key_sum, value_sum = back_near(
        (dy_own, near_dy), self_out, self_queries_set[0], self_logs[0], self_kept, self_ids
    )
    far_dy = tie(far_dy, key_sum)
    across_dy = swap(far_dy, "mp", 1)
    query_far, key_grads, value_grads, part_far, part_across = back_far(
        (far_dy, across_dy), self_out, self_queries_set[1], self_logs[1], self_kept, self_ids,
        (key_sum, value_sum), self_weights,
    )
    got = swap(part_across, "mp", 1)
    part_own, part_near = pull_near(
        [(key_grads, self_key, count), (value_grads, self_value, count), (query_near, self_query, count)], ()
    )
    got_far, sent = send_far(part_far, got, part_own)
    got_near = swap(part_near, "mp", 1)
    normed_blocks = (normed_self, near_self, far_self, across_self)
    self_pairs = outer_sums(
        [
            [
                (normed_blocks, (query_near, query_far)), (normed_blocks, (key_grads,)),
                (normed_blocks, (value_grads,)), ((dy_own, (near_dy, across_dy), far_dy), self_mixed),
            ],
        ],
        (sent, got_near), 2,
    )
    dy_cross, self_sums = norm_rows_back(
        after_cross, ln_gain, 2, (part_own, got_near, got_far), dy_own,
        (self_pairs[0][1],),
    )

    far_dyc = swap(dy_cross, "mp", 2)
    near_dyc = swap(dy_cross, "mp", 1)
    query_near, key_sum, value_sum = back_near(
        (dy_cross, near_dyc), cross_out, cross_queries_set[0], cross_logs[0], cross_kept, cross_ids
    )
    part_own_out, part_far_out, hop_out = pull_four(active_near, active_far, down_proj, (key_sum,))
    self_half = swap(self_pairs[0][1], "dp", dp_bits[0])
    far_dyc = tie(far_dyc, part_own_out, self_half)
    across_dyc = swap(far_dyc, "mp", 1)
    query_far, key_grads, value_grads, part_far, part_across = back_far(
        (far_dyc, across_dyc), cross_out, cross_queries_set[1], cross_logs[1], cross_kept, cross_ids,
        (key_sum, value_sum), (cross_key, cross_value),
    )
    dyc_blocks = (dy_cross, near_dyc, far_dyc, across_dyc)
    part_own, part_near = pull_near([(key_grads, cross_key, count), (value_grads, cross_value, count)], ())
    got = swap(part_across, "mp", 1)
    got_near = swap(part_near, "mp", 1)
    got_far, sent = send_far(part_far, got, part_own)

    up_width = up_proj.shape[1]
    heads_width = cross_query.shape[1]
    stack = slot_stack(
        table_pick, (query_near, query_far), (block_input, near_raw, far_raw, across_raw),
        (part_own, part_near, part_far, part_across), dyc_blocks, (self_sums, mlp_sums), who,
        (sent,),
    )
    input_blocks = (normed_near, normed_far)
    cross_sets = [
        [
            (input_blocks, (key_grads,)),
            (input_blocks, (value_grads,)),
            ((dy_cross, (near_dyc, across_dyc), far_dyc), cross_mixed),
        ],
    ]
    self_keep, _, self_sent = self_pairs[0]

    def dp_swap(values, step):
        return swap(values, "dp", dp_bits[step])

    def joined(mine, came):
        return (mine.astype(F32) + came.astype(F32)).astype(LOW)

    def halved(keep, *came):
        return merge([(keep, *came)], False, None)[0]

    stack_got, self_got = dp_swap(stack, 0), dp_swap(self_sent, 0)
    ((cross_keep, cross_sent),) = outer_sums(cross_sets, (stack,))
    got_far, got_near, stack, stack_got, self_got, cross_sent, hop_out, query_sent = wait(
        got_far, got_near, stack, stack_got, self_got, cross_sent, hop_out, cross_query
    )
    stack = joined(stack, stack_got)

    self_keep, self_sent = halved(self_keep, self_half, self_got)
    stack_got, self_got, cross_got = dp_swap(stack, 1), dp_swap(self_sent, 1), dp_swap(cross_sent, 0)
    far_query, near_query = swap(query_sent, "mp", 2), swap(query_sent, "mp", 1)
    got_out = swap(hop_out, "mp", 1)
    stack, stack_got, got_out, self_sent, got_far = wait(stack, stack_got, got_out, self_sent, got_far)
    stack = joined(stack, stack_got)
    sent_out = (part_far_out + got_out[:count].astype(F32)).astype(LOW)

    stack_got = dp_swap(stack, 2)
    got_far_out = swap(sent_out, "mp", 2)
    (grad_input,) = norm_rows_back(block_input, ln_gain, 1, (part_own, got_near, got_far), None)
    mlp_parts = [mlp_sum[:, :up_width].astype(F32), mlp_sum[:, up_width:].astype(F32)]
    stack, stack_got, self_got, cross_got, mlp_parts, grad_input = wait(
        stack, stack_got, self_got, cross_got, mlp_parts, grad_input
    )
    stack = joined(stack, stack_got)

    for step in range(3, dp_steps):
        self_keep, self_sent = halved(self_keep, self_got)
        cross_keep, cross_sent = halved(cross_keep, cross_got)
        stack_got, cross_got, self_got = wait(
            dp_swap(stack, step), dp_swap(cross_sent, step - 2), dp_swap(self_sent, step - 1)
        )
        stack = joined(stack, stack_got)

    far_stack, near_stack = swap(stack, "mp", 2), swap(stack, "mp", 1)
    cross_keep, cross_sent = halved(tie(cross_keep, stack), cross_got)
    cross_got = dp_swap(cross_sent, dp_steps - 2)
    self_keep, self_sent = halved(tie(self_keep, cross_sent), self_got)
    self_got = dp_swap(self_sent, dp_steps - 1)
    chunk = dim // n_dp
    own_features = lax.dynamic_slice_in_dim(normed_table, lax.axis_index("dp") * chunk, chunk, 1)
    query_sum = dot_first(own_features, stack[:slots, :heads_width])
    block_output = (
        after_self + part_own_out + got_out[count:].astype(F32) + got_far_out.astype(F32)
    )
    far_stack, cross_got, self_got, far_query, near_query, block_output, query_sum = wait(
        far_stack, cross_got, self_got, far_query, near_query, block_output, query_sum
    )

    across_stack = swap(far_stack, "mp", 1)
    across_query = swap(far_query, "mp", 1)
    cross_keep, cross_sent = halved(cross_keep, cross_got)
    cross_got = dp_swap(cross_sent, dp_steps - 1)
    across_stack, cross_sent = wait(across_stack, cross_sent)
    table_grad, ln_gain_grad, ln_bias_grad, last_bias = table_end(
        (stack, near_stack, far_stack, across_stack),
        (cross_query, near_query, far_query, across_query), ln_gain, latent_table, who,
    )
    cross_keep, self_keep, table_grad = wait(cross_keep, self_keep, table_grad)
    self_pair = merge([(self_keep, self_got)], True, [[heads_width] * 4])
    cross_pair = merge([(cross_keep, cross_got)], True, [[heads_width] * 3])

    return (
        block_output,
        grad_input,
        table_grad,
        ln_gain_grad,
        ln_bias_grad,
        last_bias[0],
        query_sum,
        *cross_pair,
        *self_pair,
        *mlp_parts,
    )


def solution(mesh):
    placed = (
        P(("dp", "mp"), None),
        P(),
        P("dp", None),
        P("dp", None),
        P(),
        P(),
        P(None, "mp"),
        P(None, "mp"),
        P(None, "mp"),
        P(None, "mp"),
        P(None, "mp"),
        P(None, "mp"),
        P(None, "mp"),
        P(None, "mp"),
        P(None, "mp"),
        P(None, "mp"),
        P(("dp", "mp"), None),
    )
    return jax.shard_map(
        body,
        mesh=mesh,
        in_specs=placed,
        out_specs=(
            P(("dp", "mp"), None),
            P(("dp", "mp"), None),
            P(),
            P(),
            P(),
            P(),
            P("dp", "mp"),
            P("dp", "mp"),
            P("dp", "mp"),
            P("dp", "mp"),
            P("dp", "mp"),
            P("dp", "mp"),
            P("dp", "mp"),
            P("dp", "mp"),
            P("dp", "mp"),
            P("dp", "mp"),
        ),
        check_vma=False,
    )
```

```python
import jax
import jax.numpy as jnp
import numpy as np
from jax import lax
from jax.experimental import pallas as pl
from jax.experimental.pallas import tpu as pltpu
from jax.sharding import PartitionSpec as P

HEAD = 128
images = 16
norm_eps = 1e-05
masked_score = -1e30
gelu_coeff = 0.7978845608028654
gelu_cubic = 0.044715
log2_e = 1.4426950408889634
score_scale = HEAD ** (-0.5)
exp2_scale = score_scale * log2_e
LOW = jnp.bfloat16
F32 = jnp.float32
VMEM_BYTES = 32 * 1024 * 1024
VMEM_LARGE = 56 * 1024 * 1024


def layer_norm(values, gain, offset):
    average = jnp.mean(values, axis=-1, keepdims=True)
    centred = values - average
    spread = jnp.mean(centred * centred, axis=-1, keepdims=True)
    return centred * lax.rsqrt(spread + norm_eps) * gain + offset


def layer_norm_back(values, gain, grad):
    average = jnp.mean(values, axis=-1, keepdims=True)
    centred = values - average
    spread = jnp.mean(centred * centred, axis=-1, keepdims=True)
    inverse = lax.rsqrt(spread + norm_eps)
    normal = centred * inverse
    scaled = grad * gain
    inner = jnp.mean(scaled * normal, axis=-1, keepdims=True)
    back = inverse * (scaled - jnp.mean(scaled, axis=-1, keepdims=True) - normal * inner)
    return (
        back,
        jnp.sum(grad * normal, axis=0, keepdims=True),
        jnp.sum(grad, axis=0, keepdims=True),
    )


def dot(left, right):
    return jnp.dot(left, right, preferred_element_type=F32)


def dot_last(left, right):
    return lax.dot_general(left, right, (((1,), (1,)), ((), ())), preferred_element_type=F32)


def dot_first(left, right):
    return lax.dot_general(left, right, (((0,), (0,)), ((), ())), preferred_element_type=F32)


def shape(dims, kind=F32):
    return jax.ShapeDtypeStruct(dims, kind)


def local_kernel(body, name, ins, outs, scratch=(), smem=(), cold=None, cold_outs=(), smem_outs=(), vmem=VMEM_BYTES, after=()):
    if after:
        ins = [tie(ins[0], *after), *ins[1:]]
    n_in, n_out = len(ins), len(outs)
    groups = [list(g) for g in (cold or [])]
    moved = [i for g in groups for i in g]
    held = [pltpu.VMEM(ins[i].shape, ins[i].dtype) for i in moved]
    held += [pltpu.VMEM(outs[o].shape, outs[o].dtype) for o in cold_outs]
    sems = []
    if moved:
        sems.append(pltpu.SemaphoreType.DMA((len(moved),)))
    if cold_outs:
        sems.append(pltpu.SemaphoreType.DMA((len(cold_outs),)))

    def run(*refs):
        inside = list(refs[:n_in])
        results = list(refs[n_in : n_in + n_out])
        rest = list(refs[n_in + n_out :])
        buffers, rest = rest[: len(held)], rest[len(held) :]
        in_sem = rest.pop(0) if moved else None
        out_sem = rest.pop(0) if cold_outs else None
        copies, waited, sent = {}, set(), {}
        for place, i in enumerate(moved):
            copies[i] = pltpu.make_async_copy(refs[i], buffers[place], in_sem.at[place])
            copies[i].start()
            inside[i] = buffers[place]
        made = list(results)
        for place, o in enumerate(cold_outs):
            made[o] = buffers[len(moved) + place]

        def need(*which):
            for k in which:
                for i in groups[k]:
                    copies[i].wait()
                waited.add(k)

        def emit(*given):
            for ref in given:
                for place, o in enumerate(cold_outs):
                    if made[o] is ref and o not in sent:
                        sent[o] = pltpu.make_async_copy(made[o], results[o], out_sem.at[place])
                        sent[o].start()

        body(need, emit, *inside, *made, *rest)
        for k in range(len(groups)):
            if k not in waited:
                need(k)
        emit(*[made[o] for o in cold_outs])
        for o in cold_outs:
            sent[o].wait()

    spaces = [pltpu.VMEM] * n_in
    for i in smem:
        spaces[i] = pltpu.SMEM
    for i in moved:
        spaces[i] = pl.ANY
    return pl.pallas_call(
        run,
        name=name,
        out_shape=list(outs),
        in_specs=[pl.BlockSpec(memory_space=s) for s in spaces],
        out_specs=[
            pl.BlockSpec(memory_space=pl.ANY if o in cold_outs else pltpu.SMEM if o in smem_outs else pltpu.VMEM)
            for o in range(n_out)
        ],
        scratch_shapes=held + sems + list(scratch),
        compiler_params=pltpu.CompilerParams(vmem_limit_bytes=vmem),
        cost_estimate=pl.CostEstimate(flops=1000, bytes_accessed=1000, transcendentals=0),
    )(*ins)


def wait(*arrays):
    return lax.optimization_barrier(arrays)


def tie(values, *others):
    return lax.optimization_barrier((values, *others))[0]


def swap(values, axis, bit):
    return lax.ppermute(values, axis, [(i, i ^ bit) for i in range(lax.axis_size(axis))])


def send_far(far_part, got, *others):
    sent = tie((far_part + got[: far_part.shape[0]].astype(F32)).astype(LOW), *others)
    return swap(sent, "mp", 2), sent


def axis_bits(axis):
    return [1 << i for i in range(lax.axis_size(axis).bit_length() - 1)]


def halving_order(bits):
    order = [0]
    for bit in reversed(bits):
        order = order + [r ^ bit for r in order]
    return np.array(order, np.int32)


def scatter_sum(values, axis, bits):
    for bit in bits:
        half = values.shape[0] // 2
        got = swap(values[half:].astype(LOW), axis, bit)
        values = values[:half] + got.astype(F32)
    return values


def gather_back(values, axis, bits):
    for bit in reversed(bits):
        values = jnp.concatenate([values, swap(values, axis, bit)])
    return values


def sum_low(values, axis, bits):
    values = values.astype(LOW)
    for bit in bits:
        values = (values.astype(F32) + swap(values, axis, bit).astype(F32)).astype(LOW)
    return values


def sum_exact(values, axis, bits):
    for bit in bits:
        values = values + swap(values, axis, bit)
    return values


def tile_active(bounds, block, tile):
    return (bounds[2, tile] <= bounds[1, block]) & (bounds[3, tile] >= bounds[0, block])


def attend_block(block, queries, keys, value_ts, q_ids, k_ids, bounds, mixed, row, out_row, logs, scratch):
    scores, peak, total, acc = scratch
    count = queries.shape[0] // 2
    heads = queries.shape[1] // HEAD
    query_rows = queries[row : row + count, :]
    ids = q_ids[:, block * count : (block + 1) * count]
    peak[...] = jnp.full(peak.shape, masked_score, F32)
    total[...] = jnp.zeros(total.shape, F32)
    acc[...] = jnp.zeros(acc.shape, F32)
    for tile in range(4):
        inner = (tile % 2) * count

        @pl.when(tile_active(bounds, block, tile))
        def _(tile=tile, inner=inner):
            allowed = k_ids[tile * count : (tile + 1) * count, :] == ids
            for h in range(heads):
                cols = slice(h * HEAD, (h + 1) * HEAD)
                part = dot_last(keys[tile // 2][inner : inner + count, cols], query_rows[:, cols])
                part = jnp.where(allowed, part, masked_score)
                scores[h, tile] = part
                peak[h : h + 1, :] = jnp.maximum(
                    peak[h : h + 1, :], jnp.max(part, axis=0, keepdims=True)
                )

    for tile in range(4):
        inner = (tile % 2) * count

        @pl.when(tile_active(bounds, block, tile))
        def _(tile=tile, inner=inner):
            for h in range(heads):
                weights = jnp.exp2((scores[h, tile] - peak[h : h + 1, :]) * exp2_scale)
                total[h : h + 1, :] += jnp.sum(weights, axis=0, keepdims=True)
                acc[h] += dot(
                    value_ts[tile // 2][h * HEAD : (h + 1) * HEAD, inner : inner + count],
                    weights.astype(LOW),
                )

    for h in range(heads):
        sums = total[h : h + 1, :]
        mixed[out_row : out_row + count, h * HEAD : (h + 1) * HEAD] = (acc[h] / sums).T.astype(LOW)
        logs[h : h + 1, out_row : out_row + count] = peak[h : h + 1, :] * exp2_scale + jnp.log2(sums)


def attend_scratch(count, heads):
    return [
        pltpu.VMEM((heads, 4, count, count), F32),
        pltpu.VMEM((8, count), F32),
        pltpu.VMEM((8, count), F32),
        pltpu.VMEM((heads, HEAD, count), F32),
    ]


def project_pair(blocks, weights, norm=None):
    count, width = blocks[0].shape[0], weights[0].shape[1]
    dim = blocks[0].shape[1]
    outs = [shape((2 * count, width), LOW) for w in weights] + [shape((width, 2 * count), LOW)] * 2
    ins = list(blocks) + list(weights)
    if norm is not None:
        outs.append(shape((2 * count, dim), LOW))
        ins += list(norm[:2])
    n_weights = len(weights)

    def body(need, emit, *refs):
        rows, ws = refs[:2], refs[2 : 2 + n_weights]
        res = refs[len(ins) :]
        if norm is not None:
            norm_into(rows, refs[2 + n_weights], refs[3 + n_weights], norm[2], res[-1])
            rows = [res[-1].at[:count], res[-1].at[count:]]
        need(0)
        project_into(rows, ws, res)

    return local_kernel(
        body, "project_pair", ins, outs, cold=[range(2, 2 + n_weights)], cold_outs=range(len(outs))
    )


def norm_into(blocks, gain, offset, index, out):
    count = blocks[0].shape[0]
    at = slice(index, index + 1)
    for b in range(2):
        rows = layer_norm(blocks[b][...].astype(F32), gain[at, :], offset[at, :])
        out[b * count : (b + 1) * count, :] = rows.astype(LOW)


def project_into(blocks, weights, res):
    count = blocks[0].shape[0]
    for i, weight in enumerate(weights):
        for b in range(2):
            part = dot(blocks[b][...], weight[...])
            res[i][b * count : (b + 1) * count, :] = part.astype(LOW)
            if i < 2:
                res[len(weights) + i][:, b * count : (b + 1) * count] = part.T.astype(LOW)


def attend_first(far, across, weights, queries_far, near_set, out_weight, ids, norm=None):
    count, dim = far.shape
    width = out_weight.shape[1]
    heads = width // HEAD
    with_query = len(weights) == 3
    q_ids, k_ids, bounds = ids
    n_weights = len(weights)
    first = [far, across, *weights, *(norm[:2] if norm else ())]
    second = [near_set[0], near_set[2], near_set[3], out_weight, q_ids, k_ids]
    if not with_query:
        second.append(queries_far)
    n_first, n_all = len(first), len(first) + len(second)
    ins = first + second + [bounds]
    pair = shape((2 * count, width), LOW)
    turned = shape((width, 2 * count), LOW)
    outs = [pair] * n_weights + [turned, turned]
    if norm is not None:
        outs.append(shape((2 * count, dim), LOW))
    n_project = len(outs)
    outs += [pair, shape((8, 2 * count)), shape((2 * count, dim), LOW)]

    def body(need, emit, *refs):
        res, scratch = refs[len(ins) : len(ins) + len(outs)], refs[len(ins) + len(outs) :]
        rows, ws = refs[:2], refs[2 : 2 + n_weights]
        near_keys, near_values, near_queries, wo, qi, ki = refs[n_first : n_first + 6]
        bnd = refs[n_all]
        if norm is not None:
            norm_into(rows, refs[2 + n_weights], refs[3 + n_weights], norm[2], res[n_project - 1])
            rows = [res[n_project - 1].at[:count], res[n_project - 1].at[count:]]
        need(0)
        project_into(rows, ws, res)
        emit(*res[:n_project])
        need(1)
        far_queries = res[2] if with_query else refs[n_first + 6]
        mixed, logs, hop = res[n_project:]
        for place, (block, source) in enumerate(((3, far_queries), (1, near_queries))):
            attend_block(
                block, source, (near_keys, res[0]), (near_values, res[n_weights + 1]),
                qi, ki, bnd, mixed, (block % 2) * count, place * count, logs, scratch,
            )
            rows_of_mixed = mixed[place * count : (place + 1) * count, :]
            hop[place * count : (place + 1) * count, :] = dot_last(rows_of_mixed, wo[...]).astype(LOW)

    return local_kernel(
        body, "attend_first", ins, outs, attend_scratch(count, heads), smem=(n_all,),
        cold=[range(2, 2 + n_weights), range(n_first, n_all)], cold_outs=range(n_project + 2),
    )


def attend_one(block, queries, near_set, far_set, out_weight, ids, after):
    width = out_weight.shape[1]
    heads = width // HEAD
    count = queries.shape[0] // 2
    dim = out_weight.shape[0]
    q_ids, k_ids, bounds = ids
    ins = [queries, near_set[0], far_set[0], near_set[1], far_set[1], out_weight, q_ids, k_ids, bounds]
    outs = [shape((count, width), LOW), shape((8, count)), shape((count, dim))]

    def body(need, emit, q, k0, k1, v0, v1, wo, qi, ki, bnd, mixed, logs, part, *scratch):
        need(0)
        attend_block(block, q, (k0, k1), (v0, v1), qi, ki, bnd, mixed, 0, 0, logs, scratch)
        part[...] = dot_last(mixed[...], wo[...])

    return local_kernel(
        body, "attend_one", ins, outs, attend_scratch(count, heads), smem=(8,),
        cold=[range(8)], cold_outs=(0, 1), after=after,
    )


def back_block(block, row, grads, queries, logs, keys, key_ts, values, q_ids, k_ids, bounds,
               query_grads, key_acc, value_acc, scratch):
    probs, grad_probs, inner_sum, acc = scratch
    count = queries.shape[0] // 2
    heads = queries.shape[1] // HEAD
    query_rows = queries[row : row + count, :]
    ids = q_ids[:, block * count : (block + 1) * count]
    inner_sum[...] = jnp.zeros(inner_sum.shape, F32)
    acc[...] = jnp.zeros(acc.shape, F32)
    for tile in range(4):
        inner = (tile % 2) * count

        @pl.when(tile_active(bounds, block, tile))
        def _(tile=tile, inner=inner):
            allowed = k_ids[tile * count : (tile + 1) * count, :] == ids
            for h in range(heads):
                cols = slice(h * HEAD, (h + 1) * HEAD)
                part = dot_last(keys[tile // 2][inner : inner + count, cols], query_rows[:, cols])
                exact = jnp.where(
                    allowed,
                    jnp.exp2(part * exp2_scale - logs[0][h : h + 1, logs[1] : logs[1] + count]),
                    0.0,
                )
                pulled = dot_last(values[tile // 2][inner : inner + count, cols], grads[:, cols])
                probs[h, tile] = exact
                grad_probs[h, tile] = pulled
                inner_sum[h : h + 1, :] += jnp.sum(exact * pulled, axis=0, keepdims=True)
                value_acc[tile * count : (tile + 1) * count, cols] += dot(
                    exact.astype(LOW), grads[:, cols]
                )

    for tile in range(4):
        inner = (tile % 2) * count

        @pl.when(tile_active(bounds, block, tile))
        def _(tile=tile, inner=inner):
            for h in range(heads):
                cols = slice(h * HEAD, (h + 1) * HEAD)
                score_grads = (
                    probs[h, tile] * (grad_probs[h, tile] - inner_sum[h : h + 1, :])
                ).astype(LOW)
                key_acc[tile * count : (tile + 1) * count, cols] += dot(
                    score_grads, query_rows[:, cols]
                )
                acc[h] += dot(key_ts[tile // 2][cols, inner : inner + count], score_grads)

    for h in range(heads):
        query_grads[row : row + count, h * HEAD : (h + 1) * HEAD] = (
            (acc[h] * score_scale).T.astype(LOW)
        )


def back_scratch(count, heads):
    return [
        pltpu.VMEM((heads, 4, count, count), F32),
        pltpu.VMEM((heads, 4, count, count), F32),
        pltpu.VMEM((8, count), F32),
        pltpu.VMEM((heads, HEAD, count), F32),
    ]


def back_near(grads, out_weight, queries, logs, kept, ids):
    count = queries.shape[0] // 2
    width = queries.shape[1]
    q_ids, k_ids, bounds = ids
    ins = [*grads, out_weight, queries, *logs, *kept, q_ids, k_ids, bounds]
    outs = [shape((2 * count, width), LOW), shape((4 * count, width)), shape((4 * count, width))]

    def body(need, emit, g0, g1, wo, q, lg, lo, k0, k1, t0, t1, v0, v1, qi, ki, bnd, dq, dk, dv, *scratch):
        need(0)
        dk[...] = jnp.zeros(dk.shape, F32)
        dv[...] = jnp.zeros(dv.shape, F32)
        for b, g in enumerate((g0, g1)):
            mixed_grads = dot(g[...], wo[...]).astype(LOW)
            logs_at = (lg, count) if b else (lo, 0)
            back_block(b, b * count, mixed_grads, q, logs_at, (k0, k1), (t0, t1), (v0, v1), qi, ki, bnd,
                       dq, dk, dv, scratch)

    return local_kernel(body, "back_near", ins, outs, back_scratch(count, width // HEAD), smem=(14,),
        cold=[range(2, 14)], cold_outs=(0,),
    )


def back_far(grads, out_weight, queries, logs, kept, ids, sums, weights, after=()):
    count = queries.shape[0] // 2
    width = queries.shape[1]
    dim = out_weight.shape[0]
    q_ids, k_ids, bounds = ids
    ins = [*grads, out_weight, queries, *logs, *kept, q_ids, k_ids, bounds, *sums, *weights]
    whole = shape((4 * count, width), LOW)
    outs = [shape((2 * count, width), LOW), whole, whole, shape((count, dim)), shape((count, dim), LOW)]

    def body(need, emit, *refs):
        g0, g1, wo, q, lg, lo, k0, k1, t0, t1, v0, v1, qi, ki, bnd, dk_in, dv_in = refs[:17]
        ws = refs[17 : 17 + len(weights)]
        dq, dk, dv, far_out, across_out, key_acc, value_acc, *scratch = refs[17 + len(weights) :]
        need(0)
        key_acc[...] = dk_in[...]
        value_acc[...] = dv_in[...]
        for b, g in enumerate((g0, g1)):
            mixed_grads = dot(g[...], wo[...]).astype(LOW)
            logs_at = (lg, 0) if b else (lo, 0)
            back_block(2 + b, b * count, mixed_grads, q, logs_at, (k0, k1), (t0, t1), (v0, v1), qi, ki, bnd,
                       dq, key_acc, value_acc, scratch)
        dk[...] = (key_acc[...] * score_scale).astype(LOW)
        dv[...] = value_acc[...].astype(LOW)
        need(1)
        for b in (1, 0):
            rows = slice((2 + b) * count, (3 + b) * count)
            part = dot_last(dk[rows, :], ws[0][...]) + dot_last(dv[rows, :], ws[1][...])
            if len(ws) == 3:
                part = part + dot_last(dq[b * count : (b + 1) * count, :], ws[2][...])
            if b:
                across_out[...] = part.astype(LOW)
            else:
                far_out[...] = part

    scratch = [pltpu.VMEM((4 * count, width), F32)] * 2 + back_scratch(count, width // HEAD)
    return local_kernel(
        body, "back_far", ins, outs, scratch, smem=(14,),
        cold=[range(2, 14), range(17, 17 + len(weights))], after=after,
    )


def pull_near(pairs, after):
    dim = pairs[0][1].shape[0]
    count = pairs[0][2]
    ins = [p[0] for p in pairs] + [p[1] for p in pairs]
    outs = [shape((count, dim)), shape((count, dim), LOW)]

    def body(need, emit, *refs):
        n = len(pairs)
        need(0)
        own_out, near_out = refs[2 * n :]
        for b in range(2):
            part = None
            for i in range(n):
                term = dot_last(refs[i][b * count : (b + 1) * count, :], refs[n + i][...])
                part = term if part is None else part + term
            if b:
                near_out[...] = part.astype(LOW)
            else:
                own_out[...] = part

    return local_kernel(
        body, "pull_near", ins, outs, cold=[range(len(pairs), 2 * len(pairs))], after=after
    )


def pull_active(grads, down_proj, after):
    count, units = grads[0].shape[0], down_proj.shape[1]

    def body(need, emit, g0, g1, down, out):
        need(0)
        for b, g in enumerate((g0, g1)):
            out[b * count : (b + 1) * count, :] = dot(g[...], down[...]).astype(LOW)

    return local_kernel(
        body, "pull_active", [*grads, down_proj], [shape((2 * count, units), LOW)], cold=[range(3)], after=after
    )[0]


def mlp_pair(rows, grads, up_proj, down_proj, after=(), pulled=None):
    count, dim = rows[0].shape
    units = up_proj.shape[1]
    step = 256
    outs = [
        shape((2 * count, units), LOW), shape((2 * count, units), LOW),
        shape((count, dim)), shape((count, dim), LOW),
    ]
    ready = pulled is not None
    ins = [*rows, up_proj, pulled] if ready else [*rows, up_proj, down_proj, *grads]

    def body(need, emit, x0, x1, up, *refs):
        active, grad_hidden, first_out, second_out = refs[-4:]
        need(0)
        for b, x in enumerate((x0, x1)):
            band = slice(b * count, (b + 1) * count)
            for at in range(0, units, step):
                hidden = dot(x[...], up[:, at : at + step])
                if ready:
                    back = refs[0][band, at : at + step].astype(F32)
                else:
                    back = dot(refs[1 + b][...], refs[0][:, at : at + step])
                square = hidden * hidden
                bent = jnp.tanh(gelu_coeff * (hidden + gelu_cubic * hidden * square))
                half = 0.5 * (1.0 + bent)
                slope = half + 0.5 * hidden * (1.0 - bent * bent) * (
                    gelu_coeff * (1.0 + 3.0 * gelu_cubic * square)
                )
                active[band, at : at + step] = (hidden * half).astype(LOW)
                grad_hidden[band, at : at + step] = (back * slope).astype(LOW)
        emit(active, grad_hidden)
        for b in (1, 0):
            part = dot_last(grad_hidden[b * count : (b + 1) * count, :], up[...])
            if b:
                second_out[...] = part.astype(LOW)
            else:
                first_out[...] = part

    return local_kernel(
        body, "mlp_pair", ins, outs, cold=[[2] if ready else range(2, 6)], cold_outs=(0, 1), after=after,
    )


def pull_four(near_rows, far_rows, weight, after):
    count, dim = near_rows.shape[0] // 2, weight.shape[0]
    outs = [shape((count, dim)), shape((count, dim)), shape((2 * count, dim), LOW)]

    def body(need, emit, x, y, w, own_out, far_out, hop):
        need(0)
        own_out[...] = dot_last(x[:count, :], w[...])
        far_out[...] = dot_last(y[:count, :], w[...])
        hop[:count, :] = dot_last(y[count:, :], w[...]).astype(LOW)
        hop[count:, :] = dot_last(x[count:, :], w[...]).astype(LOW)

    return local_kernel(
        body, "pull_four", [near_rows, far_rows, weight], outs, cold=[range(3)], cold_outs=(0, 1, 2), after=after
    )


def norm_rows(terms, gain, offset, index):
    kept = terms[0]

    def body(need, emit, k, p, n, f, g, o, after, normed):
        total = p[...] + n[n.shape[0] - p.shape[0] :, :].astype(F32) + f[...].astype(F32)
        need(0)
        total = total + k[...]
        after[...] = total
        emit(after)
        normed[...] = layer_norm(total, g[index : index + 1, :], o[index : index + 1, :]).astype(LOW)

    return local_kernel(
        body, "norm_rows", [*terms, gain, offset], [shape(kept.shape), shape(kept.shape, LOW)],
        cold=[[0]], cold_outs=(0,),
    )


def norm_rows_back(values, gain, index, terms, grads, after=(), inside=False):
    added = grads is not None

    def body(need, emit, v, g, p, n, f, *refs):
        if inside:
            need(0)
        total = p[...] + n[...].astype(F32) + f[...].astype(F32)
        if not inside:
            need(0)
        back, gain_sum, offset_sum = layer_norm_back(v[...].astype(F32), g[index : index + 1, :], total)
        if added:
            back = back + refs[0][...].astype(F32)
            out, sums = refs[1:]
            sums[0:1, :] = gain_sum
            sums[1:2, :] = offset_sum
        else:
            out = refs[0]
        out[...] = back.astype(out.dtype)

    ins = [values, gain, *terms]
    outs = [shape(values.shape, LOW if added else F32)]
    if added:
        ins.append(grads)
        outs.append(shape((2, values.shape[1])))
    return local_kernel(
        body, "norm_back", ins, outs, cold=[[0, 2, 5] if inside else [0, 5] if added else [0]], cold_outs=() if added else (0,),
        vmem=VMEM_LARGE if inside else VMEM_BYTES, after=after,
    )


def dp_orders():
    bits = axis_bits("dp")
    return [bits, bits[1:2] + bits[:1] + bits[2:]]


def outer_sums(sets, after, parts_sent=1):
    n_dp = lax.axis_size("dp")
    place = lax.axis_index("dp")
    ins, plans, places, outs = [], [], [], []
    seen = {}

    def take(array):
        if id(array) not in seen:
            seen[id(array)] = len(ins)
            ins.append(array)
        return seen[id(array)]

    for groups, bits in zip(sets, dp_orders()):
        plan = []
        for blocks, parts in groups:
            terms = []
            if len(parts) == 3:
                count = blocks[0].shape[0]
                terms = [
                    (take(blocks[0]), take(parts[0]), 0, count),
                    (take(blocks[1][1]), take(parts[1]), 0, count),
                    (take(blocks[1][0]), take(parts[1]), count, count),
                    (take(blocks[2]), take(parts[2]), 0, count),
                ]
            else:
                per = len(blocks) // len(parts)
                for b, block in enumerate(blocks):
                    count = block.shape[0]
                    terms.append((take(block), take(parts[b // per]), (b % per) * count, count))
            plan.append((terms, parts[0].shape[1]))
        plans.append(plan)
        dim = groups[0][0][0].shape[1]
        chunk = dim // n_dp
        aligned = chunk % 128 == 0
        steps = dim // 128
        width = sum(p[1] for p in plan)
        if aligned:
            repeat = chunk // 128
            spots = (jnp.asarray(halving_order(bits)) ^ place)[:, None] * repeat
            spots = (spots + jnp.arange(repeat, dtype=jnp.int32)[None, :]).reshape(steps)
        else:
            spots = jnp.arange(steps, dtype=jnp.int32)
        places.append(spots.astype(jnp.int32))
        outs += [shape((dim // 2, width))] + [shape((dim // 2 // parts_sent, width), LOW)] * parts_sent
    ins.append(jnp.stack(places))

    def body(need, emit, *refs):
        need(0)
        spots = refs[len(ins) - 1]
        results = refs[len(ins) :]

        def one(order, index, target, base):
            at = pl.multiple_of(spots[order, base + index] * 128, 128)
            column = 0
            for terms, right_width in plans[order]:
                total = None
                for left, right, row, count in terms:
                    term = dot_first(refs[left][:, pl.ds(at, 128)], refs[right][row : row + count, :])
                    total = term if total is None else total + term
                target[pl.ds(pl.multiple_of(index * 128, 128), 128), column : column + right_width] = (
                    total.astype(target.dtype)
                )
                column += right_width

        per = 1 + parts_sent
        half = steps // 2
        for piece in [*range(1, per), 0]:
            for order in range(len(plans)):
                run = half if piece == 0 else half // parts_sent
                base = 0 if piece == 0 else half + (piece - 1) * run

                @pl.loop(0, run)
                def _(index, target=results[per * order + piece], order=order, base=base):
                    one(order, index, target, base)

    results = local_kernel(
        body, "outer_sums", ins, outs, smem=(len(ins) - 1,), cold=[range(len(ins) - 1)],
        cold_outs=range(len(outs)), vmem=VMEM_LARGE, after=after,
    )
    pairs = []
    for order, bits in enumerate(dp_orders()[: len(plans)]):
        keep, *sent = results[(1 + parts_sent) * order : (1 + parts_sent) * (order + 1)]
        if not aligned:
            whole = jnp.concatenate([keep, *[part.astype(F32) for part in sent]])
            whole = whole.reshape(n_dp, chunk, keep.shape[1])
            whole = whole[jnp.asarray(halving_order(bits)) ^ place].reshape(dim, keep.shape[1])
            keep, whole = whole[: dim // 2], whole[dim // 2 :].astype(LOW)
            sent = [part for part in whole.reshape(parts_sent, dim // 2 // parts_sent, keep.shape[1])]
        pairs.append((keep, *sent))
    return pairs


def outer_whole(groups, after):
    ins = [a for blocks, parts in groups for a in (*blocks, *parts)]
    dim = groups[0][0][0].shape[1]
    width = groups[0][1][0].shape[1]
    step = 256

    def body(need, emit, *refs):
        out = refs[len(ins)]
        for k in range(len(groups)):
            need(k)
            lefts, rights = refs[6 * k : 6 * k + 4], refs[6 * k + 4 : 6 * k + 6]
            count = lefts[0].shape[0]

            @pl.loop(0, dim // step)
            def _(index, k=k, lefts=lefts, rights=rights, count=count):
                at = pl.multiple_of(index * step, step)
                total = None
                for b in range(4):
                    right = rights[b // 2][(b % 2) * count : (b % 2 + 1) * count, :]
                    term = dot_first(lefts[b][:, pl.ds(at, step)], right)
                    total = term if total is None else total + term
                out[pl.ds(at, step), k * width : (k + 1) * width] = total.astype(LOW)

    return local_kernel(
        body, "outer_whole", ins, [shape((dim, width * len(groups)), LOW)],
        cold=[range(6 * k, 6 * k + 6) for k in range(len(groups))], cold_outs=(0,), after=after,
    )[0]


def merge(pairs, last, widths, after=()):
    ins, outs, firsts = [], [], []
    for order, (keep, *came) in enumerate(pairs):
        firsts.append(len(ins))
        ins += [keep, *came]
        rows, width = keep.shape
        if last:
            outs += [shape((rows, w)) for w in widths[order]]
        else:
            outs += [shape((rows // 2, width)), shape((rows // 2, width), LOW)]

    def body(need, emit, *refs):
        results = list(refs[len(ins) :])
        for order in range(len(pairs)):
            keep, got = refs[firsts[order]], refs[firsts[order] + 1]
            if last:
                column = 0
                for w in widths[order]:
                    cols = slice(column, column + w)
                    results.pop(0)[...] = keep[:, cols] + got[:, cols].astype(F32)
                    column += w
            else:
                half = keep.shape[0] // 2
                later = got[half:, :] if len(pairs[order]) == 2 else refs[firsts[order] + 2][...]
                results.pop(0)[...] = keep[:half, :] + got[:half, :].astype(F32)
                results.pop(0)[...] = (keep[half:, :] + later.astype(F32)).astype(LOW)

    results = local_kernel(body, "merge", ins, outs, after=after)
    if last:
        return results
    return [(results[2 * i], results[2 * i + 1]) for i in range(len(pairs))]


def rows_of(source, row_start, row_count):
    return lax.dynamic_slice_in_dim(source, row_start, row_count, 0)


def turn_row(row):
    columns = []
    for at in range(0, row.shape[1], 128):
        columns.append(jnp.broadcast_to(row[:, at : at + 128], (128, 128)).T[:, 0:1])
    return jnp.concatenate(columns, axis=0)


def prepare(latent_row, input_row, member, table, gain, offset, query_weight, images):
    total = latent_row.shape[1]
    count = total // 4
    slots, dim = table.shape
    width = query_weight.shape[1]
    whole = jnp.int32
    outs = [
        shape((1, total), whole), shape((total, 1), whole), shape((total, 1), whole),
        shape((4, 4), whole), shape((4, 4), whole),
        shape((total, slots), LOW), shape((slots, dim), LOW),
        shape((2 * count, width), LOW), shape((2 * count, width), LOW), shape((count, dim)),
    ]

    def body(need, emit, lat, inp, lat_s, inp_s, who, tb, g, o, wq,
             lat_out, lat_col, inp_col, cross_ends, self_ends, pick, normed, near_q, far_q, start):
        order = [who[0, 0] ^ k for k in range(4)]
        for k in range(4):
            first = order[k] * count
            last = first + count - 1
            cross_ends[0, k] = lat_s[0, first]
            cross_ends[1, k] = lat_s[0, last]
            cross_ends[2, k] = inp_s[0, first]
            cross_ends[3, k] = inp_s[0, last]
            for r in range(2):
                self_ends[2 * r, k] = lat_s[0, first]
                self_ends[2 * r + 1, k] = lat_s[0, last]
        starts = [pl.multiple_of(at * count, count) for at in order]
        lat_rel = jnp.concatenate([lat[:, pl.ds(at, count)] for at in starts], axis=1)
        inp_rel = jnp.concatenate([inp[:, pl.ds(at, count)] for at in starts], axis=1)
        lane = lax.broadcasted_iota(whole, (1, count), 1)
        place = jnp.concatenate([lane + at for at in starts], axis=1)
        lat_all = lat[...]
        for image in range(images):
            before = jnp.sum((lat_all < image).astype(F32), axis=1, keepdims=True).astype(whole)
            place = place - jnp.where(lat_rel == image, before, 0)
        lat_out[...] = lat_rel
        lat_col[...] = turn_row(lat_rel)
        inp_col[...] = turn_row(inp_rel)
        slot = turn_row(place)
        slot_lane = lax.broadcasted_iota(whole, (total, slots), 1)
        pick[...] = jnp.where(slot == slot_lane, 1.0, 0.0).astype(LOW)
        normed[...] = layer_norm(tb[...].astype(F32), g[0:1, :], o[0:1, :]).astype(LOW)
        start[...] = dot(pick[:count, :], tb[...])
        need(0)
        queries = dot(normed[...], wq[...]).astype(LOW)
        near_q[...] = dot(pick[: 2 * count, :], queries).astype(LOW)
        far_q[...] = dot(pick[2 * count :, :], queries).astype(LOW)

    return local_kernel(
        body, "prepare",
        [latent_row, input_row, latent_row, input_row, member, table, gain, offset, query_weight],
        outs, smem=(2, 3, 4), smem_outs=(3, 4), cold=[[8]],
    )


def slot_stack(pick, query_pairs, raw_blocks, parts, grads, sums, member, after):
    count, dim = raw_blocks[0].shape
    slots, width = pick.shape[1], query_pairs[0].shape[1]
    cut = dim // (2 * width)
    ins = [pick, *query_pairs, *raw_blocks, *parts, *grads, *sums, member]

    def body(need, emit, pk, q0, q1, x0, x1, x2, x3, p0, p1, p2, p3, r0, r1, r2, r3, s0, s1, who, out):
        need(0)
        total = dot_first(pk[: 2 * count, :], q0[...]) + dot_first(pk[2 * count :, :], q1[...])
        out[:slots, :width] = total.astype(LOW)
        at = pl.multiple_of(who[0, 0] * width, width)
        total = None
        for b, r in enumerate((r0, r1, r2, r3)):
            term = dot_first(pk[b * count : (b + 1) * count, :], r[:, pl.ds(at, width)])
            total = term if total is None else total + term
        out[:slots, width:] = total.astype(LOW)
        gain_sum = offset_sum = None
        for x, p in ((x0, p0), (x1, p1), (x2, p2), (x3, p3)):
            values = x[...].astype(F32)
            centred = values - jnp.mean(values, axis=-1, keepdims=True)
            spread = jnp.mean(centred * centred, axis=-1, keepdims=True)
            back = p[...].astype(F32)
            gains = jnp.sum(back * (centred * lax.rsqrt(spread + norm_eps)), axis=0, keepdims=True)
            offsets = jnp.sum(back, axis=0, keepdims=True)
            gain_sum = gains if gain_sum is None else gain_sum + gains
            offset_sum = offsets if offset_sum is None else offset_sum + offsets
        rows = [gain_sum, offset_sum, s0[0:1, :], s0[1:2, :], s1[0:1, :], s1[1:2, :]]
        rows += [jnp.zeros((1, dim), F32)] * 2
        whole = jnp.concatenate(rows, axis=0)
        for q in range(cut):
            out[slots + 8 * q : slots + 8 * (q + 1), :] = (
                whole[:, 2 * q * width : 2 * (q + 1) * width].astype(LOW)
            )

    return local_kernel(
        body, "slot_stack", ins, [shape((slots + 8 * cut, 2 * width), LOW)],
        smem=(len(ins) - 1,), cold=[range(7)], after=after,
    )[0]


def table_end(stacks, weights, gain, table, member):
    slots, dim = table.shape
    width = stacks[0].shape[1] // 2
    cut = dim // (2 * width)
    ins = [*stacks, *weights, gain, table, member]

    def body(need, emit, *refs):
        st, ws = refs[:4], refs[4:8]
        g, tb, who = refs[8:11]
        table_out, gain_out, offset_out, last_out, residual, grads, weight = refs[11:]
        need(0)
        for k in range(4):
            at = pl.multiple_of((who[0, 0] ^ k) * width, width)
            grads[:, pl.ds(at, width)] = st[k][:slots, :width]
            residual[:, pl.ds(at, width)] = st[k][:slots, width:]
            weight[:, pl.ds(at, width)] = ws[k][...]
        total = dot_last(grads[...], weight[...])
        back, gain_sum, offset_sum = layer_norm_back(tb[...].astype(F32), g[0:1, :], total)
        table_out[...] = residual[...].astype(F32) + back
        small = [st[k][slots:, :].astype(F32) for k in range(4)]
        small = (small[0] + small[1]) + (small[2] + small[3])
        small = jnp.concatenate([small[8 * q : 8 * (q + 1), :] for q in range(cut)], axis=1)
        gain_out[0:1, :] = gain_sum
        offset_out[0:1, :] = offset_sum
        for k in range(3):
            gain_out[k + 1 : k + 2, :] = small[2 * k : 2 * k + 1, :]
            target = last_out if k == 2 else offset_out
            at = 0 if k == 2 else k + 1
            target[at : at + 1, :] = small[2 * k + 1 : 2 * k + 2, :]

    outs = [shape((slots, dim)), shape((4, dim)), shape((3, dim)), shape((1, dim))]
    return local_kernel(
        body, "table_end", ins, outs,
        [pltpu.VMEM((slots, dim), LOW), pltpu.VMEM((slots, dim), LOW), pltpu.VMEM((dim, dim), LOW)],
        smem=(10,), cold=[range(4, 8)],
    )


def body(
    block_input,
    latent_table,
    latent_segments,
    input_segments,
    ln_gain,
    ln_bias,
    cross_query,
    cross_key,
    cross_value,
    cross_out,
    self_query,
    self_key,
    self_value,
    self_out,
    up_proj,
    down_proj,
    out_grad,
):
    count, dim = block_input.shape
    member = lax.axis_index("mp")
    n_mp, n_dp = lax.axis_size("mp"), lax.axis_size("dp")
    slots = latent_table.shape[0]
    mp_bits, dp_bits = axis_bits("mp"), axis_bits("dp")
    dp_steps = len(dp_bits)

    far_raw = swap(block_input, "mp", 2)
    near_raw = swap(block_input, "mp", 1)
    near_out = swap(out_grad, "mp", 1)
    half = count // 2
    near_raw, out_1, out_2 = lax.optimization_barrier((near_raw, out_grad[:half], out_grad[half:]))

    who = member.astype(jnp.int32).reshape(1, 1)
    (latent_rel, latent_col, input_col, cross_ends, self_ends, table_pick, normed_table, queries_near,
     queries_far, start_rows) = prepare(
        latent_segments, input_segments, who, latent_table, ln_gain, ln_bias, cross_query, images
    )
    cross_ids = (latent_rel, input_col, cross_ends)
    self_ids = (latent_rel, latent_col, self_ends)

    input_norm = (ln_gain, ln_bias, 1)
    keys_near, values_near, key_ts_near, value_ts_near, normed_near = project_pair(
        (block_input, near_raw), (cross_key, cross_value), input_norm
    )
    far_raw = tie(far_raw, keys_near, queries_far)
    across_raw = swap(far_raw, "mp", 1)
    far_out_1 = swap(tie(out_1, far_raw), "mp", 2)
    (keys_far, values_far, key_ts_far, value_ts_far, normed_far, mixed_two, logs_two, hop) = attend_first(
        far_raw, across_raw, (cross_key, cross_value), queries_far,
        (keys_near, key_ts_near, value_ts_near, queries_near), cross_out, cross_ids, input_norm,
    )
    got = swap(tie(hop, far_out_1), "mp", 1)
    key_values = ((keys_near, value_ts_near), (keys_far, value_ts_far))
    mixed_far, logs_far, part_far = attend_one(2, queries_far, *key_values, cross_out, cross_ids, ())
    got_far, sent = send_far(part_far, got)
    mixed_own, logs_own, part_own = attend_one(0, queries_near, *key_values, cross_out, cross_ids, (sent,))
    cross_kept = (keys_near, keys_far, key_ts_near, key_ts_far, values_near, values_far)
    cross_queries_set = (queries_near, queries_far)
    cross_logs = ((logs_two, logs_own), (logs_two, logs_far))
    cross_mixed = (mixed_own, mixed_two, mixed_far)
    after_cross, normed_self = norm_rows((start_rows, part_own, got, got_far), ln_gain, ln_bias, 2)

    self_weights = (self_key, self_value, self_query)
    far_self = swap(normed_self, "mp", 2)
    near_self = swap(normed_self, "mp", 1)
    keys_near, values_near, queries_near, key_ts_near, value_ts_near = project_pair(
        (normed_self, near_self), self_weights
    )
    far_self = tie(far_self, keys_near)
    across_self = swap(far_self, "mp", 1)
    far_out_2 = swap(tie(out_2, far_self), "mp", 2)
    (keys_far, values_far, queries_far, key_ts_far, value_ts_far, mixed_two, logs_two, hop) = attend_first(
        far_self, across_self, self_weights, None,
        (keys_near, key_ts_near, value_ts_near, queries_near), self_out, self_ids,
    )
    got = swap(tie(hop, far_out_2), "mp", 1)
    key_values = ((keys_near, value_ts_near), (keys_far, value_ts_far))
    mixed_far, logs_far, part_far = attend_one(2, queries_far, *key_values, self_out, self_ids, ())
    got_far, sent = send_far(part_far, got)
    mixed_own, logs_own, part_own = attend_one(0, queries_near, *key_values, self_out, self_ids, (sent,))
    far_out = tie(jnp.concatenate([far_out_1, far_out_2]), part_own)
    across_out = swap(far_out, "mp", 1)
    self_kept = (keys_near, keys_far, key_ts_near, key_ts_far, values_near, values_far)
    self_queries_set = (queries_near, queries_far)
    self_logs = ((logs_two, logs_own), (logs_two, logs_far))
    self_mixed = (mixed_own, mixed_two, mixed_far)
    after_self, normed_mlp = norm_rows((after_cross, part_own, got, got_far), ln_gain, ln_bias, 3)

    far_mlp = swap(normed_mlp, "mp", 2)
    near_mlp = swap(normed_mlp, "mp", 1)
    active_near, hidden_near, part_own, part_near = mlp_pair(
        (normed_mlp, near_mlp), (out_grad, near_out), up_proj, down_proj, (across_out,)
    )
    pulled_far = pull_active((far_out, across_out), down_proj, (part_near,))
    far_mlp = tie(far_mlp, pulled_far)
    across_mlp = swap(far_mlp, "mp", 1)
    active_far, hidden_far, part_far, part_across = mlp_pair(
        (far_mlp, across_mlp), None, up_proj, None, (), pulled_far
    )
    got = swap(part_across, "mp", 1)
    got_far, sent = send_far(part_far, got)
    got_near = swap(part_near, "mp", 1)
    mlp_grads = outer_whole(
        [
            ((normed_mlp, near_mlp, far_mlp, across_mlp), (hidden_near, hidden_far)),
            ((out_grad, near_out, far_out, across_out), (active_near, active_far)),
        ],
        (sent, got_near),
    )
    mlp_sum = lax.psum_scatter(tie(mlp_grads, got_far), "dp", scatter_dimension=0, tiled=True)
    dy_own, mlp_sums = norm_rows_back(
        after_self, ln_gain, 3, (part_own, got_near, got_far), out_grad,
        (mlp_grads,), True,
    )

    far_dy = swap(dy_own, "mp", 2)
    near_dy = swap(dy_own, "mp", 1)

    query_near, key_sum, value_sum = back_near(
        (dy_own, near_dy), self_out, self_queries_set[0], self_logs[0], self_kept, self_ids
    )
    far_dy = tie(far_dy, key_sum)
    across_dy = swap(far_dy, "mp", 1)
    query_far, key_grads, value_grads, part_far, part_across = back_far(
        (far_dy, across_dy), self_out, self_queries_set[1], self_logs[1], self_kept, self_ids,
        (key_sum, value_sum), self_weights,
    )
    got = swap(part_across, "mp", 1)
    part_own, part_near = pull_near(
        [(key_grads, self_key, count), (value_grads, self_value, count), (query_near, self_query, count)], ()
    )
    got_far, sent = send_far(part_far, got, part_own)
    got_near = swap(part_near, "mp", 1)
    normed_blocks = (normed_self, near_self, far_self, across_self)
    self_pairs = outer_sums(
        [
            [
                (normed_blocks, (query_near, query_far)), (normed_blocks, (key_grads,)),
                (normed_blocks, (value_grads,)), ((dy_own, (near_dy, across_dy), far_dy), self_mixed),
            ],
        ],
        (sent, got_near), 2,
    )
    dy_cross, self_sums = norm_rows_back(
        after_cross, ln_gain, 2, (part_own, got_near, got_far), dy_own,
        (self_pairs[0][1],),
    )

    far_dyc = swap(dy_cross, "mp", 2)
    near_dyc = swap(dy_cross, "mp", 1)
    query_near, key_sum, value_sum = back_near(
        (dy_cross, near_dyc), cross_out, cross_queries_set[0], cross_logs[0], cross_kept, cross_ids
    )
    part_own_out, part_far_out, hop_out = pull_four(active_near, active_far, down_proj, (key_sum,))
    self_half = swap(self_pairs[0][1], "dp", dp_bits[0])
    far_dyc = tie(far_dyc, part_own_out, self_half)
    across_dyc = swap(far_dyc, "mp", 1)
    query_far, key_grads, value_grads, part_far, part_across = back_far(
        (far_dyc, across_dyc), cross_out, cross_queries_set[1], cross_logs[1], cross_kept, cross_ids,
        (key_sum, value_sum), (cross_key, cross_value),
    )
    dyc_blocks = (dy_cross, near_dyc, far_dyc, across_dyc)
    part_own, part_near = pull_near([(key_grads, cross_key, count), (value_grads, cross_value, count)], ())
    got = swap(part_across, "mp", 1)
    got_near = swap(part_near, "mp", 1)
    got_far, sent = send_far(part_far, got, part_own)

    up_width = up_proj.shape[1]
    heads_width = cross_query.shape[1]
    stack = slot_stack(
        table_pick, (query_near, query_far), (block_input, near_raw, far_raw, across_raw),
        (part_own, part_near, part_far, part_across), dyc_blocks, (self_sums, mlp_sums), who,
        (sent,),
    )
    input_blocks = (normed_near, normed_far)
    cross_sets = [
        [
            (input_blocks, (key_grads,)),
            (input_blocks, (value_grads,)),
            ((dy_cross, (near_dyc, across_dyc), far_dyc), cross_mixed),
        ],
    ]
    self_keep, _, self_sent = self_pairs[0]

    def dp_swap(values, step):
        return swap(values, "dp", dp_bits[step])

    def joined(mine, came):
        return (mine.astype(F32) + came.astype(F32)).astype(LOW)

    def halved(keep, *came):
        return merge([(keep, *came)], False, None)[0]

    stack_got, self_got = dp_swap(stack, 0), dp_swap(self_sent, 0)
    ((cross_keep, cross_sent),) = outer_sums(cross_sets, (stack,))
    got_far, got_near, stack, stack_got, self_got, cross_sent, hop_out, query_sent = wait(
        got_far, got_near, stack, stack_got, self_got, cross_sent, hop_out, cross_query
    )
    stack = joined(stack, stack_got)

    self_keep, self_sent = halved(self_keep, self_half, self_got)
    stack_got, self_got, cross_got = dp_swap(stack, 1), dp_swap(self_sent, 1), dp_swap(cross_sent, 0)
    far_query, near_query = swap(query_sent, "mp", 2), swap(query_sent, "mp", 1)
    got_out = swap(hop_out, "mp", 1)
    stack, stack_got, got_out, self_sent, got_far = wait(stack, stack_got, got_out, self_sent, got_far)
    stack = joined(stack, stack_got)
    sent_out = (part_far_out + got_out[:count].astype(F32)).astype(LOW)

    stack_got = dp_swap(stack, 2)
    got_far_out = swap(sent_out, "mp", 2)
    (grad_input,) = norm_rows_back(block_input, ln_gain, 1, (part_own, got_near, got_far), None)
    mlp_parts = [mlp_sum[:, :up_width].astype(F32), mlp_sum[:, up_width:].astype(F32)]
    stack, stack_got, self_got, cross_got, mlp_parts, grad_input = wait(
        stack, stack_got, self_got, cross_got, mlp_parts, grad_input
    )
    stack = joined(stack, stack_got)

    for step in range(3, dp_steps):
        self_keep, self_sent = halved(self_keep, self_got)
        cross_keep, cross_sent = halved(cross_keep, cross_got)
        stack_got, cross_got, self_got = wait(
            dp_swap(stack, step), dp_swap(cross_sent, step - 2), dp_swap(self_sent, step - 1)
        )
        stack = joined(stack, stack_got)

    far_stack, near_stack = swap(stack, "mp", 2), swap(stack, "mp", 1)
    cross_keep, cross_sent = halved(tie(cross_keep, stack), cross_got)
    cross_got = dp_swap(cross_sent, dp_steps - 2)
    self_keep, self_sent = halved(tie(self_keep, cross_sent), self_got)
    self_got = dp_swap(self_sent, dp_steps - 1)
    chunk = dim // n_dp
    own_features = lax.dynamic_slice_in_dim(normed_table, lax.axis_index("dp") * chunk, chunk, 1)
    query_sum = dot_first(own_features, stack[:slots, :heads_width])
    block_output = (
        after_self + part_own_out + got_out[count:].astype(F32) + got_far_out.astype(F32)
    )
    far_stack, cross_got, self_got, far_query, near_query, block_output, query_sum = wait(
        far_stack, cross_got, self_got, far_query, near_query, block_output, query_sum
    )

    across_stack = swap(far_stack, "mp", 1)
    across_query = swap(far_query, "mp", 1)
    cross_keep, cross_sent = halved(cross_keep, cross_got)
    cross_got = dp_swap(cross_sent, dp_steps - 1)
    across_stack, cross_sent = wait(across_stack, cross_sent)
    table_grad, ln_gain_grad, ln_bias_grad, last_bias = table_end(
        (stack, near_stack, far_stack, across_stack),
        (cross_query, near_query, far_query, across_query), ln_gain, latent_table, who,
    )
    cross_keep, self_keep, table_grad = wait(cross_keep, self_keep, table_grad)
    self_pair = merge([(self_keep, self_got)], True, [[heads_width] * 4])
    cross_pair = merge([(cross_keep, cross_got)], True, [[heads_width] * 3])

    return (
        block_output,
        grad_input,
        table_grad,
        ln_gain_grad,
        ln_bias_grad,
        last_bias[0],
        query_sum,
        *cross_pair,
        *self_pair,
        *mlp_parts,
    )


def solution(mesh):
    placed = (
        P(("dp", "mp"), None),
        P(),
        P("dp", None),
        P("dp", None),
        P(),
        P(),
        P(None, "mp"),
        P(None, "mp"),
        P(None, "mp"),
        P(None, "mp"),
        P(None, "mp"),
        P(None, "mp"),
        P(None, "mp"),
        P(None, "mp"),
        P(None, "mp"),
        P(None, "mp"),
        P(("dp", "mp"), None),
    )
    return jax.shard_map(
        body,
        mesh=mesh,
        in_specs=placed,
        out_specs=(
            P(("dp", "mp"), None),
            P(("dp", "mp"), None),
            P(),
            P(),
            P(),
            P(),
            P("dp", "mp"),
            P("dp", "mp"),
            P("dp", "mp"),
            P("dp", "mp"),
            P("dp", "mp"),
            P("dp", "mp"),
            P("dp", "mp"),
            P("dp", "mp"),
            P("dp", "mp"),
            P("dp", "mp"),
        ),
        check_vma=False,
    )
```

```python
import jax
import jax.numpy as jnp
import numpy as np
from jax import lax
from jax.experimental import pallas as pl
from jax.experimental.pallas import tpu as pltpu
from jax.sharding import PartitionSpec as P

HEAD = 128
images = 16
norm_eps = 1e-05
masked_score = -1e30
gelu_coeff = 0.7978845608028654
gelu_cubic = 0.044715
log2_e = 1.4426950408889634
score_scale = HEAD ** (-0.5)
exp2_scale = score_scale * log2_e
LOW = jnp.bfloat16
F32 = jnp.float32
VMEM_BYTES = 32 * 1024 * 1024
VMEM_LARGE = 56 * 1024 * 1024


def layer_norm(values, gain, offset):
    average = jnp.mean(values, axis=-1, keepdims=True)
    centred = values - average
    spread = jnp.mean(centred * centred, axis=-1, keepdims=True)
    return centred * lax.rsqrt(spread + norm_eps) * gain + offset


def layer_norm_back(values, gain, grad):
    average = jnp.mean(values, axis=-1, keepdims=True)
    centred = values - average
    spread = jnp.mean(centred * centred, axis=-1, keepdims=True)
    inverse = lax.rsqrt(spread + norm_eps)
    normal = centred * inverse
    scaled = grad * gain
    inner = jnp.mean(scaled * normal, axis=-1, keepdims=True)
    back = inverse * (scaled - jnp.mean(scaled, axis=-1, keepdims=True) - normal * inner)
    return (
        back,
        jnp.sum(grad * normal, axis=0, keepdims=True),
        jnp.sum(grad, axis=0, keepdims=True),
    )


def dot(left, right):
    return jnp.dot(left, right, preferred_element_type=F32)


def dot_last(left, right):
    return lax.dot_general(left, right, (((1,), (1,)), ((), ())), preferred_element_type=F32)


def dot_first(left, right):
    return lax.dot_general(left, right, (((0,), (0,)), ((), ())), preferred_element_type=F32)


def shape(dims, kind=F32):
    return jax.ShapeDtypeStruct(dims, kind)


def local_kernel(body, name, ins, outs, scratch=(), smem=(), cold=None, cold_outs=(), smem_outs=(), vmem=VMEM_BYTES, after=()):
    if after:
        ins = [tie(ins[0], *after), *ins[1:]]
    n_in, n_out = len(ins), len(outs)
    groups = [list(g) for g in (cold or [])]
    moved = [i for g in groups for i in g]
    held = [pltpu.VMEM(ins[i].shape, ins[i].dtype) for i in moved]
    held += [pltpu.VMEM(outs[o].shape, outs[o].dtype) for o in cold_outs]
    sems = []
    if moved:
        sems.append(pltpu.SemaphoreType.DMA((len(moved),)))
    if cold_outs:
        sems.append(pltpu.SemaphoreType.DMA((len(cold_outs),)))

    def run(*refs):
        inside = list(refs[:n_in])
        results = list(refs[n_in : n_in + n_out])
        rest = list(refs[n_in + n_out :])
        buffers, rest = rest[: len(held)], rest[len(held) :]
        in_sem = rest.pop(0) if moved else None
        out_sem = rest.pop(0) if cold_outs else None
        copies, waited, sent = {}, set(), {}
        for place, i in enumerate(moved):
            copies[i] = pltpu.make_async_copy(refs[i], buffers[place], in_sem.at[place])
            copies[i].start()
            inside[i] = buffers[place]
        made = list(results)
        for place, o in enumerate(cold_outs):
            made[o] = buffers[len(moved) + place]

        def need(*which):
            for k in which:
                for i in groups[k]:
                    copies[i].wait()
                waited.add(k)

        def emit(*given):
            for ref in given:
                for place, o in enumerate(cold_outs):
                    if made[o] is ref and o not in sent:
                        sent[o] = pltpu.make_async_copy(made[o], results[o], out_sem.at[place])
                        sent[o].start()

        body(need, emit, *inside, *made, *rest)
        for k in range(len(groups)):
            if k not in waited:
                need(k)
        emit(*[made[o] for o in cold_outs])
        for o in cold_outs:
            sent[o].wait()

    spaces = [pltpu.VMEM] * n_in
    for i in smem:
        spaces[i] = pltpu.SMEM
    for i in moved:
        spaces[i] = pl.ANY
    return pl.pallas_call(
        run,
        name=name,
        out_shape=list(outs),
        in_specs=[pl.BlockSpec(memory_space=s) for s in spaces],
        out_specs=[
            pl.BlockSpec(memory_space=pl.ANY if o in cold_outs else pltpu.SMEM if o in smem_outs else pltpu.VMEM)
            for o in range(n_out)
        ],
        scratch_shapes=held + sems + list(scratch),
        compiler_params=pltpu.CompilerParams(vmem_limit_bytes=vmem),
        cost_estimate=pl.CostEstimate(flops=1000, bytes_accessed=1000, transcendentals=0),
    )(*ins)


def wait(*arrays):
    return lax.optimization_barrier(arrays)


def tie(values, *others):
    return lax.optimization_barrier((values, *others))[0]


def swap(values, axis, bit):
    return lax.ppermute(values, axis, [(i, i ^ bit) for i in range(lax.axis_size(axis))])


def send_far(far_part, got, *others):
    sent = tie((far_part + got[: far_part.shape[0]].astype(F32)).astype(LOW), *others)
    return swap(sent, "mp", 2), sent


def axis_bits(axis):
    return [1 << i for i in range(lax.axis_size(axis).bit_length() - 1)]


def halving_order(bits):
    order = [0]
    for bit in reversed(bits):
        order = order + [r ^ bit for r in order]
    return np.array(order, np.int32)


def scatter_sum(values, axis, bits):
    for bit in bits:
        half = values.shape[0] // 2
        got = swap(values[half:].astype(LOW), axis, bit)
        values = values[:half] + got.astype(F32)
    return values


def gather_back(values, axis, bits):
    for bit in reversed(bits):
        values = jnp.concatenate([values, swap(values, axis, bit)])
    return values


def sum_low(values, axis, bits):
    values = values.astype(LOW)
    for bit in bits:
        values = (values.astype(F32) + swap(values, axis, bit).astype(F32)).astype(LOW)
    return values


def sum_exact(values, axis, bits):
    for bit in bits:
        values = values + swap(values, axis, bit)
    return values


def tile_active(bounds, block, tile):
    return (bounds[2, tile] <= bounds[1, block]) & (bounds[3, tile] >= bounds[0, block])


def attend_block(block, queries, keys, value_ts, q_ids, k_ids, bounds, mixed, row, out_row, logs, scratch):
    scores, peak, total, acc = scratch
    count = queries.shape[0] // 2
    heads = queries.shape[1] // HEAD
    query_rows = queries[row : row + count, :]
    ids = q_ids[:, block * count : (block + 1) * count]
    peak[...] = jnp.full(peak.shape, masked_score, F32)
    total[...] = jnp.zeros(total.shape, F32)
    acc[...] = jnp.zeros(acc.shape, F32)
    for tile in range(4):
        inner = (tile % 2) * count

        @pl.when(tile_active(bounds, block, tile))
        def _(tile=tile, inner=inner):
            allowed = k_ids[tile * count : (tile + 1) * count, :] == ids
            for h in range(heads):
                cols = slice(h * HEAD, (h + 1) * HEAD)
                part = dot_last(keys[tile // 2][inner : inner + count, cols], query_rows[:, cols])
                part = jnp.where(allowed, part, masked_score)
                scores[h, tile] = part
                peak[h : h + 1, :] = jnp.maximum(
                    peak[h : h + 1, :], jnp.max(part, axis=0, keepdims=True)
                )

    for tile in range(4):
        inner = (tile % 2) * count

        @pl.when(tile_active(bounds, block, tile))
        def _(tile=tile, inner=inner):
            for h in range(heads):
                weights = jnp.exp2((scores[h, tile] - peak[h : h + 1, :]) * exp2_scale)
                total[h : h + 1, :] += jnp.sum(weights, axis=0, keepdims=True)
                acc[h] += dot(
                    value_ts[tile // 2][h * HEAD : (h + 1) * HEAD, inner : inner + count],
                    weights.astype(LOW),
                )

    for h in range(heads):
        sums = total[h : h + 1, :]
        mixed[out_row : out_row + count, h * HEAD : (h + 1) * HEAD] = (acc[h] / sums).T.astype(LOW)
        logs[h : h + 1, out_row : out_row + count] = peak[h : h + 1, :] * exp2_scale + jnp.log2(sums)


def attend_scratch(count, heads):
    return [
        pltpu.VMEM((heads, 4, count, count), F32),
        pltpu.VMEM((8, count), F32),
        pltpu.VMEM((8, count), F32),
        pltpu.VMEM((heads, HEAD, count), F32),
    ]


def project_pair(blocks, weights, norm=None):
    count, width = blocks[0].shape[0], weights[0].shape[1]
    dim = blocks[0].shape[1]
    outs = [shape((2 * count, width), LOW) for w in weights] + [shape((width, 2 * count), LOW)] * 2
    ins = list(blocks) + list(weights)
    if norm is not None:
        outs.append(shape((2 * count, dim), LOW))
        ins += list(norm[:2])
    n_weights = len(weights)

    def body(need, emit, *refs):
        rows, ws = refs[:2], refs[2 : 2 + n_weights]
        res = refs[len(ins) :]
        if norm is not None:
            norm_into(rows, refs[2 + n_weights], refs[3 + n_weights], norm[2], res[-1])
            rows = [res[-1].at[:count], res[-1].at[count:]]
        need(0)
        project_into(rows, ws, res)

    return local_kernel(
        body, "project_pair", ins, outs, cold=[range(2, 2 + n_weights)], cold_outs=range(len(outs))
    )


def norm_into(blocks, gain, offset, index, out):
    count = blocks[0].shape[0]
    at = slice(index, index + 1)
    for b in range(2):
        rows = layer_norm(blocks[b][...].astype(F32), gain[at, :], offset[at, :])
        out[b * count : (b + 1) * count, :] = rows.astype(LOW)


def project_into(blocks, weights, res):
    count = blocks[0].shape[0]
    for i, weight in enumerate(weights):
        for b in range(2):
            part = dot(blocks[b][...], weight[...])
            res[i][b * count : (b + 1) * count, :] = part.astype(LOW)
            if i < 2:
                res[len(weights) + i][:, b * count : (b + 1) * count] = part.T.astype(LOW)


def attend_first(far, across, weights, queries_far, near_set, out_weight, ids, norm=None):
    count, dim = far.shape
    width = out_weight.shape[1]
    heads = width // HEAD
    with_query = len(weights) == 3
    q_ids, k_ids, bounds = ids
    n_weights = len(weights)
    first = [far, across, *weights, *(norm[:2] if norm else ())]
    second = [near_set[0], near_set[2], near_set[3], out_weight, q_ids, k_ids]
    if not with_query:
        second.append(queries_far)
    n_first, n_all = len(first), len(first) + len(second)
    ins = first + second + [bounds]
    pair = shape((2 * count, width), LOW)
    turned = shape((width, 2 * count), LOW)
    outs = [pair] * n_weights + [turned, turned]
    if norm is not None:
        outs.append(shape((2 * count, dim), LOW))
    n_project = len(outs)
    outs += [pair, shape((8, 2 * count)), shape((2 * count, dim), LOW)]

    def body(need, emit, *refs):
        res, scratch = refs[len(ins) : len(ins) + len(outs)], refs[len(ins) + len(outs) :]
        rows, ws = refs[:2], refs[2 : 2 + n_weights]
        near_keys, near_values, near_queries, wo, qi, ki = refs[n_first : n_first + 6]
        bnd = refs[n_all]
        if norm is not None:
            norm_into(rows, refs[2 + n_weights], refs[3 + n_weights], norm[2], res[n_project - 1])
            rows = [res[n_project - 1].at[:count], res[n_project - 1].at[count:]]
        need(0)
        project_into(rows, ws, res)
        emit(*res[:n_project])
        need(1)
        far_queries = res[2] if with_query else refs[n_first + 6]
        mixed, logs, hop = res[n_project:]
        for place, (block, source) in enumerate(((3, far_queries), (1, near_queries))):
            attend_block(
                block, source, (near_keys, res[0]), (near_values, res[n_weights + 1]),
                qi, ki, bnd, mixed, (block % 2) * count, place * count, logs, scratch,
            )
            rows_of_mixed = mixed[place * count : (place + 1) * count, :]
            hop[place * count : (place + 1) * count, :] = dot_last(rows_of_mixed, wo[...]).astype(LOW)

    return local_kernel(
        body, "attend_first", ins, outs, attend_scratch(count, heads), smem=(n_all,),
        cold=[range(2, 2 + n_weights), range(n_first, n_all)], cold_outs=range(n_project + 2),
    )


def attend_one(block, queries, near_set, far_set, out_weight, ids, after):
    width = out_weight.shape[1]
    heads = width // HEAD
    count = queries.shape[0] // 2
    dim = out_weight.shape[0]
    q_ids, k_ids, bounds = ids
    ins = [queries, near_set[0], far_set[0], near_set[1], far_set[1], out_weight, q_ids, k_ids, bounds]
    outs = [shape((count, width), LOW), shape((8, count)), shape((count, dim))]

    def body(need, emit, q, k0, k1, v0, v1, wo, qi, ki, bnd, mixed, logs, part, *scratch):
        need(0)
        attend_block(block, q, (k0, k1), (v0, v1), qi, ki, bnd, mixed, 0, 0, logs, scratch)
        part[...] = dot_last(mixed[...], wo[...])

    return local_kernel(
        body, "attend_one", ins, outs, attend_scratch(count, heads), smem=(8,),
        cold=[range(8)], cold_outs=(0, 1), after=after,
    )


def back_block(block, row, grads, queries, logs, keys, key_ts, values, q_ids, k_ids, bounds,
               query_grads, key_acc, value_acc, scratch):
    probs, grad_probs, inner_sum, acc = scratch
    count = queries.shape[0] // 2
    heads = queries.shape[1] // HEAD
    query_rows = queries[row : row + count, :]
    ids = q_ids[:, block * count : (block + 1) * count]
    inner_sum[...] = jnp.zeros(inner_sum.shape, F32)
    acc[...] = jnp.zeros(acc.shape, F32)
    for tile in range(4):
        inner = (tile % 2) * count

        @pl.when(tile_active(bounds, block, tile))
        def _(tile=tile, inner=inner):
            allowed = k_ids[tile * count : (tile + 1) * count, :] == ids
            for h in range(heads):
                cols = slice(h * HEAD, (h + 1) * HEAD)
                part = dot_last(keys[tile // 2][inner : inner + count, cols], query_rows[:, cols])
                exact = jnp.where(
                    allowed,
                    jnp.exp2(part * exp2_scale - logs[0][h : h + 1, logs[1] : logs[1] + count]),
                    0.0,
                )
                pulled = dot_last(values[tile // 2][inner : inner + count, cols], grads[:, cols])
                probs[h, tile] = exact
                grad_probs[h, tile] = pulled
                inner_sum[h : h + 1, :] += jnp.sum(exact * pulled, axis=0, keepdims=True)
                value_acc[tile * count : (tile + 1) * count, cols] += dot(
                    exact.astype(LOW), grads[:, cols]
                )

    for tile in range(4):
        inner = (tile % 2) * count

        @pl.when(tile_active(bounds, block, tile))
        def _(tile=tile, inner=inner):
            for h in range(heads):
                cols = slice(h * HEAD, (h + 1) * HEAD)
                score_grads = (
                    probs[h, tile] * (grad_probs[h, tile] - inner_sum[h : h + 1, :])
                ).astype(LOW)
                key_acc[tile * count : (tile + 1) * count, cols] += dot(
                    score_grads, query_rows[:, cols]
                )
                acc[h] += dot(key_ts[tile // 2][cols, inner : inner + count], score_grads)

    for h in range(heads):
        query_grads[row : row + count, h * HEAD : (h + 1) * HEAD] = (
            (acc[h] * score_scale).T.astype(LOW)
        )


def back_scratch(count, heads):
    return [
        pltpu.VMEM((heads, 4, count, count), F32),
        pltpu.VMEM((heads, 4, count, count), F32),
        pltpu.VMEM((8, count), F32),
        pltpu.VMEM((heads, HEAD, count), F32),
    ]


def back_near(grads, out_weight, queries, logs, kept, ids):
    count = queries.shape[0] // 2
    width = queries.shape[1]
    q_ids, k_ids, bounds = ids
    ins = [*grads, out_weight, queries, *logs, *kept, q_ids, k_ids, bounds]
    outs = [shape((2 * count, width), LOW), shape((4 * count, width)), shape((4 * count, width))]

    def body(need, emit, g0, g1, wo, q, lg, lo, k0, k1, t0, t1, v0, v1, qi, ki, bnd, dq, dk, dv, *scratch):
        need(0)
        dk[...] = jnp.zeros(dk.shape, F32)
        dv[...] = jnp.zeros(dv.shape, F32)
        for b, g in enumerate((g0, g1)):
            mixed_grads = dot(g[...], wo[...]).astype(LOW)
            logs_at = (lg, count) if b else (lo, 0)
            back_block(b, b * count, mixed_grads, q, logs_at, (k0, k1), (t0, t1), (v0, v1), qi, ki, bnd,
                       dq, dk, dv, scratch)

    return local_kernel(body, "back_near", ins, outs, back_scratch(count, width // HEAD), smem=(14,),
        cold=[range(2, 14)], cold_outs=(0,),
    )


def back_far(grads, out_weight, queries, logs, kept, ids, sums, weights, after=()):
    count = queries.shape[0] // 2
    width = queries.shape[1]
    dim = out_weight.shape[0]
    q_ids, k_ids, bounds = ids
    ins = [*grads, out_weight, queries, *logs, *kept, q_ids, k_ids, bounds, *sums, *weights]
    whole = shape((4 * count, width), LOW)
    outs = [shape((2 * count, width), LOW), whole, whole, shape((count, dim)), shape((count, dim), LOW)]

    def body(need, emit, *refs):
        g0, g1, wo, q, lg, lo, k0, k1, t0, t1, v0, v1, qi, ki, bnd, dk_in, dv_in = refs[:17]
        ws = refs[17 : 17 + len(weights)]
        dq, dk, dv, far_out, across_out, key_acc, value_acc, *scratch = refs[17 + len(weights) :]
        need(0)
        key_acc[...] = dk_in[...]
        value_acc[...] = dv_in[...]
        for b, g in enumerate((g0, g1)):
            mixed_grads = dot(g[...], wo[...]).astype(LOW)
            logs_at = (lg, 0) if b else (lo, 0)
            back_block(2 + b, b * count, mixed_grads, q, logs_at, (k0, k1), (t0, t1), (v0, v1), qi, ki, bnd,
                       dq, key_acc, value_acc, scratch)
        dk[...] = (key_acc[...] * score_scale).astype(LOW)
        dv[...] = value_acc[...].astype(LOW)
        need(1)
        for b in (1, 0):
            rows = slice((2 + b) * count, (3 + b) * count)
            part = dot_last(dk[rows, :], ws[0][...]) + dot_last(dv[rows, :], ws[1][...])
            if len(ws) == 3:
                part = part + dot_last(dq[b * count : (b + 1) * count, :], ws[2][...])
            if b:
                across_out[...] = part.astype(LOW)
            else:
                far_out[...] = part

    scratch = [pltpu.VMEM((4 * count, width), F32)] * 2 + back_scratch(count, width // HEAD)
    return local_kernel(
        body, "back_far", ins, outs, scratch, smem=(14,),
        cold=[range(2, 14), range(17, 17 + len(weights))], after=after,
    )


def pull_near(pairs, after):
    dim = pairs[0][1].shape[0]
    count = pairs[0][2]
    ins = [p[0] for p in pairs] + [p[1] for p in pairs]
    outs = [shape((count, dim)), shape((count, dim), LOW)]

    def body(need, emit, *refs):
        n = len(pairs)
        need(0)
        own_out, near_out = refs[2 * n :]
        for b in range(2):
            part = None
            for i in range(n):
                term = dot_last(refs[i][b * count : (b + 1) * count, :], refs[n + i][...])
                part = term if part is None else part + term
            if b:
                near_out[...] = part.astype(LOW)
            else:
                own_out[...] = part

    return local_kernel(
        body, "pull_near", ins, outs, cold=[range(len(pairs), 2 * len(pairs))], after=after
    )


def pull_active(grads, down_proj, after):
    count, units = grads[0].shape[0], down_proj.shape[1]

    def body(need, emit, g0, g1, down, out):
        need(0)
        for b, g in enumerate((g0, g1)):
            out[b * count : (b + 1) * count, :] = dot(g[...], down[...]).astype(LOW)

    return local_kernel(
        body, "pull_active", [*grads, down_proj], [shape((2 * count, units), LOW)], cold=[range(3)], after=after
    )[0]


def mlp_pair(rows, grads, up_proj, down_proj, after=(), pulled=None):
    count, dim = rows[0].shape
    units = up_proj.shape[1]
    step = 256
    outs = [
        shape((2 * count, units), LOW), shape((2 * count, units), LOW),
        shape((count, dim)), shape((count, dim), LOW),
    ]
    ready = pulled is not None
    ins = [*rows, up_proj, pulled] if ready else [*rows, up_proj, down_proj, *grads]

    def body(need, emit, x0, x1, up, *refs):
        active, grad_hidden, first_out, second_out = refs[-4:]
        need(0)
        for b, x in enumerate((x0, x1)):
            band = slice(b * count, (b + 1) * count)
            for at in range(0, units, step):
                hidden = dot(x[...], up[:, at : at + step])
                if ready:
                    back = refs[0][band, at : at + step].astype(F32)
                else:
                    back = dot(refs[1 + b][...], refs[0][:, at : at + step])
                square = hidden * hidden
                bent = jnp.tanh(gelu_coeff * (hidden + gelu_cubic * hidden * square))
                half = 0.5 * (1.0 + bent)
                slope = half + 0.5 * hidden * (1.0 - bent * bent) * (
                    gelu_coeff * (1.0 + 3.0 * gelu_cubic * square)
                )
                active[band, at : at + step] = (hidden * half).astype(LOW)
                grad_hidden[band, at : at + step] = (back * slope).astype(LOW)
        emit(active, grad_hidden)
        for b in (1, 0):
            part = dot_last(grad_hidden[b * count : (b + 1) * count, :], up[...])
            if b:
                second_out[...] = part.astype(LOW)
            else:
                first_out[...] = part

    return local_kernel(
        body, "mlp_pair", ins, outs, cold=[[2] if ready else range(2, 6)], cold_outs=(0, 1), after=after,
    )


def pull_four(near_rows, far_rows, weight, after):
    count, dim = near_rows.shape[0] // 2, weight.shape[0]
    outs = [shape((count, dim)), shape((count, dim)), shape((2 * count, dim), LOW)]

    def body(need, emit, x, y, w, own_out, far_out, hop):
        need(0)
        own_out[...] = dot_last(x[:count, :], w[...])
        far_out[...] = dot_last(y[:count, :], w[...])
        hop[:count, :] = dot_last(y[count:, :], w[...]).astype(LOW)
        hop[count:, :] = dot_last(x[count:, :], w[...]).astype(LOW)

    return local_kernel(
        body, "pull_four", [near_rows, far_rows, weight], outs, cold=[range(3)], cold_outs=(0, 1, 2), after=after
    )


def norm_rows(terms, gain, offset, index):
    kept = terms[0]

    def body(need, emit, k, p, n, f, g, o, after, normed):
        total = p[...] + n[n.shape[0] - p.shape[0] :, :].astype(F32) + f[...].astype(F32)
        need(0)
        total = total + k[...]
        after[...] = total
        emit(after)
        normed[...] = layer_norm(total, g[index : index + 1, :], o[index : index + 1, :]).astype(LOW)

    return local_kernel(
        body, "norm_rows", [*terms, gain, offset], [shape(kept.shape), shape(kept.shape, LOW)],
        cold=[[0]], cold_outs=(0,),
    )


def norm_rows_back(values, gain, index, terms, grads, after=(), inside=False):
    added = grads is not None

    def body(need, emit, v, g, p, n, f, *refs):
        if inside:
            need(0)
        total = p[...] + n[...].astype(F32) + f[...].astype(F32)
        if not inside:
            need(0)
        back, gain_sum, offset_sum = layer_norm_back(v[...].astype(F32), g[index : index + 1, :], total)
        if added:
            back = back + refs[0][...].astype(F32)
            out, sums = refs[1:]
            sums[0:1, :] = gain_sum
            sums[1:2, :] = offset_sum
        else:
            out = refs[0]
        out[...] = back.astype(out.dtype)

    ins = [values, gain, *terms]
    outs = [shape(values.shape, LOW if added else F32)]
    if added:
        ins.append(grads)
        outs.append(shape((2, values.shape[1])))
    return local_kernel(
        body, "norm_back", ins, outs, cold=[[0, 2, 5] if inside else [0, 5] if added else [0]], cold_outs=() if added else (0,),
        vmem=VMEM_LARGE if inside else VMEM_BYTES, after=after,
    )


def dp_orders():
    bits = axis_bits("dp")
    return [bits, bits[1:2] + bits[:1] + bits[2:]]


def outer_sums(sets, after, parts_sent=1):
    n_dp = lax.axis_size("dp")
    place = lax.axis_index("dp")
    ins, plans, places, outs = [], [], [], []
    seen = {}

    def take(array):
        if id(array) not in seen:
            seen[id(array)] = len(ins)
            ins.append(array)
        return seen[id(array)]

    for groups, bits in zip(sets, dp_orders()):
        plan = []
        for blocks, parts in groups:
            terms = []
            if len(parts) == 3:
                count = blocks[0].shape[0]
                terms = [
                    (take(blocks[0]), take(parts[0]), 0, count),
                    (take(blocks[1][1]), take(parts[1]), 0, count),
                    (take(blocks[1][0]), take(parts[1]), count, count),
                    (take(blocks[2]), take(parts[2]), 0, count),
                ]
            else:
                per = len(blocks) // len(parts)
                for b, block in enumerate(blocks):
                    count = block.shape[0]
                    terms.append((take(block), take(parts[b // per]), (b % per) * count, count))
            plan.append((terms, parts[0].shape[1]))
        plans.append(plan)
        dim = groups[0][0][0].shape[1]
        chunk = dim // n_dp
        aligned = chunk % 128 == 0
        steps = dim // 128
        width = sum(p[1] for p in plan)
        if aligned:
            repeat = chunk // 128
            spots = (jnp.asarray(halving_order(bits)) ^ place)[:, None] * repeat
            spots = (spots + jnp.arange(repeat, dtype=jnp.int32)[None, :]).reshape(steps)
        else:
            spots = jnp.arange(steps, dtype=jnp.int32)
        places.append(spots.astype(jnp.int32))
        outs += [shape((dim // 2, width))] + [shape((dim // 2 // parts_sent, width), LOW)] * parts_sent
    ins.append(jnp.stack(places))

    def body(need, emit, *refs):
        need(0)
        spots = refs[len(ins) - 1]
        results = refs[len(ins) :]

        def one(order, index, target, base):
            at = pl.multiple_of(spots[order, base + index] * 128, 128)
            column = 0
            for terms, right_width in plans[order]:
                total = None
                for left, right, row, count in terms:
                    term = dot_first(refs[left][:, pl.ds(at, 128)], refs[right][row : row + count, :])
                    total = term if total is None else total + term
                target[pl.ds(pl.multiple_of(index * 128, 128), 128), column : column + right_width] = (
                    total.astype(target.dtype)
                )
                column += right_width

        per = 1 + parts_sent
        half = steps // 2
        for piece in [*range(1, per), 0]:
            for order in range(len(plans)):
                run = half if piece == 0 else half // parts_sent
                base = 0 if piece == 0 else half + (piece - 1) * run

                @pl.loop(0, run)
                def _(index, target=results[per * order + piece], order=order, base=base):
                    one(order, index, target, base)

    results = local_kernel(
        body, "outer_sums", ins, outs, smem=(len(ins) - 1,), cold=[range(len(ins) - 1)],
        cold_outs=range(len(outs)), vmem=VMEM_LARGE, after=after,
    )
    pairs = []
    for order, bits in enumerate(dp_orders()[: len(plans)]):
        keep, *sent = results[(1 + parts_sent) * order : (1 + parts_sent) * (order + 1)]
        if not aligned:
            whole = jnp.concatenate([keep, *[part.astype(F32) for part in sent]])
            whole = whole.reshape(n_dp, chunk, keep.shape[1])
            whole = whole[jnp.asarray(halving_order(bits)) ^ place].reshape(dim, keep.shape[1])
            keep, whole = whole[: dim // 2], whole[dim // 2 :].astype(LOW)
            sent = [part for part in whole.reshape(parts_sent, dim // 2 // parts_sent, keep.shape[1])]
        pairs.append((keep, *sent))
    return pairs


def outer_whole(groups, after):
    ins = [a for blocks, parts in groups for a in (*blocks, *parts)]
    dim = groups[0][0][0].shape[1]
    width = groups[0][1][0].shape[1]
    step = 256

    def body(need, emit, *refs):
        out = refs[len(ins)]
        for k in range(len(groups)):
            need(k)
            lefts, rights = refs[6 * k : 6 * k + 4], refs[6 * k + 4 : 6 * k + 6]
            count = lefts[0].shape[0]

            @pl.loop(0, dim // step)
            def _(index, k=k, lefts=lefts, rights=rights, count=count):
                at = pl.multiple_of(index * step, step)
                total = None
                for b in range(4):
                    right = rights[b // 2][(b % 2) * count : (b % 2 + 1) * count, :]
                    term = dot_first(lefts[b][:, pl.ds(at, step)], right)
                    total = term if total is None else total + term
                out[pl.ds(at, step), k * width : (k + 1) * width] = total.astype(LOW)

    return local_kernel(
        body, "outer_whole", ins, [shape((dim, width * len(groups)), LOW)],
        cold=[range(6 * k, 6 * k + 6) for k in range(len(groups))], cold_outs=(0,), after=after,
    )[0]


def merge(pairs, last, widths, after=()):
    ins, outs, firsts = [], [], []
    for order, (keep, *came) in enumerate(pairs):
        firsts.append(len(ins))
        ins += [keep, *came]
        rows, width = keep.shape
        if last:
            outs += [shape((rows, w)) for w in widths[order]]
        else:
            outs += [shape((rows // 2, width)), shape((rows // 2, width), LOW)]

    def body(need, emit, *refs):
        results = list(refs[len(ins) :])
        for order in range(len(pairs)):
            keep, got = refs[firsts[order]], refs[firsts[order] + 1]
            if last:
                column = 0
                for w in widths[order]:
                    cols = slice(column, column + w)
                    results.pop(0)[...] = keep[:, cols] + got[:, cols].astype(F32)
                    column += w
            else:
                half = keep.shape[0] // 2
                later = got[half:, :] if len(pairs[order]) == 2 else refs[firsts[order] + 2][...]
                results.pop(0)[...] = keep[:half, :] + got[:half, :].astype(F32)
                results.pop(0)[...] = (keep[half:, :] + later.astype(F32)).astype(LOW)

    results = local_kernel(body, "merge", ins, outs, after=after)
    if last:
        return results
    return [(results[2 * i], results[2 * i + 1]) for i in range(len(pairs))]


def rows_of(source, row_start, row_count):
    return lax.dynamic_slice_in_dim(source, row_start, row_count, 0)


def turn_row(row):
    columns = []
    for at in range(0, row.shape[1], 128):
        columns.append(jnp.broadcast_to(row[:, at : at + 128], (128, 128)).T[:, 0:1])
    return jnp.concatenate(columns, axis=0)


def prepare(latent_row, input_row, member, table, gain, offset, query_weight, images):
    total = latent_row.shape[1]
    count = total // 4
    slots, dim = table.shape
    width = query_weight.shape[1]
    whole = jnp.int32
    outs = [
        shape((1, total), whole), shape((total, 1), whole), shape((total, 1), whole),
        shape((4, 4), whole), shape((4, 4), whole),
        shape((total, slots), LOW), shape((slots, dim), LOW),
        shape((2 * count, width), LOW), shape((2 * count, width), LOW), shape((count, dim)),
    ]

    def body(need, emit, lat, inp, lat_s, inp_s, who, tb, g, o, wq,
             lat_out, lat_col, inp_col, cross_ends, self_ends, pick, normed, near_q, far_q, start):
        order = [who[0, 0] ^ k for k in range(4)]
        for k in range(4):
            first = order[k] * count
            last = first + count - 1
            cross_ends[0, k] = lat_s[0, first]
            cross_ends[1, k] = lat_s[0, last]
            cross_ends[2, k] = inp_s[0, first]
            cross_ends[3, k] = inp_s[0, last]
            for r in range(2):
                self_ends[2 * r, k] = lat_s[0, first]
                self_ends[2 * r + 1, k] = lat_s[0, last]
        starts = [pl.multiple_of(at * count, count) for at in order]
        lat_rel = jnp.concatenate([lat[:, pl.ds(at, count)] for at in starts], axis=1)
        inp_rel = jnp.concatenate([inp[:, pl.ds(at, count)] for at in starts], axis=1)
        lane = lax.broadcasted_iota(whole, (1, count), 1)
        place = jnp.concatenate([lane + at for at in starts], axis=1)
        lat_all = lat[...]
        for image in range(images):
            before = jnp.sum((lat_all < image).astype(F32), axis=1, keepdims=True).astype(whole)
            place = place - jnp.where(lat_rel == image, before, 0)
        lat_out[...] = lat_rel
        lat_col[...] = turn_row(lat_rel)
        inp_col[...] = turn_row(inp_rel)
        slot = turn_row(place)
        slot_lane = lax.broadcasted_iota(whole, (total, slots), 1)
        pick[...] = jnp.where(slot == slot_lane, 1.0, 0.0).astype(LOW)
        normed[...] = layer_norm(tb[...].astype(F32), g[0:1, :], o[0:1, :]).astype(LOW)
        start[...] = dot(pick[:count, :], tb[...])
        need(0)
        queries = dot(normed[...], wq[...]).astype(LOW)
        near_q[...] = dot(pick[: 2 * count, :], queries).astype(LOW)
        far_q[...] = dot(pick[2 * count :, :], queries).astype(LOW)

    return local_kernel(
        body, "prepare",
        [latent_row, input_row, latent_row, input_row, member, table, gain, offset, query_weight],
        outs, smem=(2, 3, 4), smem_outs=(3, 4), cold=[[8]],
    )


def slot_stack(pick, query_pairs, raw_blocks, parts, grads, sums, member, after):
    count, dim = raw_blocks[0].shape
    slots, width = pick.shape[1], query_pairs[0].shape[1]
    cut = dim // (2 * width)
    ins = [pick, *query_pairs, *raw_blocks, *parts, *grads, *sums, member]

    def body(need, emit, pk, q0, q1, x0, x1, x2, x3, p0, p1, p2, p3, r0, r1, r2, r3, s0, s1, who, out):
        need(0)
        total = dot_first(pk[: 2 * count, :], q0[...]) + dot_first(pk[2 * count :, :], q1[...])
        out[:slots, :width] = total.astype(LOW)
        at = pl.multiple_of(who[0, 0] * width, width)
        total = None
        for b, r in enumerate((r0, r1, r2, r3)):
            term = dot_first(pk[b * count : (b + 1) * count, :], r[:, pl.ds(at, width)])
            total = term if total is None else total + term
        out[:slots, width:] = total.astype(LOW)
        gain_sum = offset_sum = None
        for x, p in ((x0, p0), (x1, p1), (x2, p2), (x3, p3)):
            values = x[...].astype(F32)
            centred = values - jnp.mean(values, axis=-1, keepdims=True)
            spread = jnp.mean(centred * centred, axis=-1, keepdims=True)
            back = p[...].astype(F32)
            gains = jnp.sum(back * (centred * lax.rsqrt(spread + norm_eps)), axis=0, keepdims=True)
            offsets = jnp.sum(back, axis=0, keepdims=True)
            gain_sum = gains if gain_sum is None else gain_sum + gains
            offset_sum = offsets if offset_sum is None else offset_sum + offsets
        rows = [gain_sum, offset_sum, s0[0:1, :], s0[1:2, :], s1[0:1, :], s1[1:2, :]]
        rows += [jnp.zeros((1, dim), F32)] * 2
        whole = jnp.concatenate(rows, axis=0)
        for q in range(cut):
            out[slots + 8 * q : slots + 8 * (q + 1), :] = (
                whole[:, 2 * q * width : 2 * (q + 1) * width].astype(LOW)
            )

    return local_kernel(
        body, "slot_stack", ins, [shape((slots + 8 * cut, 2 * width), LOW)],
        smem=(len(ins) - 1,), cold=[range(7)], after=after,
    )[0]


def table_end(stacks, weights, gain, table, member):
    slots, dim = table.shape
    width = stacks[0].shape[1] // 2
    cut = dim // (2 * width)
    ins = [*stacks, *weights, gain, table, member]

    def body(need, emit, *refs):
        st, ws = refs[:4], refs[4:8]
        g, tb, who = refs[8:11]
        table_out, gain_out, offset_out, last_out, residual, grads, weight = refs[11:]
        need(0)
        for k in range(4):
            at = pl.multiple_of((who[0, 0] ^ k) * width, width)
            grads[:, pl.ds(at, width)] = st[k][:slots, :width]
            residual[:, pl.ds(at, width)] = st[k][:slots, width:]
            weight[:, pl.ds(at, width)] = ws[k][...]
        total = dot_last(grads[...], weight[...])
        back, gain_sum, offset_sum = layer_norm_back(tb[...].astype(F32), g[0:1, :], total)
        table_out[...] = residual[...].astype(F32) + back
        small = [st[k][slots:, :].astype(F32) for k in range(4)]
        small = (small[0] + small[1]) + (small[2] + small[3])
        small = jnp.concatenate([small[8 * q : 8 * (q + 1), :] for q in range(cut)], axis=1)
        gain_out[0:1, :] = gain_sum
        offset_out[0:1, :] = offset_sum
        for k in range(3):
            gain_out[k + 1 : k + 2, :] = small[2 * k : 2 * k + 1, :]
            target = last_out if k == 2 else offset_out
            at = 0 if k == 2 else k + 1
            target[at : at + 1, :] = small[2 * k + 1 : 2 * k + 2, :]

    outs = [shape((slots, dim)), shape((4, dim)), shape((3, dim)), shape((1, dim))]
    return local_kernel(
        body, "table_end", ins, outs,
        [pltpu.VMEM((slots, dim), LOW), pltpu.VMEM((slots, dim), LOW), pltpu.VMEM((dim, dim), LOW)],
        smem=(10,), cold=[range(4, 8)],
    )


def body(
    block_input,
    latent_table,
    latent_segments,
    input_segments,
    ln_gain,
    ln_bias,
    cross_query,
    cross_key,
    cross_value,
    cross_out,
    self_query,
    self_key,
    self_value,
    self_out,
    up_proj,
    down_proj,
    out_grad,
):
    count, dim = block_input.shape
    member = lax.axis_index("mp")
    n_mp, n_dp = lax.axis_size("mp"), lax.axis_size("dp")
    slots = latent_table.shape[0]
    mp_bits, dp_bits = axis_bits("mp"), axis_bits("dp")
    dp_steps = len(dp_bits)

    far_raw = swap(block_input, "mp", 2)
    near_raw = swap(block_input, "mp", 1)
    near_out = swap(out_grad, "mp", 1)
    half = count // 2
    near_raw, out_1, out_2 = lax.optimization_barrier((near_raw, out_grad[:half], out_grad[half:]))

    who = member.astype(jnp.int32).reshape(1, 1)
    (latent_rel, latent_col, input_col, cross_ends, self_ends, table_pick, normed_table, queries_near,
     queries_far, start_rows) = prepare(
        latent_segments, input_segments, who, latent_table, ln_gain, ln_bias, cross_query, images
    )
    cross_ids = (latent_rel, input_col, cross_ends)
    self_ids = (latent_rel, latent_col, self_ends)

    input_norm = (ln_gain, ln_bias, 1)
    keys_near, values_near, key_ts_near, value_ts_near, normed_near = project_pair(
        (block_input, near_raw), (cross_key, cross_value), input_norm
    )
    far_raw = tie(far_raw, keys_near, queries_far)
    across_raw = swap(far_raw, "mp", 1)
    far_out_1 = swap(tie(out_1, far_raw), "mp", 2)
    (keys_far, values_far, key_ts_far, value_ts_far, normed_far, mixed_two, logs_two, hop) = attend_first(
        far_raw, across_raw, (cross_key, cross_value), queries_far,
        (keys_near, key_ts_near, value_ts_near, queries_near), cross_out, cross_ids, input_norm,
    )
    got = swap(tie(hop, far_out_1), "mp", 1)
    key_values = ((keys_near, value_ts_near), (keys_far, value_ts_far))
    mixed_far, logs_far, part_far = attend_one(2, queries_far, *key_values, cross_out, cross_ids, ())
    got_far, sent = send_far(part_far, got)
    mixed_own, logs_own, part_own = attend_one(0, queries_near, *key_values, cross_out, cross_ids, (sent,))
    cross_kept = (keys_near, keys_far, key_ts_near, key_ts_far, values_near, values_far)
    cross_queries_set = (queries_near, queries_far)
    cross_logs = ((logs_two, logs_own), (logs_two, logs_far))
    cross_mixed = (mixed_own, mixed_two, mixed_far)
    after_cross, normed_self = norm_rows((start_rows, part_own, got, got_far), ln_gain, ln_bias, 2)

    self_weights = (self_key, self_value, self_query)
    far_self = swap(normed_self, "mp", 2)
    near_self = swap(normed_self, "mp", 1)
    keys_near, values_near, queries_near, key_ts_near, value_ts_near = project_pair(
        (normed_self, near_self), self_weights
    )
    far_self = tie(far_self, keys_near)
    across_self = swap(far_self, "mp", 1)
    far_out_2 = swap(tie(out_2, far_self), "mp", 2)
    (keys_far, values_far, queries_far, key_ts_far, value_ts_far, mixed_two, logs_two, hop) = attend_first(
        far_self, across_self, self_weights, None,
        (keys_near, key_ts_near, value_ts_near, queries_near), self_out, self_ids,
    )
    got = swap(tie(hop, far_out_2), "mp", 1)
    key_values = ((keys_near, value_ts_near), (keys_far, value_ts_far))
    mixed_far, logs_far, part_far = attend_one(2, queries_far, *key_values, self_out, self_ids, ())
    got_far, sent = send_far(part_far, got)
    mixed_own, logs_own, part_own = attend_one(0, queries_near, *key_values, self_out, self_ids, (sent,))
    far_out = tie(jnp.concatenate([far_out_1, far_out_2]), part_own)
    across_out = swap(far_out, "mp", 1)
    self_kept = (keys_near, keys_far, key_ts_near, key_ts_far, values_near, values_far)
    self_queries_set = (queries_near, queries_far)
    self_logs = ((logs_two, logs_own), (logs_two, logs_far))
    self_mixed = (mixed_own, mixed_two, mixed_far)
    after_self, normed_mlp = norm_rows((after_cross, part_own, got, got_far), ln_gain, ln_bias, 3)

    far_mlp = swap(normed_mlp, "mp", 2)
    near_mlp = swap(normed_mlp, "mp", 1)
    active_near, hidden_near, part_own, part_near = mlp_pair(
        (normed_mlp, near_mlp), (out_grad, near_out), up_proj, down_proj, (across_out,)
    )
    pulled_far = pull_active((far_out, across_out), down_proj, (part_near,))
    far_mlp = tie(far_mlp, pulled_far)
    across_mlp = swap(far_mlp, "mp", 1)
    active_far, hidden_far, part_far, part_across = mlp_pair(
        (far_mlp, across_mlp), None, up_proj, None, (), pulled_far
    )
    got = swap(part_across, "mp", 1)
    got_far, sent = send_far(part_far, got)
    got_near = swap(part_near, "mp", 1)
    mlp_grads = outer_whole(
        [
            ((normed_mlp, near_mlp, far_mlp, across_mlp), (hidden_near, hidden_far)),
            ((out_grad, near_out, far_out, across_out), (active_near, active_far)),
        ],
        (sent, got_near),
    )
    mlp_sum = lax.psum_scatter(tie(mlp_grads, got_far), "dp", scatter_dimension=0, tiled=True)
    dy_own, mlp_sums = norm_rows_back(
        after_self, ln_gain, 3, (part_own, got_near, got_far), out_grad,
        (mlp_grads,), True,
    )

    far_dy = swap(dy_own, "mp", 2)
    near_dy = swap(dy_own, "mp", 1)

    query_near, key_sum, value_sum = back_near(
        (dy_own, near_dy), self_out, self_queries_set[0], self_logs[0], self_kept, self_ids
    )
    far_dy = tie(far_dy, key_sum)
    across_dy = swap(far_dy, "mp", 1)
    query_far, key_grads, value_grads, part_far, part_across = back_far(
        (far_dy, across_dy), self_out, self_queries_set[1], self_logs[1], self_kept, self_ids,
        (key_sum, value_sum), self_weights,
    )
    got = swap(part_across, "mp", 1)
    part_own, part_near = pull_near(
        [(key_grads, self_key, count), (value_grads, self_value, count), (query_near, self_query, count)], ()
    )
    got_far, sent = send_far(part_far, got, part_own)
    got_near = swap(part_near, "mp", 1)
    normed_blocks = (normed_self, near_self, far_self, across_self)
    self_pairs = outer_sums(
        [
            [
                (normed_blocks, (query_near, query_far)), (normed_blocks, (key_grads,)),
                (normed_blocks, (value_grads,)), ((dy_own, (near_dy, across_dy), far_dy), self_mixed),
            ],
        ],
        (sent, got_near), 2,
    )
    dy_cross, self_sums = norm_rows_back(
        after_cross, ln_gain, 2, (part_own, got_near, got_far), dy_own,
        (self_pairs[0][1],),
    )

    far_dyc = swap(dy_cross, "mp", 2)
    near_dyc = swap(dy_cross, "mp", 1)
    query_near, key_sum, value_sum = back_near(
        (dy_cross, near_dyc), cross_out, cross_queries_set[0], cross_logs[0], cross_kept, cross_ids
    )
    part_own_out, part_far_out, hop_out = pull_four(active_near, active_far, down_proj, (key_sum,))
    self_half = swap(self_pairs[0][1], "dp", dp_bits[0])
    far_dyc = tie(far_dyc, part_own_out, self_half)
    across_dyc = swap(far_dyc, "mp", 1)
    query_far, key_grads, value_grads, part_far, part_across = back_far(
        (far_dyc, across_dyc), cross_out, cross_queries_set[1], cross_logs[1], cross_kept, cross_ids,
        (key_sum, value_sum), (cross_key, cross_value),
    )
    dyc_blocks = (dy_cross, near_dyc, far_dyc, across_dyc)
    part_own, part_near = pull_near([(key_grads, cross_key, count), (value_grads, cross_value, count)], ())
    got = swap(part_across, "mp", 1)
    got_near = swap(part_near, "mp", 1)
    got_far, sent = send_far(part_far, got, part_own)

    up_width = up_proj.shape[1]
    heads_width = cross_query.shape[1]
    stack = slot_stack(
        table_pick, (query_near, query_far), (block_input, near_raw, far_raw, across_raw),
        (part_own, part_near, part_far, part_across), dyc_blocks, (self_sums, mlp_sums), who,
        (sent,),
    )
    input_blocks = (normed_near, normed_far)
    cross_sets = [
        [
            (input_blocks, (key_grads,)),
            (input_blocks, (value_grads,)),
            ((dy_cross, (near_dyc, across_dyc), far_dyc), cross_mixed),
        ],
    ]
    self_keep, _, self_sent = self_pairs[0]

    def dp_swap(values, step):
        return swap(values, "dp", dp_bits[step])

    def joined(mine, came):
        return (mine.astype(F32) + came.astype(F32)).astype(LOW)

    def halved(keep, *came):
        return merge([(keep, *came)], False, None)[0]

    stack_got, self_got = dp_swap(stack, 0), dp_swap(self_sent, 0)
    ((cross_keep, cross_sent),) = outer_sums(cross_sets, (stack,))
    got_far, got_near, stack, stack_got, self_got, cross_sent, hop_out, query_sent = wait(
        got_far, got_near, stack, stack_got, self_got, cross_sent, hop_out, cross_query
    )
    stack = joined(stack, stack_got)

    self_keep, self_sent = halved(self_keep, self_half, self_got)
    stack_got, self_got, cross_got = dp_swap(stack, 1), dp_swap(self_sent, 1), dp_swap(cross_sent, 0)
    far_query, near_query = swap(query_sent, "mp", 2), swap(query_sent, "mp", 1)
    got_out = swap(hop_out, "mp", 1)
    stack, stack_got, got_out, self_sent, got_far = wait(stack, stack_got, got_out, self_sent, got_far)
    stack = joined(stack, stack_got)
    sent_out = (part_far_out + got_out[:count].astype(F32)).astype(LOW)

    stack_got = dp_swap(stack, 2)
    got_far_out = swap(sent_out, "mp", 2)
    (grad_input,) = norm_rows_back(block_input, ln_gain, 1, (part_own, got_near, got_far), None)
    mlp_parts = [mlp_sum[:, :up_width].astype(F32), mlp_sum[:, up_width:].astype(F32)]
    stack, stack_got, self_got, cross_got, mlp_parts, grad_input = wait(
        stack, stack_got, self_got, cross_got, mlp_parts, grad_input
    )

    for step in range(3, dp_steps):
        stack = joined(stack, stack_got)
        self_keep, self_sent = halved(self_keep, self_got)
        cross_keep, cross_sent = halved(cross_keep, cross_got)
        stack_got, cross_got, self_got = wait(
            dp_swap(stack, step), dp_swap(cross_sent, step - 2), dp_swap(self_sent, step - 1)
        )

    cross_keep, cross_sent = halved(cross_keep, cross_got)
    stack = joined(tie(stack, cross_sent), stack_got)
    far_stack, near_stack = swap(stack, "mp", 2), swap(stack, "mp", 1)
    cross_got = dp_swap(cross_sent, dp_steps - 2)
    self_keep, self_sent = halved(tie(self_keep, cross_sent), self_got)
    self_got = dp_swap(self_sent, dp_steps - 1)
    chunk = dim // n_dp
    own_features = lax.dynamic_slice_in_dim(normed_table, lax.axis_index("dp") * chunk, chunk, 1)
    query_sum = dot_first(own_features, stack[:slots, :heads_width])
    block_output = (
        after_self + part_own_out + got_out[count:].astype(F32) + got_far_out.astype(F32)
    )
    far_stack, cross_got, self_got, far_query, near_query, block_output, query_sum = wait(
        far_stack, cross_got, self_got, far_query, near_query, block_output, query_sum
    )

    across_stack = swap(far_stack, "mp", 1)
    across_query = swap(far_query, "mp", 1)
    cross_keep, cross_sent = halved(cross_keep, cross_got)
    cross_got = dp_swap(cross_sent, dp_steps - 1)
    across_stack, cross_sent = wait(across_stack, cross_sent)
    table_grad, ln_gain_grad, ln_bias_grad, last_bias = table_end(
        (stack, near_stack, far_stack, across_stack),
        (cross_query, near_query, far_query, across_query), ln_gain, latent_table, who,
    )
    cross_keep, self_keep, table_grad = wait(cross_keep, self_keep, table_grad)
    self_pair = merge([(self_keep, self_got)], True, [[heads_width] * 4])
    cross_pair = merge([(cross_keep, cross_got)], True, [[heads_width] * 3])

    return (
        block_output,
        grad_input,
        table_grad,
        ln_gain_grad,
        ln_bias_grad,
        last_bias[0],
        query_sum,
        *cross_pair,
        *self_pair,
        *mlp_parts,
    )


def solution(mesh):
    placed = (
        P(("dp", "mp"), None),
        P(),
        P("dp", None),
        P("dp", None),
        P(),
        P(),
        P(None, "mp"),
        P(None, "mp"),
        P(None, "mp"),
        P(None, "mp"),
        P(None, "mp"),
        P(None, "mp"),
        P(None, "mp"),
        P(None, "mp"),
        P(None, "mp"),
        P(None, "mp"),
        P(("dp", "mp"), None),
    )
    return jax.shard_map(
        body,
        mesh=mesh,
        in_specs=placed,
        out_specs=(
            P(("dp", "mp"), None),
            P(("dp", "mp"), None),
            P(),
            P(),
            P(),
            P(),
            P("dp", "mp"),
            P("dp", "mp"),
            P("dp", "mp"),
            P("dp", "mp"),
            P("dp", "mp"),
            P("dp", "mp"),
            P("dp", "mp"),
            P("dp", "mp"),
            P("dp", "mp"),
            P("dp", "mp"),
        ),
        check_vma=False,
    )
```

```python
import jax
import jax.numpy as jnp
import numpy as np
from jax import lax
from jax.experimental import pallas as pl
from jax.experimental.pallas import tpu as pltpu
from jax.sharding import PartitionSpec as P

HEAD = 128
images = 16
norm_eps = 1e-05
masked_score = -1e30
gelu_coeff = 0.7978845608028654
gelu_cubic = 0.044715
log2_e = 1.4426950408889634
score_scale = HEAD ** (-0.5)
exp2_scale = score_scale * log2_e
LOW = jnp.bfloat16
F32 = jnp.float32
VMEM_BYTES = 32 * 1024 * 1024
VMEM_LARGE = 56 * 1024 * 1024


def layer_norm(values, gain, offset):
    average = jnp.mean(values, axis=-1, keepdims=True)
    centred = values - average
    spread = jnp.mean(centred * centred, axis=-1, keepdims=True)
    return centred * lax.rsqrt(spread + norm_eps) * gain + offset


def layer_norm_back(values, gain, grad):
    average = jnp.mean(values, axis=-1, keepdims=True)
    centred = values - average
    spread = jnp.mean(centred * centred, axis=-1, keepdims=True)
    inverse = lax.rsqrt(spread + norm_eps)
    normal = centred * inverse
    scaled = grad * gain
    inner = jnp.mean(scaled * normal, axis=-1, keepdims=True)
    back = inverse * (scaled - jnp.mean(scaled, axis=-1, keepdims=True) - normal * inner)
    return (
        back,
        jnp.sum(grad * normal, axis=0, keepdims=True),
        jnp.sum(grad, axis=0, keepdims=True),
    )


def dot(left, right):
    return jnp.dot(left, right, preferred_element_type=F32)


def dot_last(left, right):
    return lax.dot_general(left, right, (((1,), (1,)), ((), ())), preferred_element_type=F32)


def dot_first(left, right):
    return lax.dot_general(left, right, (((0,), (0,)), ((), ())), preferred_element_type=F32)


def shape(dims, kind=F32):
    return jax.ShapeDtypeStruct(dims, kind)


def local_kernel(body, name, ins, outs, scratch=(), smem=(), cold=None, cold_outs=(), smem_outs=(), vmem=VMEM_BYTES, after=()):
    if after:
        ins = [tie(ins[0], *after), *ins[1:]]
    n_in, n_out = len(ins), len(outs)
    groups = [list(g) for g in (cold or [])]
    moved = [i for g in groups for i in g]
    held = [pltpu.VMEM(ins[i].shape, ins[i].dtype) for i in moved]
    held += [pltpu.VMEM(outs[o].shape, outs[o].dtype) for o in cold_outs]
    sems = []
    if moved:
        sems.append(pltpu.SemaphoreType.DMA((len(moved),)))
    if cold_outs:
        sems.append(pltpu.SemaphoreType.DMA((len(cold_outs),)))

    def run(*refs):
        inside = list(refs[:n_in])
        results = list(refs[n_in : n_in + n_out])
        rest = list(refs[n_in + n_out :])
        buffers, rest = rest[: len(held)], rest[len(held) :]
        in_sem = rest.pop(0) if moved else None
        out_sem = rest.pop(0) if cold_outs else None
        copies, waited, sent = {}, set(), {}
        for place, i in enumerate(moved):
            copies[i] = pltpu.make_async_copy(refs[i], buffers[place], in_sem.at[place])
            copies[i].start()
            inside[i] = buffers[place]
        made = list(results)
        for place, o in enumerate(cold_outs):
            made[o] = buffers[len(moved) + place]

        def need(*which):
            for k in which:
                for i in groups[k]:
                    copies[i].wait()
                waited.add(k)

        def emit(*given):
            for ref in given:
                for place, o in enumerate(cold_outs):
                    if made[o] is ref and o not in sent:
                        sent[o] = pltpu.make_async_copy(made[o], results[o], out_sem.at[place])
                        sent[o].start()

        body(need, emit, *inside, *made, *rest)
        for k in range(len(groups)):
            if k not in waited:
                need(k)
        emit(*[made[o] for o in cold_outs])
        for o in cold_outs:
            sent[o].wait()

    spaces = [pltpu.VMEM] * n_in
    for i in smem:
        spaces[i] = pltpu.SMEM
    for i in moved:
        spaces[i] = pl.ANY
    return pl.pallas_call(
        run,
        name=name,
        out_shape=list(outs),
        in_specs=[pl.BlockSpec(memory_space=s) for s in spaces],
        out_specs=[
            pl.BlockSpec(memory_space=pl.ANY if o in cold_outs else pltpu.SMEM if o in smem_outs else pltpu.VMEM)
            for o in range(n_out)
        ],
        scratch_shapes=held + sems + list(scratch),
        compiler_params=pltpu.CompilerParams(vmem_limit_bytes=vmem),
        cost_estimate=pl.CostEstimate(flops=1000, bytes_accessed=1000, transcendentals=0),
    )(*ins)


def wait(*arrays):
    return lax.optimization_barrier(arrays)


def tie(values, *others):
    return lax.optimization_barrier((values, *others))[0]


def swap(values, axis, bit):
    return lax.ppermute(values, axis, [(i, i ^ bit) for i in range(lax.axis_size(axis))])


def send_far(far_part, got, *others):
    sent = tie((far_part + got[: far_part.shape[0]].astype(F32)).astype(LOW), *others)
    return swap(sent, "mp", 2), sent


def axis_bits(axis):
    return [1 << i for i in range(lax.axis_size(axis).bit_length() - 1)]


def halving_order(bits):
    order = [0]
    for bit in reversed(bits):
        order = order + [r ^ bit for r in order]
    return np.array(order, np.int32)


def scatter_sum(values, axis, bits):
    for bit in bits:
        half = values.shape[0] // 2
        got = swap(values[half:].astype(LOW), axis, bit)
        values = values[:half] + got.astype(F32)
    return values


def gather_back(values, axis, bits):
    for bit in reversed(bits):
        values = jnp.concatenate([values, swap(values, axis, bit)])
    return values


def sum_low(values, axis, bits):
    values = values.astype(LOW)
    for bit in bits:
        values = (values.astype(F32) + swap(values, axis, bit).astype(F32)).astype(LOW)
    return values


def sum_exact(values, axis, bits):
    for bit in bits:
        values = values + swap(values, axis, bit)
    return values


def tile_active(bounds, block, tile):
    return (bounds[2, tile] <= bounds[1, block]) & (bounds[3, tile] >= bounds[0, block])


def attend_block(block, queries, keys, value_ts, q_ids, k_ids, bounds, mixed, row, out_row, logs, scratch):
    scores, peak, total, acc = scratch
    count = queries.shape[0] // 2
    heads = queries.shape[1] // HEAD
    query_rows = queries[row : row + count, :]
    ids = q_ids[:, block * count : (block + 1) * count]
    peak[...] = jnp.full(peak.shape, masked_score, F32)
    total[...] = jnp.zeros(total.shape, F32)
    acc[...] = jnp.zeros(acc.shape, F32)
    for tile in range(4):
        inner = (tile % 2) * count

        @pl.when(tile_active(bounds, block, tile))
        def _(tile=tile, inner=inner):
            allowed = k_ids[tile * count : (tile + 1) * count, :] == ids
            for h in range(heads):
                cols = slice(h * HEAD, (h + 1) * HEAD)
                part = dot_last(keys[tile // 2][inner : inner + count, cols], query_rows[:, cols])
                part = jnp.where(allowed, part, masked_score)
                scores[h, tile] = part
                peak[h : h + 1, :] = jnp.maximum(
                    peak[h : h + 1, :], jnp.max(part, axis=0, keepdims=True)
                )

    for tile in range(4):
        inner = (tile % 2) * count

        @pl.when(tile_active(bounds, block, tile))
        def _(tile=tile, inner=inner):
            for h in range(heads):
                weights = jnp.exp2((scores[h, tile] - peak[h : h + 1, :]) * exp2_scale)
                total[h : h + 1, :] += jnp.sum(weights, axis=0, keepdims=True)
                acc[h] += dot(
                    value_ts[tile // 2][h * HEAD : (h + 1) * HEAD, inner : inner + count],
                    weights.astype(LOW),
                )

    for h in range(heads):
        sums = total[h : h + 1, :]
        mixed[out_row : out_row + count, h * HEAD : (h + 1) * HEAD] = (acc[h] / sums).T.astype(LOW)
        logs[h : h + 1, out_row : out_row + count] = peak[h : h + 1, :] * exp2_scale + jnp.log2(sums)


def attend_scratch(count, heads):
    return [
        pltpu.VMEM((heads, 4, count, count), F32),
        pltpu.VMEM((8, count), F32),
        pltpu.VMEM((8, count), F32),
        pltpu.VMEM((heads, HEAD, count), F32),
    ]


def project_pair(blocks, weights, norm=None):
    count, width = blocks[0].shape[0], weights[0].shape[1]
    dim = blocks[0].shape[1]
    outs = [shape((2 * count, width), LOW) for w in weights] + [shape((width, 2 * count), LOW)] * 2
    ins = list(blocks) + list(weights)
    if norm is not None:
        outs.append(shape((2 * count, dim), LOW))
        ins += list(norm[:2])
    n_weights = len(weights)

    def body(need, emit, *refs):
        rows, ws = refs[:2], refs[2 : 2 + n_weights]
        res = refs[len(ins) :]
        if norm is not None:
            norm_into(rows, refs[2 + n_weights], refs[3 + n_weights], norm[2], res[-1])
            rows = [res[-1].at[:count], res[-1].at[count:]]
        need(0)
        project_into(rows, ws, res)

    return local_kernel(
        body, "project_pair", ins, outs, cold=[range(2, 2 + n_weights)], cold_outs=range(len(outs))
    )


def norm_into(blocks, gain, offset, index, out):
    count = blocks[0].shape[0]
    at = slice(index, index + 1)
    for b in range(2):
        rows = layer_norm(blocks[b][...].astype(F32), gain[at, :], offset[at, :])
        out[b * count : (b + 1) * count, :] = rows.astype(LOW)


def project_into(blocks, weights, res):
    count = blocks[0].shape[0]
    for i, weight in enumerate(weights):
        for b in range(2):
            part = dot(blocks[b][...], weight[...])
            res[i][b * count : (b + 1) * count, :] = part.astype(LOW)
            if i < 2:
                res[len(weights) + i][:, b * count : (b + 1) * count] = part.T.astype(LOW)


def attend_first(far, across, weights, queries_far, near_set, out_weight, ids, norm=None):
    count, dim = far.shape
    width = out_weight.shape[1]
    heads = width // HEAD
    with_query = len(weights) == 3
    q_ids, k_ids, bounds = ids
    n_weights = len(weights)
    first = [far, across, *weights, *(norm[:2] if norm else ())]
    second = [near_set[0], near_set[2], near_set[3], out_weight, q_ids, k_ids]
    if not with_query:
        second.append(queries_far)
    n_first, n_all = len(first), len(first) + len(second)
    ins = first + second + [bounds]
    pair = shape((2 * count, width), LOW)
    turned = shape((width, 2 * count), LOW)
    outs = [pair] * n_weights + [turned, turned]
    if norm is not None:
        outs.append(shape((2 * count, dim), LOW))
    n_project = len(outs)
    outs += [pair, shape((8, 2 * count)), shape((2 * count, dim), LOW)]

    def body(need, emit, *refs):
        res, scratch = refs[len(ins) : len(ins) + len(outs)], refs[len(ins) + len(outs) :]
        rows, ws = refs[:2], refs[2 : 2 + n_weights]
        near_keys, near_values, near_queries, wo, qi, ki = refs[n_first : n_first + 6]
        bnd = refs[n_all]
        if norm is not None:
            norm_into(rows, refs[2 + n_weights], refs[3 + n_weights], norm[2], res[n_project - 1])
            rows = [res[n_project - 1].at[:count], res[n_project - 1].at[count:]]
        need(0)
        project_into(rows, ws, res)
        emit(*res[:n_project])
        need(1)
        far_queries = res[2] if with_query else refs[n_first + 6]
        mixed, logs, hop = res[n_project:]
        for place, (block, source) in enumerate(((3, far_queries), (1, near_queries))):
            attend_block(
                block, source, (near_keys, res[0]), (near_values, res[n_weights + 1]),
                qi, ki, bnd, mixed, (block % 2) * count, place * count, logs, scratch,
            )
            rows_of_mixed = mixed[place * count : (place + 1) * count, :]
            hop[place * count : (place + 1) * count, :] = dot_last(rows_of_mixed, wo[...]).astype(LOW)

    return local_kernel(
        body, "attend_first", ins, outs, attend_scratch(count, heads), smem=(n_all,),
        cold=[range(2, 2 + n_weights), range(n_first, n_all)], cold_outs=range(n_project + 2),
    )


def attend_one(block, queries, near_set, far_set, out_weight, ids, after):
    width = out_weight.shape[1]
    heads = width // HEAD
    count = queries.shape[0] // 2
    dim = out_weight.shape[0]
    q_ids, k_ids, bounds = ids
    ins = [queries, near_set[0], far_set[0], near_set[1], far_set[1], out_weight, q_ids, k_ids, bounds]
    outs = [shape((count, width), LOW), shape((8, count)), shape((count, dim))]

    def body(need, emit, q, k0, k1, v0, v1, wo, qi, ki, bnd, mixed, logs, part, *scratch):
        need(0)
        attend_block(block, q, (k0, k1), (v0, v1), qi, ki, bnd, mixed, 0, 0, logs, scratch)
        part[...] = dot_last(mixed[...], wo[...])

    return local_kernel(
        body, "attend_one", ins, outs, attend_scratch(count, heads), smem=(8,),
        cold=[range(8)], cold_outs=(0, 1), after=after,
    )


def back_block(block, row, grads, queries, logs, keys, key_ts, values, q_ids, k_ids, bounds,
               query_grads, key_acc, value_acc, scratch):
    probs, grad_probs, inner_sum, acc = scratch
    count = queries.shape[0] // 2
    heads = queries.shape[1] // HEAD
    query_rows = queries[row : row + count, :]
    ids = q_ids[:, block * count : (block + 1) * count]
    inner_sum[...] = jnp.zeros(inner_sum.shape, F32)
    acc[...] = jnp.zeros(acc.shape, F32)
    for tile in range(4):
        inner = (tile % 2) * count

        @pl.when(tile_active(bounds, block, tile))
        def _(tile=tile, inner=inner):
            allowed = k_ids[tile * count : (tile + 1) * count, :] == ids
            for h in range(heads):
                cols = slice(h * HEAD, (h + 1) * HEAD)
                part = dot_last(keys[tile // 2][inner : inner + count, cols], query_rows[:, cols])
                exact = jnp.where(
                    allowed,
                    jnp.exp2(part * exp2_scale - logs[0][h : h + 1, logs[1] : logs[1] + count]),
                    0.0,
                )
                pulled = dot_last(values[tile // 2][inner : inner + count, cols], grads[:, cols])
                probs[h, tile] = exact
                grad_probs[h, tile] = pulled
                inner_sum[h : h + 1, :] += jnp.sum(exact * pulled, axis=0, keepdims=True)
                value_acc[tile * count : (tile + 1) * count, cols] += dot(
                    exact.astype(LOW), grads[:, cols]
                )

    for tile in range(4):
        inner = (tile % 2) * count

        @pl.when(tile_active(bounds, block, tile))
        def _(tile=tile, inner=inner):
            for h in range(heads):
                cols = slice(h * HEAD, (h + 1) * HEAD)
                score_grads = (
                    probs[h, tile] * (grad_probs[h, tile] - inner_sum[h : h + 1, :])
                ).astype(LOW)
                key_acc[tile * count : (tile + 1) * count, cols] += dot(
                    score_grads, query_rows[:, cols]
                )
                acc[h] += dot(key_ts[tile // 2][cols, inner : inner + count], score_grads)

    for h in range(heads):
        query_grads[row : row + count, h * HEAD : (h + 1) * HEAD] = (
            (acc[h] * score_scale).T.astype(LOW)
        )


def back_scratch(count, heads):
    return [
        pltpu.VMEM((heads, 4, count, count), F32),
        pltpu.VMEM((heads, 4, count, count), F32),
        pltpu.VMEM((8, count), F32),
        pltpu.VMEM((heads, HEAD, count), F32),
    ]


def back_near(grads, out_weight, queries, logs, kept, ids):
    count = queries.shape[0] // 2
    width = queries.shape[1]
    q_ids, k_ids, bounds = ids
    ins = [*grads, out_weight, queries, *logs, *kept, q_ids, k_ids, bounds]
    outs = [shape((2 * count, width), LOW), shape((4 * count, width)), shape((4 * count, width))]

    def body(need, emit, g0, g1, wo, q, lg, lo, k0, k1, t0, t1, v0, v1, qi, ki, bnd, dq, dk, dv, *scratch):
        need(0)
        dk[...] = jnp.zeros(dk.shape, F32)
        dv[...] = jnp.zeros(dv.shape, F32)
        for b, g in enumerate((g0, g1)):
            mixed_grads = dot(g[...], wo[...]).astype(LOW)
            logs_at = (lg, count) if b else (lo, 0)
            back_block(b, b * count, mixed_grads, q, logs_at, (k0, k1), (t0, t1), (v0, v1), qi, ki, bnd,
                       dq, dk, dv, scratch)

    return local_kernel(body, "back_near", ins, outs, back_scratch(count, width // HEAD), smem=(14,),
        cold=[range(2, 14)], cold_outs=(0,),
    )


def back_far(grads, out_weight, queries, logs, kept, ids, sums, weights, after=()):
    count = queries.shape[0] // 2
    width = queries.shape[1]
    dim = out_weight.shape[0]
    q_ids, k_ids, bounds = ids
    ins = [*grads, out_weight, queries, *logs, *kept, q_ids, k_ids, bounds, *sums, *weights]
    whole = shape((4 * count, width), LOW)
    outs = [shape((2 * count, width), LOW), whole, whole, shape((count, dim)), shape((count, dim), LOW)]

    def body(need, emit, *refs):
        g0, g1, wo, q, lg, lo, k0, k1, t0, t1, v0, v1, qi, ki, bnd, dk_in, dv_in = refs[:17]
        ws = refs[17 : 17 + len(weights)]
        dq, dk, dv, far_out, across_out, key_acc, value_acc, *scratch = refs[17 + len(weights) :]
        need(0)
        key_acc[...] = dk_in[...]
        value_acc[...] = dv_in[...]
        for b, g in enumerate((g0, g1)):
            mixed_grads = dot(g[...], wo[...]).astype(LOW)
            logs_at = (lg, 0) if b else (lo, 0)
            back_block(2 + b, b * count, mixed_grads, q, logs_at, (k0, k1), (t0, t1), (v0, v1), qi, ki, bnd,
                       dq, key_acc, value_acc, scratch)
        dk[...] = (key_acc[...] * score_scale).astype(LOW)
        dv[...] = value_acc[...].astype(LOW)
        need(1)
        for b in (1, 0):
            rows = slice((2 + b) * count, (3 + b) * count)
            part = dot_last(dk[rows, :], ws[0][...]) + dot_last(dv[rows, :], ws[1][...])
            if len(ws) == 3:
                part = part + dot_last(dq[b * count : (b + 1) * count, :], ws[2][...])
            if b:
                across_out[...] = part.astype(LOW)
            else:
                far_out[...] = part

    scratch = [pltpu.VMEM((4 * count, width), F32)] * 2 + back_scratch(count, width // HEAD)
    return local_kernel(
        body, "back_far", ins, outs, scratch, smem=(14,),
        cold=[range(2, 14), range(17, 17 + len(weights))], after=after,
    )


def pull_near(pairs, after):
    dim = pairs[0][1].shape[0]
    count = pairs[0][2]
    ins = [p[0] for p in pairs] + [p[1] for p in pairs]
    outs = [shape((count, dim)), shape((count, dim), LOW)]

    def body(need, emit, *refs):
        n = len(pairs)
        need(0)
        own_out, near_out = refs[2 * n :]
        for b in range(2):
            part = None
            for i in range(n):
                term = dot_last(refs[i][b * count : (b + 1) * count, :], refs[n + i][...])
                part = term if part is None else part + term
            if b:
                near_out[...] = part.astype(LOW)
            else:
                own_out[...] = part

    return local_kernel(
        body, "pull_near", ins, outs, cold=[range(len(pairs), 2 * len(pairs))], after=after
    )


def pull_active(grads, down_proj, after):
    count, units = grads[0].shape[0], down_proj.shape[1]

    def body(need, emit, g0, g1, down, out):
        need(0)
        for b, g in enumerate((g0, g1)):
            out[b * count : (b + 1) * count, :] = dot(g[...], down[...]).astype(LOW)

    return local_kernel(
        body, "pull_active", [*grads, down_proj], [shape((2 * count, units), LOW)], cold=[range(3)], after=after
    )[0]


def mlp_pair(rows, grads, up_proj, down_proj, after=(), pulled=None):
    count, dim = rows[0].shape
    units = up_proj.shape[1]
    step = 256
    outs = [
        shape((2 * count, units), LOW), shape((2 * count, units), LOW),
        shape((count, dim)), shape((count, dim), LOW),
    ]
    ready = pulled is not None
    ins = [*rows, up_proj, pulled] if ready else [*rows, up_proj, down_proj, *grads]

    def body(need, emit, x0, x1, up, *refs):
        active, grad_hidden, first_out, second_out = refs[-4:]
        need(0)
        for b, x in enumerate((x0, x1)):
            band = slice(b * count, (b + 1) * count)
            for at in range(0, units, step):
                hidden = dot(x[...], up[:, at : at + step])
                if ready:
                    back = refs[0][band, at : at + step].astype(F32)
                else:
                    back = dot(refs[1 + b][...], refs[0][:, at : at + step])
                square = hidden * hidden
                bent = jnp.tanh(gelu_coeff * (hidden + gelu_cubic * hidden * square))
                half = 0.5 * (1.0 + bent)
                slope = half + 0.5 * hidden * (1.0 - bent * bent) * (
                    gelu_coeff * (1.0 + 3.0 * gelu_cubic * square)
                )
                active[band, at : at + step] = (hidden * half).astype(LOW)
                grad_hidden[band, at : at + step] = (back * slope).astype(LOW)
        emit(active, grad_hidden)
        for b in (1, 0):
            part = dot_last(grad_hidden[b * count : (b + 1) * count, :], up[...])
            if b:
                second_out[...] = part.astype(LOW)
            else:
                first_out[...] = part

    return local_kernel(
        body, "mlp_pair", ins, outs, cold=[[2] if ready else range(2, 6)], cold_outs=(0, 1), after=after,
    )


def pull_four(near_rows, far_rows, weight, after):
    count, dim = near_rows.shape[0] // 2, weight.shape[0]
    outs = [shape((count, dim)), shape((count, dim)), shape((2 * count, dim), LOW)]

    def body(need, emit, x, y, w, own_out, far_out, hop):
        need(0)
        own_out[...] = dot_last(x[:count, :], w[...])
        far_out[...] = dot_last(y[:count, :], w[...])
        hop[:count, :] = dot_last(y[count:, :], w[...]).astype(LOW)
        hop[count:, :] = dot_last(x[count:, :], w[...]).astype(LOW)

    return local_kernel(
        body, "pull_four", [near_rows, far_rows, weight], outs, cold=[range(3)], cold_outs=(0, 1, 2), after=after
    )


def norm_rows(terms, gain, offset, index):
    kept = terms[0]

    def body(need, emit, k, p, n, f, g, o, after, normed):
        total = p[...] + n[n.shape[0] - p.shape[0] :, :].astype(F32) + f[...].astype(F32)
        need(0)
        total = total + k[...]
        after[...] = total
        emit(after)
        normed[...] = layer_norm(total, g[index : index + 1, :], o[index : index + 1, :]).astype(LOW)

    return local_kernel(
        body, "norm_rows", [*terms, gain, offset], [shape(kept.shape), shape(kept.shape, LOW)],
        cold=[[0]], cold_outs=(0,),
    )


def norm_rows_back(values, gain, index, terms, grads, after=(), inside=False):
    added = grads is not None

    def body(need, emit, v, g, p, n, f, *refs):
        if inside:
            need(0)
        total = p[...] + n[...].astype(F32) + f[...].astype(F32)
        if not inside:
            need(0)
        back, gain_sum, offset_sum = layer_norm_back(v[...].astype(F32), g[index : index + 1, :], total)
        if added:
            back = back + refs[0][...].astype(F32)
            out, sums = refs[1:]
            sums[0:1, :] = gain_sum
            sums[1:2, :] = offset_sum
        else:
            out = refs[0]
        out[...] = back.astype(out.dtype)

    ins = [values, gain, *terms]
    outs = [shape(values.shape, LOW if added else F32)]
    if added:
        ins.append(grads)
        outs.append(shape((2, values.shape[1])))
    return local_kernel(
        body, "norm_back", ins, outs, cold=[[0, 2, 5] if inside else [0, 5] if added else [0]], cold_outs=() if added else (0,),
        vmem=VMEM_LARGE if inside else VMEM_BYTES, after=after,
    )


def dp_orders():
    bits = axis_bits("dp")
    return [bits, bits[1:2] + bits[:1] + bits[2:]]


def outer_sums(sets, after, parts_sent=1):
    n_dp = lax.axis_size("dp")
    place = lax.axis_index("dp")
    ins, plans, places, outs = [], [], [], []
    seen = {}

    def take(array):
        if id(array) not in seen:
            seen[id(array)] = len(ins)
            ins.append(array)
        return seen[id(array)]

    for groups, bits in zip(sets, dp_orders()):
        plan = []
        for blocks, parts in groups:
            terms = []
            if len(parts) == 3:
                count = blocks[0].shape[0]
                terms = [
                    (take(blocks[0]), take(parts[0]), 0, count),
                    (take(blocks[1][1]), take(parts[1]), 0, count),
                    (take(blocks[1][0]), take(parts[1]), count, count),
                    (take(blocks[2]), take(parts[2]), 0, count),
                ]
            else:
                per = len(blocks) // len(parts)
                for b, block in enumerate(blocks):
                    count = block.shape[0]
                    terms.append((take(block), take(parts[b // per]), (b % per) * count, count))
            plan.append((terms, parts[0].shape[1]))
        plans.append(plan)
        dim = groups[0][0][0].shape[1]
        chunk = dim // n_dp
        aligned = chunk % 128 == 0
        steps = dim // 128
        width = sum(p[1] for p in plan)
        if aligned:
            repeat = chunk // 128
            spots = (jnp.asarray(halving_order(bits)) ^ place)[:, None] * repeat
            spots = (spots + jnp.arange(repeat, dtype=jnp.int32)[None, :]).reshape(steps)
        else:
            spots = jnp.arange(steps, dtype=jnp.int32)
        places.append(spots.astype(jnp.int32))
        outs += [shape((dim // 2, width))] + [shape((dim // 2 // parts_sent, width), LOW)] * parts_sent
    ins.append(jnp.stack(places))

    def body(need, emit, *refs):
        need(0)
        spots = refs[len(ins) - 1]
        results = refs[len(ins) :]

        def one(order, index, target, base):
            at = pl.multiple_of(spots[order, base + index] * 128, 128)
            column = 0
            for terms, right_width in plans[order]:
                total = None
                for left, right, row, count in terms:
                    term = dot_first(refs[left][:, pl.ds(at, 128)], refs[right][row : row + count, :])
                    total = term if total is None else total + term
                target[pl.ds(pl.multiple_of(index * 128, 128), 128), column : column + right_width] = (
                    total.astype(target.dtype)
                )
                column += right_width

        per = 1 + parts_sent
        half = steps // 2
        for piece in [*range(1, per), 0]:
            for order in range(len(plans)):
                run = half if piece == 0 else half // parts_sent
                base = 0 if piece == 0 else half + (piece - 1) * run

                @pl.loop(0, run)
                def _(index, target=results[per * order + piece], order=order, base=base):
                    one(order, index, target, base)

    results = local_kernel(
        body, "outer_sums", ins, outs, smem=(len(ins) - 1,), cold=[range(len(ins) - 1)],
        cold_outs=range(len(outs)), vmem=VMEM_LARGE, after=after,
    )
    pairs = []
    for order, bits in enumerate(dp_orders()[: len(plans)]):
        keep, *sent = results[(1 + parts_sent) * order : (1 + parts_sent) * (order + 1)]
        if not aligned:
            whole = jnp.concatenate([keep, *[part.astype(F32) for part in sent]])
            whole = whole.reshape(n_dp, chunk, keep.shape[1])
            whole = whole[jnp.asarray(halving_order(bits)) ^ place].reshape(dim, keep.shape[1])
            keep, whole = whole[: dim // 2], whole[dim // 2 :].astype(LOW)
            sent = [part for part in whole.reshape(parts_sent, dim // 2 // parts_sent, keep.shape[1])]
        pairs.append((keep, *sent))
    return pairs


def outer_whole(groups, after):
    ins = [a for blocks, parts in groups for a in (*blocks, *parts)]
    dim = groups[0][0][0].shape[1]
    width = groups[0][1][0].shape[1]
    step = 256

    def body(need, emit, *refs):
        out = refs[len(ins)]
        for k in range(len(groups)):
            need(k)
            lefts, rights = refs[6 * k : 6 * k + 4], refs[6 * k + 4 : 6 * k + 6]
            count = lefts[0].shape[0]

            @pl.loop(0, dim // step)
            def _(index, k=k, lefts=lefts, rights=rights, count=count):
                at = pl.multiple_of(index * step, step)
                total = None
                for b in range(4):
                    right = rights[b // 2][(b % 2) * count : (b % 2 + 1) * count, :]
                    term = dot_first(lefts[b][:, pl.ds(at, step)], right)
                    total = term if total is None else total + term
                out[pl.ds(at, step), k * width : (k + 1) * width] = total.astype(LOW)

    return local_kernel(
        body, "outer_whole", ins, [shape((dim, width * len(groups)), LOW)],
        cold=[range(6 * k, 6 * k + 6) for k in range(len(groups))], cold_outs=(0,), after=after,
    )[0]


def merge(pairs, last, widths, after=()):
    ins, outs, firsts = [], [], []
    for order, (keep, *came) in enumerate(pairs):
        firsts.append(len(ins))
        ins += [keep, *came]
        rows, width = keep.shape
        if last:
            outs += [shape((rows, w)) for w in widths[order]]
        else:
            outs += [shape((rows // 2, width)), shape((rows // 2, width), LOW)]

    def body(need, emit, *refs):
        results = list(refs[len(ins) :])
        for order in range(len(pairs)):
            keep, got = refs[firsts[order]], refs[firsts[order] + 1]
            if last:
                column = 0
                for w in widths[order]:
                    cols = slice(column, column + w)
                    results.pop(0)[...] = keep[:, cols] + got[:, cols].astype(F32)
                    column += w
            else:
                half = keep.shape[0] // 2
                later = got[half:, :] if len(pairs[order]) == 2 else refs[firsts[order] + 2][...]
                results.pop(0)[...] = keep[:half, :] + got[:half, :].astype(F32)
                results.pop(0)[...] = (keep[half:, :] + later.astype(F32)).astype(LOW)

    results = local_kernel(body, "merge", ins, outs, after=after)
    if last:
        return results
    return [(results[2 * i], results[2 * i + 1]) for i in range(len(pairs))]


def rows_of(source, row_start, row_count):
    return lax.dynamic_slice_in_dim(source, row_start, row_count, 0)


def turn_row(row):
    columns = []
    for at in range(0, row.shape[1], 128):
        columns.append(jnp.broadcast_to(row[:, at : at + 128], (128, 128)).T[:, 0:1])
    return jnp.concatenate(columns, axis=0)


def prepare(latent_row, input_row, member, table, gain, offset, query_weight, images):
    total = latent_row.shape[1]
    count = total // 4
    slots, dim = table.shape
    width = query_weight.shape[1]
    whole = jnp.int32
    outs = [
        shape((1, total), whole), shape((total, 1), whole), shape((total, 1), whole),
        shape((4, 4), whole), shape((4, 4), whole),
        shape((total, slots), LOW), shape((slots, dim), LOW),
        shape((2 * count, width), LOW), shape((2 * count, width), LOW), shape((count, dim)),
    ]

    def body(need, emit, lat, inp, lat_s, inp_s, who, tb, g, o, wq,
             lat_out, lat_col, inp_col, cross_ends, self_ends, pick, normed, near_q, far_q, start):
        order = [who[0, 0] ^ k for k in range(4)]
        for k in range(4):
            first = order[k] * count
            last = first + count - 1
            cross_ends[0, k] = lat_s[0, first]
            cross_ends[1, k] = lat_s[0, last]
            cross_ends[2, k] = inp_s[0, first]
            cross_ends[3, k] = inp_s[0, last]
            for r in range(2):
                self_ends[2 * r, k] = lat_s[0, first]
                self_ends[2 * r + 1, k] = lat_s[0, last]
        starts = [pl.multiple_of(at * count, count) for at in order]
        lat_rel = jnp.concatenate([lat[:, pl.ds(at, count)] for at in starts], axis=1)
        inp_rel = jnp.concatenate([inp[:, pl.ds(at, count)] for at in starts], axis=1)
        lane = lax.broadcasted_iota(whole, (1, count), 1)
        place = jnp.concatenate([lane + at for at in starts], axis=1)
        lat_all = lat[...]
        for image in range(images):
            before = jnp.sum((lat_all < image).astype(F32), axis=1, keepdims=True).astype(whole)
            place = place - jnp.where(lat_rel == image, before, 0)
        lat_out[...] = lat_rel
        lat_col[...] = turn_row(lat_rel)
        inp_col[...] = turn_row(inp_rel)
        slot = turn_row(place)
        slot_lane = lax.broadcasted_iota(whole, (total, slots), 1)
        pick[...] = jnp.where(slot == slot_lane, 1.0, 0.0).astype(LOW)
        normed[...] = layer_norm(tb[...].astype(F32), g[0:1, :], o[0:1, :]).astype(LOW)
        start[...] = dot(pick[:count, :], tb[...])
        need(0)
        queries = dot(normed[...], wq[...]).astype(LOW)
        near_q[...] = dot(pick[: 2 * count, :], queries).astype(LOW)
        far_q[...] = dot(pick[2 * count :, :], queries).astype(LOW)

    return local_kernel(
        body, "prepare",
        [latent_row, input_row, latent_row, input_row, member, table, gain, offset, query_weight],
        outs, smem=(2, 3, 4), smem_outs=(3, 4), cold=[[8]],
    )


def slot_stack(pick, query_pairs, raw_blocks, parts, grads, sums, member, after):
    count, dim = raw_blocks[0].shape
    slots, width = pick.shape[1], query_pairs[0].shape[1]
    cut = dim // (2 * width)
    ins = [pick, *query_pairs, *raw_blocks, *parts, *grads, *sums, member]

    def body(need, emit, pk, q0, q1, x0, x1, x2, x3, p0, p1, p2, p3, r0, r1, r2, r3, s0, s1, who, out):
        need(0)
        total = dot_first(pk[: 2 * count, :], q0[...]) + dot_first(pk[2 * count :, :], q1[...])
        out[:slots, :width] = total.astype(LOW)
        at = pl.multiple_of(who[0, 0] * width, width)
        total = None
        for b, r in enumerate((r0, r1, r2, r3)):
            term = dot_first(pk[b * count : (b + 1) * count, :], r[:, pl.ds(at, width)])
            total = term if total is None else total + term
        out[:slots, width:] = total.astype(LOW)
        gain_sum = offset_sum = None
        for x, p in ((x0, p0), (x1, p1), (x2, p2), (x3, p3)):
            values = x[...].astype(F32)
            centred = values - jnp.mean(values, axis=-1, keepdims=True)
            spread = jnp.mean(centred * centred, axis=-1, keepdims=True)
            back = p[...].astype(F32)
            gains = jnp.sum(back * (centred * lax.rsqrt(spread + norm_eps)), axis=0, keepdims=True)
            offsets = jnp.sum(back, axis=0, keepdims=True)
            gain_sum = gains if gain_sum is None else gain_sum + gains
            offset_sum = offsets if offset_sum is None else offset_sum + offsets
        rows = [gain_sum, offset_sum, s0[0:1, :], s0[1:2, :], s1[0:1, :], s1[1:2, :]]
        rows += [jnp.zeros((1, dim), F32)] * 2
        whole = jnp.concatenate(rows, axis=0)
        pieces = [whole[:, 2 * q * width : 2 * (q + 1) * width] for q in range(cut)]
        out[slots:, :] = jnp.concatenate(pieces, axis=0).astype(LOW)

    return local_kernel(
        body, "slot_stack", ins, [shape((slots + 8 * cut, 2 * width), LOW)],
        smem=(len(ins) - 1,), cold=[range(7)], after=after,
    )[0]


def table_end(stacks, weights, gain, table, member):
    slots, dim = table.shape
    width = stacks[0].shape[1] // 2
    cut = dim // (2 * width)
    ins = [*stacks, *weights, gain, table, member]

    def body(need, emit, *refs):
        st, ws = refs[:4], refs[4:8]
        g, tb, who = refs[8:11]
        table_out, gain_out, offset_out, last_out, residual, grads, weight = refs[11:]
        need(0)
        for k in range(4):
            at = pl.multiple_of((who[0, 0] ^ k) * width, width)
            grads[:, pl.ds(at, width)] = st[k][:slots, :width]
            residual[:, pl.ds(at, width)] = st[k][:slots, width:]
            weight[:, pl.ds(at, width)] = ws[k][...]
        total = dot_last(grads[...], weight[...])
        back, gain_sum, offset_sum = layer_norm_back(tb[...].astype(F32), g[0:1, :], total)
        table_out[...] = residual[...].astype(F32) + back
        small = [st[k][slots:, :].astype(F32) for k in range(4)]
        small = (small[0] + small[1]) + (small[2] + small[3])
        small = jnp.concatenate([small[8 * q : 8 * (q + 1), :] for q in range(cut)], axis=1)
        gain_out[0:1, :] = gain_sum
        offset_out[0:1, :] = offset_sum
        for k in range(3):
            gain_out[k + 1 : k + 2, :] = small[2 * k : 2 * k + 1, :]
            target = last_out if k == 2 else offset_out
            at = 0 if k == 2 else k + 1
            target[at : at + 1, :] = small[2 * k + 1 : 2 * k + 2, :]

    outs = [shape((slots, dim)), shape((4, dim)), shape((3, dim)), shape((1, dim))]
    return local_kernel(
        body, "table_end", ins, outs,
        [pltpu.VMEM((slots, dim), LOW), pltpu.VMEM((slots, dim), LOW), pltpu.VMEM((dim, dim), LOW)],
        smem=(10,), cold=[range(4, 8)],
    )


def body(
    block_input,
    latent_table,
    latent_segments,
    input_segments,
    ln_gain,
    ln_bias,
    cross_query,
    cross_key,
    cross_value,
    cross_out,
    self_query,
    self_key,
    self_value,
    self_out,
    up_proj,
    down_proj,
    out_grad,
):
    count, dim = block_input.shape
    member = lax.axis_index("mp")
    n_mp, n_dp = lax.axis_size("mp"), lax.axis_size("dp")
    slots = latent_table.shape[0]
    mp_bits, dp_bits = axis_bits("mp"), axis_bits("dp")
    dp_steps = len(dp_bits)

    far_raw = swap(block_input, "mp", 2)
    near_raw = swap(block_input, "mp", 1)
    near_out = swap(out_grad, "mp", 1)
    half = count // 2
    near_raw, out_1, out_2 = lax.optimization_barrier((near_raw, out_grad[:half], out_grad[half:]))

    who = member.astype(jnp.int32).reshape(1, 1)
    (latent_rel, latent_col, input_col, cross_ends, self_ends, table_pick, normed_table, queries_near,
     queries_far, start_rows) = prepare(
        latent_segments, input_segments, who, latent_table, ln_gain, ln_bias, cross_query, images
    )
    cross_ids = (latent_rel, input_col, cross_ends)
    self_ids = (latent_rel, latent_col, self_ends)

    input_norm = (ln_gain, ln_bias, 1)
    keys_near, values_near, key_ts_near, value_ts_near, normed_near = project_pair(
        (block_input, near_raw), (cross_key, cross_value), input_norm
    )
    far_raw = tie(far_raw, keys_near, queries_far)
    across_raw = swap(far_raw, "mp", 1)
    far_out_1 = swap(tie(out_1, far_raw), "mp", 2)
    (keys_far, values_far, key_ts_far, value_ts_far, normed_far, mixed_two, logs_two, hop) = attend_first(
        far_raw, across_raw, (cross_key, cross_value), queries_far,
        (keys_near, key_ts_near, value_ts_near, queries_near), cross_out, cross_ids, input_norm,
    )
    got = swap(tie(hop, far_out_1), "mp", 1)
    key_values = ((keys_near, value_ts_near), (keys_far, value_ts_far))
    mixed_far, logs_far, part_far = attend_one(2, queries_far, *key_values, cross_out, cross_ids, ())
    got_far, sent = send_far(part_far, got)
    mixed_own, logs_own, part_own = attend_one(0, queries_near, *key_values, cross_out, cross_ids, (sent,))
    cross_kept = (keys_near, keys_far, key_ts_near, key_ts_far, values_near, values_far)
    cross_queries_set = (queries_near, queries_far)
    cross_logs = ((logs_two, logs_own), (logs_two, logs_far))
    cross_mixed = (mixed_own, mixed_two, mixed_far)
    after_cross, normed_self = norm_rows((start_rows, part_own, got, got_far), ln_gain, ln_bias, 2)

    self_weights = (self_key, self_value, self_query)
    far_self = swap(normed_self, "mp", 2)
    near_self = swap(normed_self, "mp", 1)
    keys_near, values_near, queries_near, key_ts_near, value_ts_near = project_pair(
        (normed_self, near_self), self_weights
    )
    far_self = tie(far_self, keys_near)
    across_self = swap(far_self, "mp", 1)
    far_out_2 = swap(tie(out_2, far_self), "mp", 2)
    (keys_far, values_far, queries_far, key_ts_far, value_ts_far, mixed_two, logs_two, hop) = attend_first(
        far_self, across_self, self_weights, None,
        (keys_near, key_ts_near, value_ts_near, queries_near), self_out, self_ids,
    )
    got = swap(tie(hop, far_out_2), "mp", 1)
    key_values = ((keys_near, value_ts_near), (keys_far, value_ts_far))
    mixed_far, logs_far, part_far = attend_one(2, queries_far, *key_values, self_out, self_ids, ())
    got_far, sent = send_far(part_far, got)
    mixed_own, logs_own, part_own = attend_one(0, queries_near, *key_values, self_out, self_ids, (sent,))
    far_out = tie(jnp.concatenate([far_out_1, far_out_2]), part_own)
    across_out = swap(far_out, "mp", 1)
    self_kept = (keys_near, keys_far, key_ts_near, key_ts_far, values_near, values_far)
    self_queries_set = (queries_near, queries_far)
    self_logs = ((logs_two, logs_own), (logs_two, logs_far))
    self_mixed = (mixed_own, mixed_two, mixed_far)
    after_self, normed_mlp = norm_rows((after_cross, part_own, got, got_far), ln_gain, ln_bias, 3)

    far_mlp = swap(normed_mlp, "mp", 2)
    near_mlp = swap(normed_mlp, "mp", 1)
    active_near, hidden_near, part_own, part_near = mlp_pair(
        (normed_mlp, near_mlp), (out_grad, near_out), up_proj, down_proj, (across_out,)
    )
    pulled_far = pull_active((far_out, across_out), down_proj, (part_near,))
    far_mlp = tie(far_mlp, pulled_far)
    across_mlp = swap(far_mlp, "mp", 1)
    active_far, hidden_far, part_far, part_across = mlp_pair(
        (far_mlp, across_mlp), None, up_proj, None, (), pulled_far
    )
    got = swap(part_across, "mp", 1)
    got_far, sent = send_far(part_far, got)
    got_near = swap(part_near, "mp", 1)
    mlp_grads = outer_whole(
        [
            ((normed_mlp, near_mlp, far_mlp, across_mlp), (hidden_near, hidden_far)),
            ((out_grad, near_out, far_out, across_out), (active_near, active_far)),
        ],
        (sent, got_near),
    )
    mlp_sum = lax.psum_scatter(tie(mlp_grads, got_far), "dp", scatter_dimension=0, tiled=True)
    dy_own, mlp_sums = norm_rows_back(
        after_self, ln_gain, 3, (part_own, got_near, got_far), out_grad,
        (mlp_grads,), True,
    )

    far_dy = swap(dy_own, "mp", 2)
    near_dy = swap(dy_own, "mp", 1)

    query_near, key_sum, value_sum = back_near(
        (dy_own, near_dy), self_out, self_queries_set[0], self_logs[0], self_kept, self_ids
    )
    far_dy = tie(far_dy, key_sum)
    across_dy = swap(far_dy, "mp", 1)
    query_far, key_grads, value_grads, part_far, part_across = back_far(
        (far_dy, across_dy), self_out, self_queries_set[1], self_logs[1], self_kept, self_ids,
        (key_sum, value_sum), self_weights,
    )
    got = swap(part_across, "mp", 1)
    part_own, part_near = pull_near(
        [(key_grads, self_key, count), (value_grads, self_value, count), (query_near, self_query, count)], ()
    )
    got_far, sent = send_far(part_far, got, part_own)
    got_near = swap(part_near, "mp", 1)
    normed_blocks = (normed_self, near_self, far_self, across_self)
    self_pairs = outer_sums(
        [
            [
                (normed_blocks, (query_near, query_far)), (normed_blocks, (key_grads,)),
                (normed_blocks, (value_grads,)), ((dy_own, (near_dy, across_dy), far_dy), self_mixed),
            ],
        ],
        (sent, got_near), 2,
    )
    dy_cross, self_sums = norm_rows_back(
        after_cross, ln_gain, 2, (part_own, got_near, got_far), dy_own,
        (self_pairs[0][1],),
    )

    far_dyc = swap(dy_cross, "mp", 2)
    near_dyc = swap(dy_cross, "mp", 1)
    query_near, key_sum, value_sum = back_near(
        (dy_cross, near_dyc), cross_out, cross_queries_set[0], cross_logs[0], cross_kept, cross_ids
    )
    part_own_out, part_far_out, hop_out = pull_four(active_near, active_far, down_proj, (key_sum,))
    self_half = swap(self_pairs[0][1], "dp", dp_bits[0])
    far_dyc = tie(far_dyc, part_own_out, self_half)
    across_dyc = swap(far_dyc, "mp", 1)
    query_far, key_grads, value_grads, part_far, part_across = back_far(
        (far_dyc, across_dyc), cross_out, cross_queries_set[1], cross_logs[1], cross_kept, cross_ids,
        (key_sum, value_sum), (cross_key, cross_value),
    )
    dyc_blocks = (dy_cross, near_dyc, far_dyc, across_dyc)
    part_own, part_near = pull_near([(key_grads, cross_key, count), (value_grads, cross_value, count)], ())
    got = swap(part_across, "mp", 1)
    got_near = swap(part_near, "mp", 1)
    got_far, sent = send_far(part_far, got, part_own)

    up_width = up_proj.shape[1]
    heads_width = cross_query.shape[1]
    stack = slot_stack(
        table_pick, (query_near, query_far), (block_input, near_raw, far_raw, across_raw),
        (part_own, part_near, part_far, part_across), dyc_blocks, (self_sums, mlp_sums), who,
        (sent,),
    )
    input_blocks = (normed_near, normed_far)
    cross_sets = [
        [
            (input_blocks, (key_grads,)),
            (input_blocks, (value_grads,)),
            ((dy_cross, (near_dyc, across_dyc), far_dyc), cross_mixed),
        ],
    ]
    self_keep, _, self_sent = self_pairs[0]

    def dp_swap(values, step):
        return swap(values, "dp", dp_bits[step])

    def joined(mine, came):
        return (mine.astype(F32) + came.astype(F32)).astype(LOW)

    def halved(keep, *came):
        return merge([(keep, *came)], False, None)[0]

    stack_got, self_got = dp_swap(stack, 0), dp_swap(self_sent, 0)
    ((cross_keep, cross_sent),) = outer_sums(cross_sets, (stack,))
    got_far, got_near, stack, stack_got, self_got, cross_sent, hop_out, query_sent = wait(
        got_far, got_near, stack, stack_got, self_got, cross_sent, hop_out, cross_query
    )
    stack = joined(stack, stack_got)

    self_keep, self_sent = halved(self_keep, self_half, self_got)
    stack_got, self_got, cross_got = dp_swap(stack, 1), dp_swap(self_sent, 1), dp_swap(cross_sent, 0)
    far_query, near_query = swap(query_sent, "mp", 2), swap(query_sent, "mp", 1)
    got_out = swap(hop_out, "mp", 1)
    stack, stack_got, got_out, self_sent, got_far = wait(stack, stack_got, got_out, self_sent, got_far)
    stack = joined(stack, stack_got)
    sent_out = (part_far_out + got_out[:count].astype(F32)).astype(LOW)

    stack_got = dp_swap(stack, 2)
    got_far_out = swap(sent_out, "mp", 2)
    (grad_input,) = norm_rows_back(block_input, ln_gain, 1, (part_own, got_near, got_far), None)
    mlp_parts = [mlp_sum[:, :up_width].astype(F32), mlp_sum[:, up_width:].astype(F32)]
    stack, stack_got, self_got, cross_got, mlp_parts, grad_input = wait(
        stack, stack_got, self_got, cross_got, mlp_parts, grad_input
    )

    for step in range(3, dp_steps):
        stack = joined(stack, stack_got)
        self_keep, self_sent = halved(self_keep, self_got)
        cross_keep, cross_sent = halved(cross_keep, cross_got)
        stack_got, cross_got, self_got = wait(
            dp_swap(stack, step), dp_swap(cross_sent, step - 2), dp_swap(self_sent, step - 1)
        )

    cross_keep, cross_sent = halved(cross_keep, cross_got)
    stack = joined(tie(stack, cross_sent), stack_got)
    far_stack, near_stack = swap(stack, "mp", 2), swap(stack, "mp", 1)
    cross_got = dp_swap(cross_sent, dp_steps - 2)
    self_keep, self_sent = halved(tie(self_keep, cross_sent), self_got)
    self_got = dp_swap(self_sent, dp_steps - 1)
    chunk = dim // n_dp
    own_features = lax.dynamic_slice_in_dim(normed_table, lax.axis_index("dp") * chunk, chunk, 1)
    query_sum = dot_first(own_features, stack[:slots, :heads_width])
    block_output = (
        after_self + part_own_out + got_out[count:].astype(F32) + got_far_out.astype(F32)
    )
    far_stack, cross_got, self_got, far_query, near_query, block_output, query_sum = wait(
        far_stack, cross_got, self_got, far_query, near_query, block_output, query_sum
    )

    across_stack = swap(far_stack, "mp", 1)
    across_query = swap(far_query, "mp", 1)
    cross_keep, cross_sent = halved(cross_keep, cross_got)
    cross_got = dp_swap(cross_sent, dp_steps - 1)
    across_stack, cross_sent = wait(across_stack, cross_sent)
    table_grad, ln_gain_grad, ln_bias_grad, last_bias = table_end(
        (stack, near_stack, far_stack, across_stack),
        (cross_query, near_query, far_query, across_query), ln_gain, latent_table, who,
    )
    cross_keep, self_keep, table_grad = wait(cross_keep, self_keep, table_grad)
    self_pair = merge([(self_keep, self_got)], True, [[heads_width] * 4])
    cross_pair = merge([(cross_keep, cross_got)], True, [[heads_width] * 3])

    return (
        block_output,
        grad_input,
        table_grad,
        ln_gain_grad,
        ln_bias_grad,
        last_bias[0],
        query_sum,
        *cross_pair,
        *self_pair,
        *mlp_parts,
    )


def solution(mesh):
    placed = (
        P(("dp", "mp"), None),
        P(),
        P("dp", None),
        P("dp", None),
        P(),
        P(),
        P(None, "mp"),
        P(None, "mp"),
        P(None, "mp"),
        P(None, "mp"),
        P(None, "mp"),
        P(None, "mp"),
        P(None, "mp"),
        P(None, "mp"),
        P(None, "mp"),
        P(None, "mp"),
        P(("dp", "mp"), None),
    )
    return jax.shard_map(
        body,
        mesh=mesh,
        in_specs=placed,
        out_specs=(
            P(("dp", "mp"), None),
            P(("dp", "mp"), None),
            P(),
            P(),
            P(),
            P(),
            P("dp", "mp"),
            P("dp", "mp"),
            P("dp", "mp"),
            P("dp", "mp"),
            P("dp", "mp"),
            P("dp", "mp"),
            P("dp", "mp"),
            P("dp", "mp"),
            P("dp", "mp"),
            P("dp", "mp"),
        ),
        check_vma=False,
    )
```
